32 devices in a mesh: wide: 8 (over z, y), narrow: 4 (over x, core).
Axes of the slice: x: 2, y: 2, z: 4, core: 2. Of those that a mesh axis runs over, the one named last changes fastest.
Arguments:
- tokens: bfloat16 [98304, 768], P(('wide', 'narrow')), may hold values from -6 to 6
- labels: int32 [96], P(('wide', 'narrow')), may hold values from 0 to 2
- qkv_weight: bfloat16 [768, 2304], replicated, may hold values from -0.21875 to 0.21875
- out_weight: bfloat16 [768, 768], replicated, may hold values from -1.75 to 1.75
- up_weight: bfloat16 [768, 3072], replicated, may hold values from -0.21875 to 0.21875
- down_weight: bfloat16 [3072, 768], replicated, may hold values from -0.109375 to 0.109375
- ffn_bias: float32 [3072], replicated, may hold values from -4 to 4
- layer_biases: float32 [6, 768], replicated, may hold values from -4 to 4
- norm_gains: float32 [2, 768], replicated, may hold values from 0.5 to 1.5
- pool_weight: float32 [768, 768], replicated, may hold values from -0.21875 to 0.21875
- pool_moment: float32 [768, 768], replicated, may hold values from -3 to 3
- class_weight: float32 [768, 3], replicated, may hold values from -0.21875 to 0.21875
- class_moment: float32 [768, 3], replicated, may hold values from -20 to 20
- ramp_biases: float32 [771], replicated, may hold values from -3 to 3
- bias_moment: float32 [771], replicated, may hold values from -6 to 6
- start_factor: float32 [768, 8], replicated, may hold values from -6 to 6
- error_buffer: float32 [24576, 768], P(('wide', 'narrow')), may hold values from -0.75 to 0.75
Outputs:
- layer_out: bfloat16 [98304, 768], P(('wide', 'narrow'))
- pool_moment_new: float32 [768, 768], replicated
- pool_weight_new: float32 [768, 768], replicated
- class_moment_new: float32 [768, 3], replicated
- class_weight_new: float32 [768, 3], replicated
- bias_moment_new: float32 [771], replicated
- ramp_biases_new: float32 [771], replicated
- error_new: float32 [24576, 768], P(('wide', 'narrow'))
- factor_new: float32 [768, 8], replicated
The draws below stay inside these ranges and needn't reach their ends.
All inputs are finite; a program needn't handle non-finite values.
Results may differ from the reference program's by a relative error of at most 0.012.
Values sent between devices are 32-bit elements; how exact they have to be, the bound alone decides.
A program may use at most 192 MiB of HBM per device.

```python
import jax
import jax.numpy as jnp
from jax import lax

D = 768
HEADS = 12
HEAD_DIM = 64
FF = 3072
CLASSES = 3
RANK = 8
SEQ_LEN = 1024
SEQ_DEV = 3
SEQS = 96
TOKENS = 98304
ERROR_ROWS = 24576
N_WIDE = 8
N_NARROW = 4


def place_ends(values, key, least, largest):
    longest = values.shape.index(max(values.shape))
    spots = []
    for shift in (0, 1):
        where = [jax.random.randint(jax.random.fold_in(key, axis), (), 0, length) for axis, length in enumerate(values.shape)]
        where[longest] = (where[longest] + shift) % values.shape[longest]
        spots.append(tuple(where))
    return values.at[spots[0]].set(least).at[spots[1]].set(largest)


def steps_of(rng, shape, cuts, least, top_value):
    def one(axis_at, parts):
        draws = jax.random.uniform(jax.random.fold_in(jax.random.fold_in(rng, 6), axis_at), (parts,), jnp.float32, least / len(cuts), top_value / len(cuts))
        return jnp.repeat(jnp.exp(draws), shape[axis_at] // parts).reshape((-1,) + (1,) * (len(shape) - axis_at - 1))

    level = one(*cuts[0])
    for cut in cuts[1:]:
        level = level * one(*cut)
    return level


def gaussian(stream_key, dims, width, reach, split=(), kind=jnp.bfloat16):
    values = width * jax.random.normal(stream_key, dims, jnp.float32)
    if split:
        values = values * steps_of(stream_key, dims, split, -0.22, 0.18)
    return jnp.clip(values, -reach, reach).astype(kind)


def setup_inputs(seed: int = 0) -> dict:
    key_list = jax.random.split(jax.random.key(seed), 18)
    return {
        "tokens": gaussian(key_list[0], (TOKENS, D), 1.0, 6.0, ((0, 32),)),
        "labels": place_ends(jax.random.randint(key_list[1], (SEQS,), 0, CLASSES), jax.random.fold_in(key_list[1], 1), 0, CLASSES - 1).astype(jnp.int32),
        "qkv_weight": gaussian(key_list[2], (D, 3 * D), D ** -0.5, 0.21875),
        "out_weight": gaussian(key_list[3], (D, D), (max(D // 64, 1)) ** -0.5, 1.75),
        "up_weight": gaussian(key_list[4], (D, FF), D ** -0.5, 0.21875),
        "down_weight": gaussian(key_list[5], (FF, D), FF ** -0.5, 0.109375),
        "ffn_bias": gaussian(key_list[6], (FF,), 0.3, 4.0, (), jnp.float32),
        "layer_biases": gaussian(key_list[7], (6, D), 0.3, 4.0, (), jnp.float32),
        "norm_gains": jnp.clip(1.0 + 0.1 * jax.random.normal(key_list[8], (2, D), jnp.float32), 0.5, 1.5),
        "pool_weight": gaussian(key_list[9], (D, D), D ** -0.5, 0.21875, (), jnp.float32),
        "pool_moment": gaussian(key_list[10], (D, D), (0.02 * SEQS ** 0.5), 3.0, (), jnp.float32),
        "class_weight": gaussian(key_list[11], (D, CLASSES), D ** -0.5, 0.21875, (), jnp.float32),
        "class_moment": gaussian(key_list[12], (D, CLASSES), (0.35 * SEQS ** 0.5), 20.0, (), jnp.float32),
        "ramp_biases": gaussian(key_list[13], (D + CLASSES,), 0.2, 3.0, (), jnp.float32),
        "bias_moment": gaussian(key_list[14], (D + CLASSES,), (0.1 * SEQS ** 0.5), 6.0, (), jnp.float32),
        "start_factor": gaussian(key_list[15], (D, RANK), 1.0, 6.0, (), jnp.float32),
        "error_buffer": gaussian(key_list[16], (ERROR_ROWS, D), 0.05, 0.75, ((0, 32),), jnp.float32),
    }


@jax.custom_vjp
def low(v):
    return lax.optimization_barrier(v.astype(jnp.bfloat16)).astype(jnp.float32)

@jax.custom_vjp
def low_back(v):
    return v

def low_keep(v):
    return (low(v), None)

def low_pass(kept, grad):
    return (grad,)

def back_keep(v):
    return (v, None)

def back_low(kept, grad):
    return (low(grad),)
low.defvjp(low_keep, low_pass)
low_back.defvjp(back_keep, back_low)
precise = lax.Precision.HIGHEST
MOMENTUM = 0.9
RATE_POOL = 0.03
RATE_HEAD = 0.002
RATE_BIAS = 0.03

def norm_rows(values, gain_vec, shift_vec):
    row_mean = lax.optimization_barrier(jnp.mean(values, -1, keepdims=True))
    centred = values - row_mean
    variance = lax.optimization_barrier(jnp.mean(centred * centred, -1, keepdims=True))
    return centred * lax.rsqrt(variance + 1e-12) * gain_vec + shift_vec

def encode(sequence, qkv_weight, out_weight, up_weight, down_weight, ffn_bias, layer_biases, norm_gains):
    qkv_bias = jnp.concatenate([layer_biases[0], jnp.zeros_like(layer_biases[0]), layer_biases[1]])
    packed = low(jnp.dot(sequence, qkv_weight, precision=precise) + qkv_bias)
    length = sequence.shape[0]
    queries = packed[:, :D].reshape(length, HEADS, HEAD_DIM)
    key_heads = packed[:, D:2 * D].reshape(length, HEADS, HEAD_DIM)
    value_heads = packed[:, 2 * D:].reshape(length, HEADS, HEAD_DIM)
    score_scale = 1.0 / HEAD_DIM ** 0.5
    scores = jnp.einsum('qhd,khd->hqk', queries, key_heads, precision=precise) * score_scale
    attn_weights = low(jax.nn.softmax(scores, axis=-1))
    context = low(jnp.einsum('hqk,khd->qhd', attn_weights, value_heads, precision=precise).reshape(length, D))
    attention = jnp.dot(context, out_weight, precision=precise) + layer_biases[2]
    middle = low(norm_rows(sequence + attention, norm_gains[0], layer_biases[3]))
    hidden = low(jax.nn.gelu(jnp.dot(middle, up_weight, precision=precise) + ffn_bias, approximate=False))
    branch = jnp.dot(hidden, down_weight, precision=precise) + layer_biases[4]
    return low(norm_rows(middle + branch, norm_gains[1], layer_biases[5]))

def orthonormal(factor):
    columns = []
    for column_index in range(RANK):
        vector = factor[:, column_index]
        for earlier in columns:
            vector = vector - jnp.sum(earlier * vector) * earlier
        vector = vector * lax.rsqrt(jnp.sum(vector * vector) + 1e-06)
        columns.append(vector)
    return jnp.stack(columns, 1)

def ramp_loss(pool_w, biases, class_w, rows_in, label_rows):
    pre = low_back(jnp.dot(rows_in, low(pool_w), precision=precise) + biases[:D])
    pooled = low(jnp.tanh(pre))
    logits = low_back(jnp.dot(pooled, low(class_w), precision=precise) + biases[D:])
    log_probs = jax.nn.log_softmax(logits, axis=-1)
    targets = (label_rows[:, None] == jnp.arange(CLASSES, dtype=jnp.int32)[None, :]).astype(logits.dtype)
    return -jnp.sum(log_probs * targets)

def reference(tokens, labels, qkv_weight, out_weight, up_weight, down_weight, ffn_bias, layer_biases, norm_gains, pool_weight, pool_moment, class_weight, class_moment, ramp_biases, bias_moment, start_factor, error_buffer):
    weight_list = [w.astype(jnp.float32) for w in (qkv_weight, out_weight, up_weight, down_weight)]
    sequences = tokens.astype(jnp.float32).reshape(SEQS, SEQ_LEN, D)

    def encode_one(sequence):
        return encode(sequence, weight_list[0], weight_list[1], weight_list[2], weight_list[3], ffn_bias, layer_biases, norm_gains)
    encoded = lax.map(encode_one, sequences)
    layer_out = encoded.reshape(TOKENS, D).astype(jnp.bfloat16)
    groups = N_WIDE * N_NARROW
    first_rows = encoded[:, 0, :].reshape(groups, SEQ_DEV, D)
    label_groups = labels.reshape(groups, SEQ_DEV)

    def local_grads(inputs):
        rows_in, label_rows = inputs
        unused, back = jax.vjp(lambda pool_w, biases, class_w: ramp_loss(pool_w, biases, class_w, rows_in, label_rows), pool_weight, ramp_biases, class_weight)
        return back(jnp.ones((), unused.dtype))
    grad_pool, grad_bias, grad_class = lax.map(local_grads, (first_rows, label_groups))
    combined = grad_pool + error_buffer.reshape(groups, D, D)
    factor_sum = lax.optimization_barrier(jnp.sum(jnp.einsum('gij,jr->gir', combined, start_factor, precision=precise), 0))
    basis_cols = orthonormal(factor_sum)
    factor_new = lax.optimization_barrier(jnp.sum(jnp.einsum('gij,ir->gjr', combined, basis_cols, precision=precise), 0))
    approx = jnp.dot(basis_cols, factor_new.T, precision=precise)
    error_new = (combined - approx[None] / groups).reshape(ERROR_ROWS, D)
    pool_moment_new = MOMENTUM * pool_moment + approx
    pool_weight_new = pool_weight - RATE_POOL * pool_moment_new
    class_moment_new = MOMENTUM * class_moment + lax.optimization_barrier(jnp.sum(grad_class, 0))
    class_weight_new = class_weight - RATE_HEAD * class_moment_new
    bias_moment_new = MOMENTUM * bias_moment + lax.optimization_barrier(jnp.sum(grad_bias, 0))
    ramp_biases_new = ramp_biases - RATE_BIAS * bias_moment_new
    return (layer_out, pool_moment_new, pool_weight_new, class_moment_new, class_weight_new, bias_moment_new, ramp_biases_new, error_new, factor_new)
```

```python
import functools

import jax
import jax.numpy as jnp
from jax import lax
from jax.experimental import pallas as pl
from jax.experimental.pallas import tpu as pltpu
from jax.sharding import PartitionSpec as P

HEAD_DIM = 64
SEQ_LEN = 1024
PAIR = 128
V_ROWS = 80
ROW_TILE = 16
LANES = 128
BLOCK = 512
LOG2E = 1.4426950408889634
SAFE = 2.0**100
MOMENTUM = 0.9
RATE_POOL = 0.03
RATE_HEAD = 0.002
RATE_BIAS = 0.03
VMEM_BYTES = 60 * 1024 * 1024

f32 = jnp.float32
bf16 = jnp.bfloat16
NT = ((1,), (1,))
TN = ((0,), (0,))


def dot(left, right, contract=((1,), (0,)), precision=None):
    return lax.dot_general(
        left, right, (contract, ((), ())), precision=precision, preferred_element_type=f32
    )


dot_full = functools.partial(dot, precision=lax.Precision.HIGHEST)


def norm_rows(values, gain, shift):
    centred = values - jnp.mean(values, -1, keepdims=True)
    variance = jnp.mean(centred * centred, -1, keepdims=True)
    return centred * lax.rsqrt(variance + 1e-12) * gain + shift


def gelu(values):
    half = 0.5 * values
    return half * lax.erf(values * 0.7071067811865476) + half


def head_sums(scores, values_aug, shifted):
    if shifted:
        scores = scores - jnp.max(scores, 0, keepdims=True)
    return dot(values_aug, jnp.exp2(scores * LOG2E).astype(bf16))


def put_context(context_t, head, sums):
    scale = 1.0 / sums[HEAD_DIM : HEAD_DIM + 8]
    groups = [sums[g : g + 8] * scale for g in range(0, HEAD_DIM, 8)]
    rows = pl.ds(pl.multiple_of(head * HEAD_DIM, HEAD_DIM), HEAD_DIM)
    context_t[rows, :] = jnp.concatenate(groups, 0).astype(bf16)


def attention_kernel(
    unroll,
    tokens,
    qkv_weight,
    layer_biases,
    context,
    first_context,
    first_tokens,
    query_weight_t,
    value_weight_t,
    query_bias,
    value_bias,
    keys,
    queries_t,
    values_t,
    context_t,
    low,
    high,
):
    length, width = tokens.shape
    heads = width // HEAD_DIM

    @pl.when(pl.program_id(0) == 0)
    def _():
        query_weight_t[...] = qkv_weight[:, :width].T
        value_weight_t[...] = qkv_weight[:, 2 * width :].T
        columns = jnp.concatenate([layer_biases[...], jnp.zeros((2, width), f32)], 0).T
        query_bias[...] = jnp.broadcast_to(columns[:, 0:1], (width, LANES))
        value_bias[...] = jnp.broadcast_to(columns[:, 1:2], (width, LANES))
        queries_t[...] = jnp.zeros_like(queries_t)
        values_t[:, HEAD_DIM:, :] = jnp.ones((heads, V_ROWS - HEAD_DIM, length), bf16)

    def wide_bias(bias):
        return jnp.concatenate([bias[...]] * (length // LANES), 1)

    sequence = tokens[...]
    key_rows = dot(sequence, qkv_weight[:, width : 2 * width]).astype(bf16)
    for pair in range(heads // 2):
        keys[pair] = key_rows[:, pair * PAIR : (pair + 1) * PAIR]
    query_cols = (dot(query_weight_t[...], sequence, NT) + wide_bias(query_bias)).astype(bf16)
    query_cols = query_cols * jnp.bfloat16(1.0 / HEAD_DIM**0.5)
    value_cols = (dot(value_weight_t[...], sequence, NT) + wide_bias(value_bias)).astype(bf16)
    for head in range(heads):
        own = slice(head * HEAD_DIM, (head + 1) * HEAD_DIM)
        half = (head % 2) * HEAD_DIM
        queries_t[head, half : half + HEAD_DIM, :] = query_cols[own]
        values_t[head, :HEAD_DIM, :] = value_cols[own]

    low[...] = jnp.ones_like(low)
    high[...] = jnp.ones_like(high)

    @pl.loop(0, heads // unroll)
    def _(group):
        for offset in range(unroll):
            head = group * unroll + offset
            sums = head_sums(dot(keys[head // 2], queries_t[head]), values_t[head], False)
            denominators = sums[HEAD_DIM : HEAD_DIM + 8]
            low[...] = jnp.minimum(low[...], denominators)
            high[...] = jnp.maximum(high[...], denominators)
            put_context(context_t, head, sums)

    in_range = (jnp.min(low[...]) > 1.0 / SAFE) & (jnp.max(high[...]) < SAFE)

    @pl.when(jnp.logical_not(in_range))
    def _():
        @pl.loop(0, heads)
        def _(head):
            sums = head_sums(dot(keys[head // 2], queries_t[head]), values_t[head], True)
            put_context(context_t, head, sums)

    done = context_t[...].T
    context[...] = done
    first_context[...] = done[:ROW_TILE]
    first_tokens[...] = sequence[:ROW_TILE]


def attention(tokens, qkv_weight, layer_biases):
    rows, width = tokens.shape
    count = rows // SEQ_LEN
    heads = width // HEAD_DIM
    by_sequence = lambda i: (i, 0)
    whole = lambda i: (0, 0)
    return pl.pallas_call(
        functools.partial(attention_kernel, 3),
        grid=(count,),
        in_specs=[
            pl.BlockSpec((SEQ_LEN, width), by_sequence),
            pl.BlockSpec((width, 3 * width), whole, pipeline_mode=pl.Buffered(1)),
            pl.BlockSpec((6, width), whole),
        ],
        out_specs=[
            pl.BlockSpec((SEQ_LEN, width), by_sequence),
            pl.BlockSpec((ROW_TILE, width), by_sequence),
            pl.BlockSpec((ROW_TILE, width), by_sequence),
        ],
        out_shape=[
            jax.ShapeDtypeStruct((rows, width), bf16),
            jax.ShapeDtypeStruct((ROW_TILE * count, width), bf16),
            jax.ShapeDtypeStruct((ROW_TILE * count, width), bf16),
        ],
        scratch_shapes=[
            pltpu.VMEM((width, width), bf16),
            pltpu.VMEM((width, width), bf16),
            pltpu.VMEM((width, LANES), f32),
            pltpu.VMEM((width, LANES), f32),
            pltpu.VMEM((heads // 2, SEQ_LEN, PAIR), bf16),
            pltpu.VMEM((heads, PAIR, SEQ_LEN), bf16),
            pltpu.VMEM((heads, V_ROWS, SEQ_LEN), bf16),
            pltpu.VMEM((width, SEQ_LEN), bf16),
            pltpu.VMEM((8, SEQ_LEN), f32),
            pltpu.VMEM((8, SEQ_LEN), f32),
        ],
        compiler_params=pltpu.CompilerParams(vmem_limit_bytes=VMEM_BYTES),
        name="attention",
    )(tokens, qkv_weight, layer_biases)


def layer_tail(tokens, context, out_weight, up_weight, down_weight, ffn_bias, biases, gains):
    attended = dot(context, out_weight) + biases[2:3]
    middle = norm_rows(tokens.astype(f32) + attended, gains[0:1], biases[3:4]).astype(bf16)
    hidden = gelu(dot(middle, up_weight) + ffn_bias).astype(bf16)
    branch = dot(hidden, down_weight) + biases[4:5]
    return norm_rows(middle.astype(f32) + branch, gains[1:2], biases[5:6]).astype(bf16)


def orthonormal_rows(factor):
    index = lax.broadcasted_iota(jnp.int32, factor.shape, 0)
    for row in range(factor.shape[0]):
        vector = factor[row : row + 1]
        vector = vector * lax.rsqrt(jnp.sum(vector * vector, -1, keepdims=True) + 1e-06)
        along = jnp.sum(factor * vector, -1, keepdims=True)
        factor = jnp.where(index > row, factor - along * vector, factor)
        factor = jnp.where(index == row, vector, factor)
    return factor


def exchange(slots, send_sem, recv_sem, value, me, count, device_of):
    slots[me] = value
    copies = []
    for step in range(1, count):
        copy = pltpu.make_async_remote_copy(
            src_ref=slots.at[me],
            dst_ref=slots.at[me],
            send_sem=send_sem.at[step],
            recv_sem=recv_sem.at[me],
            device_id=device_of(lax.rem(me + step, count)),
            device_id_type=pl.DeviceIdType.MESH,
        )
        copy.start()
        copies.append(copy)
    for step in range(1, count):
        source = lax.rem(me + count - step, count)
        pltpu.make_async_remote_copy(
            src_ref=slots.at[source],
            dst_ref=slots.at[source],
            send_sem=send_sem.at[step],
            recv_sem=recv_sem.at[source],
            device_id=device_of(source),
            device_id_type=pl.DeviceIdType.MESH,
        ).wait_recv()
    for copy in copies:
        copy.wait_send()
    total = slots[0]
    for other in range(1, count):
        total = total + slots[other]
    return total


def ramp_kernel(
    n_wide,
    n_narrow,
    labels,
    first_tokens,
    first_context,
    out_weight,
    up_weight,
    down_weight,
    ffn_bias,
    layer_biases,
    norm_gains,
    pool_weight,
    class_weight_t,
    ramp_biases,
    start_t,
    error,
    basis_out,
    factor_out,
    head_out,
    rows_out,
    grads_out,
    bias_row,
    narrow_one,
    wide_one,
    narrow_two,
    wide_two,
    send_sem,
    recv_sem,
):
    wide, narrow = lax.axis_index("wide"), lax.axis_index("narrow")
    width = error.shape[1]
    rank = start_t.shape[0]
    classes = class_weight_t.shape[0]
    rows = first_tokens.shape[0]

    along_narrow = lambda other: (wide, other)
    along_wide = lambda other: (other, narrow)

    barrier = pltpu.get_barrier_semaphore()
    for step in range(1, n_narrow):
        pl.semaphore_signal(
            barrier,
            inc=1,
            device_id=along_narrow(lax.rem(narrow + step, n_narrow)),
            device_id_type=pl.DeviceIdType.MESH,
        )
    for step in range(1, n_wide):
        pl.semaphore_signal(
            barrier,
            inc=1,
            device_id=along_wide(lax.rem(wide + step, n_wide)),
            device_id_type=pl.DeviceIdType.MESH,
        )
    pl.semaphore_wait(barrier, n_narrow + n_wide - 2)

    bias_row[...] = jnp.zeros_like(bias_row)
    bias_row[:, : width + classes] = ramp_biases[...]

    first_rows = layer_tail(
        first_tokens[...],
        first_context[...],
        out_weight[...],
        up_weight[...],
        down_weight[...],
        ffn_bias[...],
        layer_biases[...],
        norm_gains[...],
    )
    class_low = jnp.concatenate(
        [class_weight_t[...], jnp.zeros((LANES - classes, width), f32)], 0
    ).astype(bf16)
    pre = dot(first_rows, pool_weight[...].astype(bf16)) + bias_row[:, :width]
    pooled = jnp.tanh(pre)
    pooled_low = pooled.astype(bf16)
    logits = dot(pooled_low, class_low, NT) + bias_row[:, width:]
    lane = lax.broadcasted_iota(jnp.int32, logits.shape, 1)
    row = lax.broadcasted_iota(jnp.int32, logits.shape, 0)
    target = jnp.full(logits.shape, -1, jnp.int32)
    for index in range(rows // ROW_TILE):
        target = jnp.where(row == index * ROW_TILE, labels[index], target)
    logits = jnp.where(lane < classes, logits, -jnp.inf)
    powers = jnp.exp(logits - jnp.max(logits, -1, keepdims=True))
    softened = powers / jnp.sum(powers, -1, keepdims=True)
    grad_logits = softened - (lane == target).astype(f32)
    grad_logits = jnp.where(row % ROW_TILE == 0, grad_logits, 0.0).astype(bf16)
    grad_class = dot(grad_logits, pooled_low, TN)[:8]
    grad_pooled = dot(grad_logits, class_low)
    grad_pre = (grad_pooled * (1.0 - pooled * pooled)).astype(bf16)
    rows_wide = first_rows.astype(f32)
    grads_wide = grad_pre.astype(f32)
    bias_sum = jnp.sum(grads_wide, 0, keepdims=True)
    logit_sum = jnp.concatenate(
        [
            jnp.sum(grad_logits.astype(f32), 0, keepdims=True),
            jnp.zeros((1, width - LANES), f32),
        ],
        1,
    )
    index = lax.broadcasted_iota(jnp.int32, grad_class.shape, 0)
    head = jnp.where(index == classes, bias_sum, grad_class)
    head = jnp.where(index == classes + 1, logit_sum, head)

    factor = dot_full(start_t[...], error[...], NT)
    factor = factor + dot_full(dot_full(start_t[...], grads_wide, NT), rows_wide)

    total = exchange(
        narrow_one,
        send_sem.at[0],
        recv_sem.at[0],
        jnp.concatenate([factor, head], 0),
        narrow,
        n_narrow,
        along_narrow,
    )
    total = exchange(
        wide_one, send_sem.at[1], recv_sem.at[1], total, wide, n_wide, along_wide
    )
    head_out[...] = total[rank:]
    basis = orthonormal_rows(total[:rank])
    basis_out[...] = basis
    factor = dot_full(basis, error[...])
    factor = factor + dot_full(dot_full(basis, rows_wide, NT), grads_wide)
    factor = exchange(
        narrow_two, send_sem.at[2], recv_sem.at[2], factor, narrow, n_narrow, along_narrow
    )
    factor_out[...] = exchange(
        wide_two, send_sem.at[3], recv_sem.at[3], factor, wide, n_wide, along_wide
    )
    rows_out[...] = first_rows
    grads_out[...] = grad_pre


def ramp(n_wide, n_narrow, labels, *operands):
    first_tokens = operands[0]
    start_t = operands[11]
    rank, width = start_t.shape
    rows = first_tokens.shape[0]
    most = max(n_wide, n_narrow)
    vmem = pl.BlockSpec(memory_space=pltpu.VMEM)
    return pl.pallas_call(
        functools.partial(ramp_kernel, n_wide, n_narrow),
        in_specs=[pl.BlockSpec(memory_space=pltpu.SMEM)] + [vmem] * len(operands),
        out_specs=[vmem] * 5,
        out_shape=[
            jax.ShapeDtypeStruct((rank, width), f32),
            jax.ShapeDtypeStruct((rank, width), f32),
            jax.ShapeDtypeStruct((8, width), f32),
            jax.ShapeDtypeStruct((rows, width), bf16),
            jax.ShapeDtypeStruct((rows, width), bf16),
        ],
        scratch_shapes=[
            pltpu.VMEM((1, width + LANES), f32),
            pltpu.VMEM((n_narrow, rank + 8, width), f32),
            pltpu.VMEM((n_wide, rank + 8, width), f32),
            pltpu.VMEM((n_narrow, rank, width), f32),
            pltpu.VMEM((n_wide, rank, width), f32),
            pltpu.SemaphoreType.DMA((4, most)),
            pltpu.SemaphoreType.DMA((4, most)),
        ],
        compiler_params=pltpu.CompilerParams(
            vmem_limit_bytes=VMEM_BYTES, collective_id=0, has_side_effects=True
        ),
        name="ramp",
    )(labels, *operands)


def finish_kernel(
    devices,
    tokens,
    context,
    out_weight,
    up_weight,
    down_weight,
    ffn_bias,
    layer_biases,
    norm_gains,
    basis_part,
    factor,
    rows_part,
    grads,
    head,
    error,
    pool_weight,
    pool_moment,
    class_weight_t,
    class_moment_t,
    ramp_biases,
    bias_moment,
    layer_out,
    error_new,
    pool_weight_new,
    pool_moment_new,
    class_weight_new,
    class_moment_new,
    ramp_biases_new,
    bias_moment_new,
):
    width = tokens.shape[1]
    classes = class_weight_t.shape[0]
    layer_out[...] = layer_tail(
        tokens[...],
        context[...],
        out_weight[...],
        up_weight[...],
        down_weight[...],
        ffn_bias[...],
        layer_biases[...],
        norm_gains[...],
    )
    approx = dot_full(basis_part[...], factor[...], TN)
    combined = dot(rows_part[...], grads[...], TN) + error[...]
    error_new[...] = combined - approx / devices
    moment = MOMENTUM * pool_moment[...] + approx
    pool_moment_new[...] = moment
    pool_weight_new[...] = pool_weight[...] - RATE_POOL * moment

    @pl.when(pl.program_id(0) == 0)
    def _():
        moment = MOMENTUM * class_moment_t[...] + head[:classes]
        class_moment_new[...] = moment
        class_weight_new[...] = class_weight_t[...] - RATE_HEAD * moment
        total = jnp.concatenate(
            [head[classes : classes + 1], head[classes + 1 : classes + 2, :classes]], 1
        )
        moment = MOMENTUM * bias_moment[...] + total
        bias_moment_new[...] = moment
        ramp_biases_new[...] = ramp_biases[...] - RATE_BIAS * moment


def finish(devices, *operands):
    rows, width = operands[0].shape
    steps = rows // BLOCK
    part = width // steps
    once = pl.Buffered(1)
    by_rows = pl.BlockSpec((BLOCK, width), lambda i: (i, 0))
    by_part = pl.BlockSpec((part, width), lambda i: (i, 0))
    by_lanes = lambda array: pl.BlockSpec((array.shape[0], part), lambda i: (0, i))
    whole = lambda array: pl.BlockSpec(array.shape, lambda i: (0, 0), pipeline_mode=once)
    kinds = "tthhhhhhlhlhhpppwwww"
    specs = []
    for kind, operand in zip(kinds, operands, strict=True):
        if kind == "t":
            specs.append(by_rows)
        elif kind == "p":
            specs.append(by_part)
        elif kind == "l":
            specs.append(by_lanes(operand))
        else:
            specs.append(whole(operand))
    like = lambda array: jax.ShapeDtypeStruct(array.shape, array.dtype)
    small = lambda array: pl.BlockSpec(array.shape, lambda i: (0, 0))
    error, pool_weight, pool_moment = operands[13:16]
    rest = operands[16:20]
    return pl.pallas_call(
        functools.partial(finish_kernel, devices),
        grid=(steps,),
        in_specs=specs,
        out_specs=[by_rows, by_part, by_part, by_part] + [small(a) for a in rest],
        out_shape=[
            like(a) for a in (operands[0], error, pool_weight, pool_moment, *rest)
        ],
        compiler_params=pltpu.CompilerParams(vmem_limit_bytes=VMEM_BYTES),
        name="finish",
    )(*operands)


def body(
    n_wide,
    n_narrow,
    tokens,
    labels,
    qkv_weight,
    out_weight,
    up_weight,
    down_weight,
    ffn_bias,
    layer_biases,
    norm_gains,
    pool_weight,
    pool_moment,
    class_weight,
    class_moment,
    ramp_biases,
    bias_moment,
    start_factor,
    error_buffer,
):
    ffn_row = ffn_bias.reshape(1, -1)
    ramp_row = ramp_biases.reshape(1, -1)
    moment_row = bias_moment.reshape(1, -1)
    context, first_context, first_tokens = attention(tokens, qkv_weight, layer_biases)
    basis, factor, head, first_rows, grads = ramp(
        n_wide,
        n_narrow,
        labels,
        first_tokens,
        first_context,
        out_weight,
        up_weight,
        down_weight,
        ffn_row,
        layer_biases,
        norm_gains,
        pool_weight,
        class_weight.T,
        ramp_row,
        start_factor.T,
        error_buffer,
    )
    (
        layer_out,
        error_new,
        pool_weight_new,
        pool_moment_new,
        class_weight_new,
        class_moment_new,
        ramp_biases_new,
        bias_moment_new,
    ) = finish(
        n_wide * n_narrow,
        tokens,
        context,
        out_weight,
        up_weight,
        down_weight,
        ffn_row,
        layer_biases,
        norm_gains,
        basis,
        factor,
        first_rows,
        grads,
        head,
        error_buffer,
        pool_weight,
        pool_moment,
        class_weight.T,
        class_moment.T,
        ramp_row,
        moment_row,
    )
    return (
        layer_out,
        pool_moment_new,
        pool_weight_new,
        class_moment_new.T,
        class_weight_new.T,
        bias_moment_new.reshape(-1),
        ramp_biases_new.reshape(-1),
        error_new,
        factor.T,
    )


def solution(mesh):
    split = P(("wide", "narrow"), None)
    in_specs = (split, P(("wide", "narrow"))) + (P(),) * 14 + (split,)
    out_specs = (split,) + (P(),) * 6 + (split, P())
    return jax.shard_map(
        functools.partial(body, mesh.shape["wide"], mesh.shape["narrow"]),
        mesh=mesh,
        in_specs=in_specs,
        out_specs=out_specs,
        check_vma=False,
    )
```

```python
import functools

import jax
import jax.numpy as jnp
from jax import lax
from jax.experimental import pallas as pl
from jax.experimental.pallas import tpu as pltpu
from jax.sharding import PartitionSpec as P

HEAD_DIM = 64
SEQ_LEN = 1024
PAIR = 128
V_ROWS = 80
ROW_TILE = 16
LANES = 128
SLICE = 128
RAMP_STEPS = 6
LOG2E = 1.4426950408889634
SAFE = 2.0**100
MOMENTUM = 0.9
RATE_POOL = 0.03
RATE_HEAD = 0.002
RATE_BIAS = 0.03
MIB = 1024 * 1024

f32 = jnp.float32
bf16 = jnp.bfloat16
NT = ((1,), (1,))
TN = ((0,), (0,))


def dot(left, right, contract=((1,), (0,))):
    return lax.dot_general(left, right, (contract, ((), ())), preferred_element_type=f32)


def norm_rows(values, gain, shift):
    centred = values - jnp.mean(values, -1, keepdims=True)
    variance = jnp.mean(centred * centred, -1, keepdims=True)
    return centred * lax.rsqrt(variance + 1e-12) * gain + shift


def gelu(values):
    half = 0.5 * values
    return half * lax.erf(values * 0.7071067811865476) + half


def head_sums(scores, values_aug, shifted):
    if shifted:
        scores = scores - jnp.max(scores, 0, keepdims=True)
    return dot(values_aug, jnp.exp2(scores * LOG2E).astype(bf16))


def put_context(context_t, head, sums):
    scale = 1.0 / sums[HEAD_DIM : HEAD_DIM + 8]
    groups = [sums[g : g + 8] * scale for g in range(0, HEAD_DIM, 8)]
    rows = pl.ds(pl.multiple_of(head * HEAD_DIM, HEAD_DIM), HEAD_DIM)
    context_t[rows, :] = jnp.concatenate(groups, 0).astype(bf16)


def attention_kernel(
    unroll,
    tokens,
    qkv_weight,
    layer_biases,
    context,
    query_weight_t,
    value_weight_t,
    query_bias,
    value_bias,
    keys,
    queries_t,
    values_t,
    context_t,
    low,
    high,
):
    length, width = tokens.shape
    heads = width // HEAD_DIM

    @pl.when(pl.program_id(0) == 0)
    def _():
        query_weight_t[...] = qkv_weight[:, :width].T
        value_weight_t[...] = qkv_weight[:, 2 * width :].T
        columns = jnp.concatenate([layer_biases[...], jnp.zeros((2, width), f32)], 0).T
        query_bias[...] = jnp.broadcast_to(columns[:, 0:1], (width, LANES))
        value_bias[...] = jnp.broadcast_to(columns[:, 1:2], (width, LANES))
        queries_t[...] = jnp.zeros_like(queries_t)
        values_t[:, HEAD_DIM:, :] = jnp.ones((heads, V_ROWS - HEAD_DIM, length), bf16)

    def wide_bias(bias):
        return jnp.concatenate([bias[...]] * (length // LANES), 1)

    sequence = tokens[...]
    key_rows = dot(sequence, qkv_weight[:, width : 2 * width]).astype(bf16)
    for pair in range(heads // 2):
        keys[pair] = key_rows[:, pair * PAIR : (pair + 1) * PAIR]
    query_cols = (dot(query_weight_t[...], sequence, NT) + wide_bias(query_bias)).astype(bf16)
    query_cols = query_cols * jnp.bfloat16(1.0 / HEAD_DIM**0.5)
    value_cols = (dot(value_weight_t[...], sequence, NT) + wide_bias(value_bias)).astype(bf16)
    for head in range(heads):
        own = slice(head * HEAD_DIM, (head + 1) * HEAD_DIM)
        half = (head % 2) * HEAD_DIM
        queries_t[head, half : half + HEAD_DIM, :] = query_cols[own]
        values_t[head, :HEAD_DIM, :] = value_cols[own]

    low[...] = jnp.ones_like(low)
    high[...] = jnp.ones_like(high)

    @pl.loop(0, heads // unroll)
    def _(group):
        for offset in range(unroll):
            head = group * unroll + offset
            sums = head_sums(dot(keys[head // 2], queries_t[head]), values_t[head], False)
            denominators = sums[HEAD_DIM : HEAD_DIM + 8]
            low[...] = jnp.minimum(low[...], denominators)
            high[...] = jnp.maximum(high[...], denominators)
            put_context(context_t, head, sums)

    in_range = (jnp.min(low[...]) > 1.0 / SAFE) & (jnp.max(high[...]) < SAFE)

    @pl.when(jnp.logical_not(in_range))
    def _():
        @pl.loop(0, heads)
        def _(head):
            sums = head_sums(dot(keys[head // 2], queries_t[head]), values_t[head], True)
            put_context(context_t, head, sums)

    context[...] = context_t[...].T


def attention(tokens, qkv_weight, layer_biases):
    rows, width = tokens.shape
    count = rows // SEQ_LEN
    heads = width // HEAD_DIM
    by_sequence = lambda i: (i, 0)
    whole = lambda i: (0, 0)
    return pl.pallas_call(
        functools.partial(attention_kernel, 3),
        grid=(count,),
        in_specs=[
            pl.BlockSpec((SEQ_LEN, width), by_sequence),
            pl.BlockSpec((width, 3 * width), whole, pipeline_mode=pl.Buffered(1)),
            pl.BlockSpec((6, width), whole),
        ],
        out_specs=pl.BlockSpec((SEQ_LEN, width), by_sequence),
        out_shape=jax.ShapeDtypeStruct((rows, width), bf16),
        scratch_shapes=[
            pltpu.VMEM((width, width), bf16),
            pltpu.VMEM((width, width), bf16),
            pltpu.VMEM((width, LANES), f32),
            pltpu.VMEM((width, LANES), f32),
            pltpu.VMEM((heads // 2, SEQ_LEN, PAIR), bf16),
            pltpu.VMEM((heads, PAIR, SEQ_LEN), bf16),
            pltpu.VMEM((heads, V_ROWS, SEQ_LEN), bf16),
            pltpu.VMEM((width, SEQ_LEN), bf16),
            pltpu.VMEM((8, SEQ_LEN), f32),
            pltpu.VMEM((8, SEQ_LEN), f32),
        ],
        compiler_params=pltpu.CompilerParams(vmem_limit_bytes=40 * MIB),
        name="attention",
    )(tokens, qkv_weight, layer_biases)


def layer_tail(tokens, context, out_weight, up_weight, down_weight, ffn_bias, biases, gains):
    width = out_weight.shape[1]
    tokens = tokens[...].reshape(-1, width)
    attended = dot(context[...].reshape(-1, width), out_weight[...]) + biases[2:3]
    middle = norm_rows(tokens.astype(f32) + attended, gains[0:1], biases[3:4]).astype(bf16)
    ffn_row = ffn_bias[...].reshape(1, -1)
    hidden = gelu(dot(middle, up_weight[...]) + ffn_row).astype(bf16)
    branch = dot(hidden, down_weight[...]) + biases[4:5]
    return norm_rows(middle.astype(f32) + branch, gains[1:2], biases[5:6]).astype(bf16)


def orthonormal_rows(factor):
    index = lax.broadcasted_iota(jnp.int32, factor.shape, 0)
    for row in range(factor.shape[0]):
        vector = factor[row : row + 1]
        vector = vector * lax.rsqrt(jnp.sum(vector * vector, -1, keepdims=True) + 1e-06)
        along = jnp.sum(factor * vector, -1, keepdims=True)
        factor = jnp.where(index > row, factor - along * vector, factor)
        factor = jnp.where(index == row, vector, factor)
    return factor


def split(values):
    first = values.astype(bf16).astype(f32)
    second = (values - first).astype(bf16).astype(f32)
    return first, second, values - first - second


def stacked(values):
    return jnp.concatenate(split(values), 0).astype(bf16)


def folded(values):
    rows = values.shape[0] // 3
    return values[:rows] + values[rows : 2 * rows] + values[2 * rows :]


class Exchange:
    def __init__(self, slots, send_sem, recv_sem, me, count, device_of):
        self.slots, self.send_sem, self.recv_sem = slots, send_sem, recv_sem
        self.me, self.count, self.device_of = me, count, device_of

    def copy(self, step, slot, device):
        return pltpu.make_async_remote_copy(
            src_ref=self.slots.at[slot],
            dst_ref=self.slots.at[slot],
            send_sem=self.send_sem.at[step],
            recv_sem=self.recv_sem.at[slot],
            device_id=self.device_of(device),
            device_id_type=pl.DeviceIdType.MESH,
        )

    def greet(self, barrier):
        for step in range(1, self.count):
            pl.semaphore_signal(
                barrier,
                inc=1,
                device_id=self.device_of(lax.rem(self.me + step, self.count)),
                device_id_type=pl.DeviceIdType.MESH,
            )

    def start(self, value):
        self.slots[self.me] = value
        for step in range(1, self.count):
            self.copy(step, self.me, lax.rem(self.me + step, self.count)).start()

    def total(self):
        for step in range(1, self.count):
            source = lax.rem(self.me + self.count - step, self.count)
            self.copy(step, source, source).wait_recv()
            self.copy(step, self.me, lax.rem(self.me + step, self.count)).wait_send()
        total = self.slots[0]
        for other in range(1, self.count):
            total = total + self.slots[other]
        return total


def ramp_kernel(
    n_wide,
    n_narrow,
    labels,
    tokens,
    context,
    out_weight,
    up_weight,
    down_weight,
    ffn_bias,
    layer_biases,
    norm_gains,
    pool_weight,
    class_weight_t,
    ramp_biases,
    start_t,
    error,
    layer_part,
    basis_out,
    factor_out,
    head_out,
    rows_out,
    grads_out,
    bias_row,
    error_high,
    error_low,
    factor_error,
    narrow_one,
    wide_one,
    narrow_two,
    wide_two,
    send_sem,
    recv_sem,
):
    step = pl.program_id(0)
    wide, narrow = lax.axis_index("wide"), lax.axis_index("narrow")
    count = tokens.shape[0]
    width = error.shape[1]
    rank = start_t.shape[0]
    classes = class_weight_t.shape[0]

    def group(index, slots, by_narrow):
        semaphores = send_sem.at[index], recv_sem.at[index]
        if by_narrow:
            return Exchange(slots, *semaphores, narrow, n_narrow, lambda i: (wide, i))
        return Exchange(slots, *semaphores, wide, n_wide, lambda i: (i, narrow))

    sum_one_narrow = group(0, narrow_one, True)
    sum_one_wide = group(1, wide_one, False)
    sum_two_narrow = group(2, narrow_two, True)
    sum_two_wide = group(3, wide_two, False)
    barrier = pltpu.get_barrier_semaphore()

    @pl.when(step == 0)
    def _():
        sum_one_narrow.greet(barrier)
        sum_one_wide.greet(barrier)
        bias_row[...] = jnp.zeros_like(bias_row)
        bias_row[:, : width + classes] = ramp_biases[...].reshape(1, -1)
        high = error[...].astype(bf16)
        low = (error[...] - high.astype(f32)).astype(bf16)
        error_high[...] = high
        error_low[...] = low
        start = stacked(start_t[...])
        factor_error[...] = folded(dot(start, high, NT) + dot(start, low, NT))

    rows = layer_tail(
        tokens, context, out_weight, up_weight, down_weight, ffn_bias, layer_biases, norm_gains
    )
    layer_part[...] = rows.reshape(layer_part.shape)

    @pl.when(step == 0)
    def _():
        first_rows = jnp.concatenate(
            [layer_part[index, :ROW_TILE] for index in range(count)], 0
        )
        class_low = jnp.concatenate(
            [class_weight_t[...], jnp.zeros((LANES - classes, width), f32)], 0
        ).astype(bf16)
        pre = dot(first_rows, pool_weight[...].astype(bf16)) + bias_row[:, :width]
        pooled = jnp.tanh(pre)
        pooled_low = pooled.astype(bf16)
        logits = dot(pooled_low, class_low, NT) + bias_row[:, width:]
        lane = lax.broadcasted_iota(jnp.int32, logits.shape, 1)
        row = lax.broadcasted_iota(jnp.int32, logits.shape, 0)
        target = jnp.full(logits.shape, -1, jnp.int32)
        for index in range(count):
            target = jnp.where(row == index * ROW_TILE, labels[index], target)
        logits = jnp.where(lane < classes, logits, -jnp.inf)
        powers = jnp.exp(logits - jnp.max(logits, -1, keepdims=True))
        softened = powers / jnp.sum(powers, -1, keepdims=True)
        grad_logits = softened - (lane == target).astype(f32)
        grad_logits = jnp.where(row % ROW_TILE == 0, grad_logits, 0.0).astype(bf16)
        grad_class = dot(grad_logits, pooled_low, TN)[:8]
        grad_pooled = dot(grad_logits, class_low)
        grad_pre = (grad_pooled * (1.0 - pooled * pooled)).astype(bf16)
        bias_sum = jnp.sum(grad_pre.astype(f32), 0, keepdims=True)
        logit_sum = jnp.concatenate(
            [
                jnp.sum(grad_logits.astype(f32), 0, keepdims=True),
                jnp.zeros((1, width - LANES), f32),
            ],
            1,
        )
        index = lax.broadcasted_iota(jnp.int32, grad_class.shape, 0)
        head = jnp.where(index == classes, bias_sum, grad_class)
        head = jnp.where(index == classes + 1, logit_sum, head)
        inner = folded(dot(stacked(start_t[...]), grad_pre, NT))
        factor = factor_error[...] + folded(dot(stacked(inner), first_rows))
        rows_out[...] = first_rows
        grads_out[...] = grad_pre
        pl.semaphore_wait(barrier, n_narrow + n_wide - 2)
        sum_one_narrow.start(jnp.concatenate([factor, head], 0))

    @pl.when(step == 1)
    def _():
        sum_one_wide.start(sum_one_narrow.total())

    @pl.when(step == 3)
    def _():
        total = sum_one_wide.total()
        head_out[...] = total[rank:]
        basis = orthonormal_rows(total[:rank])
        basis_out[...] = basis
        basis = stacked(basis)
        inner = folded(dot(basis, rows_out[...], NT))
        factor = folded(dot(basis, error_high[...]) + dot(basis, error_low[...]))
        sum_two_narrow.start(factor + folded(dot(stacked(inner), grads_out[...])))

    @pl.when(step == 4)
    def _():
        sum_two_wide.start(sum_two_narrow.total())

    @pl.when(step == 5)
    def _():
        factor_out[...] = sum_two_wide.total()


def ramp(n_wide, n_narrow, labels, *operands):
    tokens = operands[0]
    start_t = operands[11]
    rank, width = start_t.shape
    count = tokens.shape[0]
    most = max(n_wide, n_narrow)
    block = pl.BlockSpec((count, SLICE, width), lambda i: (0, i, 0))
    vmem = pl.BlockSpec(memory_space=pltpu.VMEM)
    first = ROW_TILE * count
    return pl.pallas_call(
        functools.partial(ramp_kernel, n_wide, n_narrow),
        grid=(RAMP_STEPS,),
        in_specs=[pl.BlockSpec(memory_space=pltpu.SMEM), block, block]
        + [vmem] * (len(operands) - 2),
        out_specs=[block] + [vmem] * 5,
        out_shape=[
            jax.ShapeDtypeStruct((count, RAMP_STEPS * SLICE, width), bf16),
            jax.ShapeDtypeStruct((rank, width), f32),
            jax.ShapeDtypeStruct((rank, width), f32),
            jax.ShapeDtypeStruct((8, width), f32),
            jax.ShapeDtypeStruct((first, width), bf16),
            jax.ShapeDtypeStruct((first, width), bf16),
        ],
        scratch_shapes=[
            pltpu.VMEM((1, width + LANES), f32),
            pltpu.VMEM((width, width), bf16),
            pltpu.VMEM((width, width), bf16),
            pltpu.VMEM((rank, width), f32),
            pltpu.VMEM((n_narrow, rank + 8, width), f32),
            pltpu.VMEM((n_wide, rank + 8, width), f32),
            pltpu.VMEM((n_narrow, rank, width), f32),
            pltpu.VMEM((n_wide, rank, width), f32),
            pltpu.SemaphoreType.DMA((4, most)),
            pltpu.SemaphoreType.DMA((4, most)),
        ],
        compiler_params=pltpu.CompilerParams(
            vmem_limit_bytes=40 * MIB, collective_id=0, has_side_effects=True
        ),
        name="ramp",
    )(labels, *operands)


def finish_kernel(
    devices,
    steps,
    tokens,
    context,
    layer_part,
    out_weight,
    up_weight,
    down_weight,
    ffn_bias,
    layer_biases,
    norm_gains,
    basis_part,
    factor,
    rows_part,
    grads,
    head,
    error,
    pool_weight,
    pool_moment,
    class_weight_t,
    class_moment_t,
    ramp_biases,
    bias_moment,
    layer_out,
    error_new,
    pool_weight_new,
    pool_moment_new,
    class_weight_new,
    class_moment_new,
    ramp_biases_new,
    bias_moment_new,
    done,
    part_sem,
    done_sem,
):
    step = pl.program_id(0)
    count, _, width = tokens.shape
    classes = class_weight_t.shape[0]
    ready = layer_part.shape[1]

    part_copy = pltpu.make_async_copy(layer_part, layer_out.at[:, pl.ds(0, ready)], part_sem)

    def done_copy(index):
        where = pl.ds(ready + index * SLICE, SLICE)
        return pltpu.make_async_copy(done.at[index], layer_out.at[:, where], done_sem.at[index])

    @pl.when(step == 0)
    def _():
        part_copy.start()

    high, middle, low = split(basis_part[...])
    left = jnp.concatenate([high, high, middle, middle, high, low], 0).astype(bf16)
    high, middle, low = split(factor[...])
    right = jnp.concatenate([high, middle, high, middle, low, high], 0).astype(bf16)
    approx = dot(left, right, TN)
    combined = dot(rows_part[...], grads[...], TN) + error[...]
    error_new[...] = combined - approx * (1.0 / devices)
    moment = MOMENTUM * pool_moment[...] + approx
    pool_moment_new[...] = moment
    pool_weight_new[...] = pool_weight[...] - RATE_POOL * moment

    rows = layer_tail(
        tokens, context, out_weight, up_weight, down_weight, ffn_bias, layer_biases, norm_gains
    )
    for index in range(steps):

        @pl.when(step == index)
        def _():
            done[index] = rows.reshape(count, SLICE, width)
            done_copy(index).start()

    @pl.when(step == 0)
    def _():
        moment = MOMENTUM * class_moment_t[...] + head[:classes]
        class_moment_new[...] = moment
        class_weight_new[...] = class_weight_t[...] - RATE_HEAD * moment
        total = jnp.concatenate(
            [head[classes : classes + 1], head[classes + 1 : classes + 2, :classes]], 1
        )
        moment = MOMENTUM * bias_moment[...] + total.reshape(-1)
        bias_moment_new[...] = moment
        ramp_biases_new[...] = ramp_biases[...] - RATE_BIAS * moment

    @pl.when(step == steps - 1)
    def _():
        part_copy.wait()
        for index in range(steps):
            done_copy(index).wait()


def finish(devices, *operands):
    count, length, width = operands[0].shape
    steps = length // SLICE - RAMP_STEPS
    part = width // steps
    block = pl.BlockSpec((count, SLICE, width), lambda i: (0, i + RAMP_STEPS, 0))
    by_part = pl.BlockSpec((part, width), lambda i: (i, 0))
    vmem = pl.BlockSpec(memory_space=pltpu.VMEM)
    anywhere = pl.BlockSpec(memory_space=pl.ANY)
    specs = []
    for kind, operand in zip("bbavvvvvvlvlvvpppvvvv", operands, strict=True):
        lanes = pl.BlockSpec((operand.shape[0], part), lambda i: (0, i))
        specs.append({"b": block, "a": anywhere, "v": vmem, "l": lanes, "p": by_part}[kind])
    like = lambda array: jax.ShapeDtypeStruct(array.shape, array.dtype)
    return pl.pallas_call(
        functools.partial(finish_kernel, devices, steps),
        grid=(steps,),
        in_specs=specs,
        out_specs=[anywhere] + [by_part] * 3 + [vmem] * 4,
        out_shape=[like(operands[0])] + [like(array) for array in operands[14:21]],
        scratch_shapes=[
            pltpu.VMEM((steps, count, SLICE, width), bf16),
            pltpu.SemaphoreType.DMA,
            pltpu.SemaphoreType.DMA((steps,)),
        ],
        compiler_params=pltpu.CompilerParams(vmem_limit_bytes=40 * MIB),
        name="finish",
    )(*operands)


def body(
    n_wide,
    n_narrow,
    tokens,
    labels,
    qkv_weight,
    out_weight,
    up_weight,
    down_weight,
    ffn_bias,
    layer_biases,
    norm_gains,
    pool_weight,
    pool_moment,
    class_weight,
    class_moment,
    ramp_biases,
    bias_moment,
    start_factor,
    error_buffer,
):
    width = tokens.shape[1]
    context = attention(tokens, qkv_weight, layer_biases).reshape(-1, SEQ_LEN, width)
    sequences = tokens.reshape(-1, SEQ_LEN, width)
    layer = (out_weight, up_weight, down_weight, ffn_bias, layer_biases, norm_gains)
    layer_part, basis, factor, head, first_rows, grads = ramp(
        n_wide,
        n_narrow,
        labels,
        sequences,
        context,
        *layer,
        pool_weight,
        class_weight.T,
        ramp_biases,
        start_factor.T,
        error_buffer,
    )
    (
        layer_out,
        error_new,
        pool_weight_new,
        pool_moment_new,
        class_weight_new,
        class_moment_new,
        ramp_biases_new,
        bias_moment_new,
    ) = finish(
        n_wide * n_narrow,
        sequences,
        context,
        layer_part,
        *layer,
        basis,
        factor,
        first_rows,
        grads,
        head,
        error_buffer,
        pool_weight,
        pool_moment,
        class_weight.T,
        class_moment.T,
        ramp_biases,
        bias_moment,
    )
    return (
        layer_out.reshape(tokens.shape),
        pool_moment_new,
        pool_weight_new,
        class_moment_new.T,
        class_weight_new.T,
        bias_moment_new,
        ramp_biases_new,
        error_new,
        factor.T,
    )


def solution(mesh):
    rows = P(("wide", "narrow"), None)
    in_specs = (rows, P(("wide", "narrow"))) + (P(),) * 14 + (rows,)
    out_specs = (rows,) + (P(),) * 6 + (rows, P())
    return jax.shard_map(
        functools.partial(body, mesh.shape["wide"], mesh.shape["narrow"]),
        mesh=mesh,
        in_specs=in_specs,
        out_specs=out_specs,
        check_vma=False,
    )
```

```python
import functools

import jax
import jax.numpy as jnp
from jax import lax
from jax.experimental import pallas as pl
from jax.experimental.pallas import tpu as pltpu
from jax.sharding import PartitionSpec as P

HEAD_DIM = 64
SEQ_LEN = 1024
PAIR = 128
V_ROWS = 80
ROW_TILE = 16
LANES = 128
SLICE = 128
RAMP_STEPS = 6
LOG2E = 1.4426950408889634
SAFE = 2.0**100
MOMENTUM = 0.9
RATE_POOL = 0.03
RATE_HEAD = 0.002
RATE_BIAS = 0.03
MIB = 1024 * 1024
ATTENTION_MIB = 36
RAMP_MIB = 18
FINISH_MIB = 18

f32 = jnp.float32
bf16 = jnp.bfloat16
NT = ((1,), (1,))
TN = ((0,), (0,))


def in_hbm(array):
    return pltpu.with_memory_space_constraint(array, pltpu.HBM)


def dot(left, right, contract=((1,), (0,))):
    return lax.dot_general(left, right, (contract, ((), ())), preferred_element_type=f32)


def norm_rows(values, gain, shift):
    centred = values - jnp.mean(values, -1, keepdims=True)
    variance = jnp.mean(centred * centred, -1, keepdims=True)
    return centred * lax.rsqrt(variance + 1e-12) * gain + shift


def gelu(values):
    half = 0.5 * values
    return half * lax.erf(values * 0.7071067811865476) + half


def head_sums(scores, values_aug, shifted):
    if shifted:
        scores = scores - jnp.max(scores, 0, keepdims=True)
    return dot(values_aug, jnp.exp2(scores * LOG2E).astype(bf16))


def put_context(context_t, head, sums):
    scale = 1.0 / sums[HEAD_DIM : HEAD_DIM + 8]
    groups = [sums[g : g + 8] * scale for g in range(0, HEAD_DIM, 8)]
    rows = pl.ds(pl.multiple_of(head * HEAD_DIM, HEAD_DIM), HEAD_DIM)
    context_t[rows, :] = jnp.concatenate(groups, 0).astype(bf16)


def attention_kernel(unroll, carried, tokens, qkv_weight, layer_biases, *refs):
    sources, context, targets = refs[:carried], refs[carried], refs[carried + 1 :][:carried]
    (
        query_weight,
        key_weight,
        value_weight,
        query_weight_t,
        value_weight_t,
        query_bias,
        value_bias,
        sequences,
        keys,
        queries_t,
        values_t,
        context_t,
        done,
        low,
        high,
        weight_sem,
        token_sem,
        done_sem,
        carry_sem,
    ) = refs[2 * carried + 1 :]
    step = pl.program_id(0)
    steps = pl.num_programs(0)
    _, length, width = sequences.shape
    heads = width // HEAD_DIM

    def weight_copy(index, into):
        columns = qkv_weight.at[:, pl.ds(index * width, width)]
        return pltpu.make_async_copy(columns, into, weight_sem.at[index])

    def token_copy(index):
        rows = tokens.at[pl.ds(pl.multiple_of(index * length, length), length)]
        slot = lax.rem(index, 2)
        return pltpu.make_async_copy(rows, sequences.at[slot], token_sem.at[slot])

    def done_copy(index):
        rows = context.at[pl.ds(pl.multiple_of(index * length, length), length)]
        return pltpu.make_async_copy(done, rows, done_sem)

    carries = [
        pltpu.make_async_copy(source, target, carry_sem.at[index])
        for index, (source, target) in enumerate(zip(sources, targets, strict=True))
    ]
    query_copy = weight_copy(0, query_weight)
    key_copy = weight_copy(1, key_weight)
    value_copy = weight_copy(2, value_weight)

    @pl.when(step == 0)
    def _():
        query_copy.start()
        value_copy.start()
        token_copy(0).start()
        key_copy.start()
        columns = jnp.concatenate([layer_biases[...], jnp.zeros((2, width), f32)], 0).T
        query_bias[...] = jnp.broadcast_to(columns[:, 0:1], (width, LANES))
        value_bias[...] = jnp.broadcast_to(columns[:, 1:2], (width, LANES))
        queries_t[...] = jnp.zeros_like(queries_t)
        values_t[:, HEAD_DIM:, :] = jnp.ones((heads, V_ROWS - HEAD_DIM, length), bf16)
        query_copy.wait()
        query_weight_t[...] = query_weight[...].T
        value_copy.wait()
        value_weight_t[...] = value_weight[...].T
        key_copy.wait()
        for copy in carries:
            copy.start()

    token_copy(step).wait()

    @pl.when(step + 1 < steps)
    def _():
        token_copy(step + 1).start()

    def wide_bias(bias):
        return jnp.concatenate([bias[...]] * (length // LANES), 1)

    sequence = sequences[lax.rem(step, 2)]
    key_rows = dot(sequence, key_weight[...]).astype(bf16)
    for pair in range(heads // 2):
        keys[pair] = key_rows[:, pair * PAIR : (pair + 1) * PAIR]

    query_cols = ((dot(query_weight_t[...], sequence, NT) + wide_bias(query_bias)) * 0.125).astype(bf16)
    value_cols = (dot(value_weight_t[...], sequence, NT) + wide_bias(value_bias)).astype(bf16)
    for head in range(heads):
        own = slice(head * HEAD_DIM, (head + 1) * HEAD_DIM)
        half = (head % 2) * HEAD_DIM
        queries_t[head, half : half + HEAD_DIM, :] = query_cols[own]
        values_t[head, :HEAD_DIM, :] = value_cols[own]

    low[...] = jnp.ones_like(low)
    high[...] = jnp.ones_like(high)

    @pl.loop(0, heads // unroll)
    def _(group):
        for offset in range(unroll):
            head = group * unroll + offset
            sums = head_sums(dot(keys[head // 2], queries_t[head]), values_t[head], False)
            denominators = sums[HEAD_DIM : HEAD_DIM + 8]
            low[...] = jnp.minimum(low[...], denominators)
            high[...] = jnp.maximum(high[...], denominators)
            put_context(context_t, head, sums)

    in_range = (jnp.min(low[...]) > 1.0 / SAFE) & (jnp.max(high[...]) < SAFE)

    @pl.when(jnp.logical_not(in_range))
    def _():
        @pl.loop(0, heads)
        def _(head):
            sums = head_sums(dot(keys[head // 2], queries_t[head]), values_t[head], True)
            put_context(context_t, head, sums)

    @pl.when(step > 0)
    def _():
        done_copy(step - 1).wait()

    done[...] = context_t[...].T
    done_copy(step).start()

    @pl.when(step == steps - 1)
    def _():
        for copy in carries:
            copy.wait()
        done_copy(step).wait()


def attention(tokens, qkv_weight, layer_biases, carried):
    rows, width = tokens.shape
    count = rows // SEQ_LEN
    heads = width // HEAD_DIM
    hbm = pl.BlockSpec(memory_space=pltpu.HBM)
    square = pltpu.VMEM((width, width), bf16)
    return pl.pallas_call(
        functools.partial(attention_kernel, 3, len(carried)),
        grid=(count,),
        in_specs=[hbm, hbm, pl.BlockSpec((6, width), lambda i: (0, 0))] + [hbm] * len(carried),
        out_specs=[hbm] + [pl.BlockSpec(memory_space=pltpu.VMEM)] * len(carried),
        out_shape=[pltpu.HBM((rows, width), bf16)]
        + [pltpu.VMEM(array.shape, array.dtype) for array in carried],
        scratch_shapes=[square] * 5
        + [
            pltpu.VMEM((width, LANES), f32),
            pltpu.VMEM((width, LANES), f32),
            pltpu.VMEM((2, SEQ_LEN, width), bf16),
            pltpu.VMEM((heads // 2, SEQ_LEN, PAIR), bf16),
            pltpu.VMEM((heads, PAIR, SEQ_LEN), bf16),
            pltpu.VMEM((heads, V_ROWS, SEQ_LEN), bf16),
            pltpu.VMEM((width, SEQ_LEN), bf16),
            pltpu.VMEM((SEQ_LEN, width), bf16),
            pltpu.VMEM((8, SEQ_LEN), f32),
            pltpu.VMEM((8, SEQ_LEN), f32),
            pltpu.SemaphoreType.DMA((3,)),
            pltpu.SemaphoreType.DMA((2,)),
            pltpu.SemaphoreType.DMA,
            pltpu.SemaphoreType.DMA((len(carried),)),
        ],
        compiler_params=pltpu.CompilerParams(vmem_limit_bytes=ATTENTION_MIB * MIB),
        name="attention",
    )(in_hbm(tokens), in_hbm(qkv_weight), layer_biases, *[in_hbm(array) for array in carried])


def flat(block):
    return block[...].reshape(-1, block.shape[-1])


def to_middle(tokens, context, out_weight, biases, gains):
    attended = dot(flat(context), out_weight[...]) + biases[2:3]
    return norm_rows(flat(tokens).astype(f32) + attended, gains[0:1], biases[3:4]).astype(bf16)


def to_sums(middle, up_weight, down_weight, ffn_bias, biases):
    hidden = gelu(dot(middle, up_weight[...]) + ffn_bias[...].reshape(1, -1)).astype(bf16)
    return middle.astype(f32) + dot(hidden, down_weight[...]) + biases[4:5]


def to_layer(sums, biases, gains):
    return norm_rows(sums, gains[1:2], biases[5:6]).astype(bf16)


def orthonormal_rows(factor):
    index = lax.broadcasted_iota(jnp.int32, factor.shape, 0)
    for row in range(factor.shape[0]):
        vector = factor[row : row + 1]
        vector = vector * lax.rsqrt(jnp.sum(vector * vector, -1, keepdims=True) + 1e-06)
        along = jnp.sum(factor * vector, -1, keepdims=True)
        factor = jnp.where(index > row, factor - along * vector, factor)
        factor = jnp.where(index == row, vector, factor)
    return factor


def split(values):
    first = values.astype(bf16).astype(f32)
    second = (values - first).astype(bf16).astype(f32)
    return first, second, values - first - second


def stacked(values):
    return jnp.concatenate(split(values), 0).astype(bf16)


def folded(values):
    rows = values.shape[0] // 3
    return values[:rows] + values[rows : 2 * rows] + values[2 * rows :]


class Exchange:
    def __init__(self, slots, send_sem, recv_sem, me, count, device_of):
        self.slots, self.send_sem, self.recv_sem = slots, send_sem, recv_sem
        self.me, self.count, self.device_of = me, count, device_of

    def copy(self, step, slot, device):
        return pltpu.make_async_remote_copy(
            src_ref=self.slots.at[slot],
            dst_ref=self.slots.at[slot],
            send_sem=self.send_sem.at[step],
            recv_sem=self.recv_sem.at[slot],
            device_id=self.device_of(device),
            device_id_type=pl.DeviceIdType.MESH,
        )

    def greet(self, barrier):
        for step in range(1, self.count):
            pl.semaphore_signal(
                barrier,
                inc=1,
                device_id=self.device_of(lax.rem(self.me + step, self.count)),
                device_id_type=pl.DeviceIdType.MESH,
            )

    def start(self, value):
        self.slots[self.me] = value
        for step in range(1, self.count):
            self.copy(step, self.me, lax.rem(self.me + step, self.count)).start()

    def total(self):
        for step in range(1, self.count):
            source = lax.rem(self.me + self.count - step, self.count)
            self.copy(step, source, source).wait_recv()
            self.copy(step, self.me, lax.rem(self.me + step, self.count)).wait_send()
        total = self.slots[0]
        for other in range(1, self.count):
            total = total + self.slots[other]
        return total


def ramp_kernel(
    n_wide,
    n_narrow,
    labels,
    first_tokens,
    first_context,
    tokens,
    context,
    out_weight,
    up_weight,
    down_weight,
    ffn_bias,
    layer_biases,
    norm_gains,
    pool_weight,
    class_weight_t,
    ramp_biases,
    start_t,
    error,
    layer_part,
    middle,
    sums,
    basis_out,
    factor_out,
    head_out,
    rows_out,
    grads_out,
    next_middle,
    next_sums,
    bias_row,
    error_high,
    error_low,
    factor_error,
    narrow_one,
    wide_one,
    narrow_two,
    wide_two,
    send_sem,
    recv_sem,
):
    step = pl.program_id(0)
    wide, narrow = lax.axis_index("wide"), lax.axis_index("narrow")
    count = tokens.shape[0]
    width = error.shape[1]
    rank = start_t.shape[0]
    classes = class_weight_t.shape[0]

    def group(index, slots, by_narrow):
        semaphores = send_sem.at[index], recv_sem.at[index]
        if by_narrow:
            return Exchange(slots, *semaphores, narrow, n_narrow, lambda i: (wide, i))
        return Exchange(slots, *semaphores, wide, n_wide, lambda i: (i, narrow))

    sum_one_narrow = group(0, narrow_one, True)
    sum_one_wide = group(1, wide_one, False)
    sum_two_narrow = group(2, narrow_two, True)
    sum_two_wide = group(3, wide_two, False)
    barrier = pltpu.get_barrier_semaphore()

    @pl.when(step == 0)
    def _():
        sum_one_narrow.greet(barrier)
        sum_one_wide.greet(barrier)
        bias_row[...] = jnp.zeros_like(bias_row)
        bias_row[:, : width + classes] = ramp_biases[...].reshape(1, -1)
        high = error[...].astype(bf16)
        low = (error[...] - high.astype(f32)).astype(bf16)
        error_high[...] = high
        error_low[...] = low
        start = stacked(start_t[...])
        factor_error[...] = folded(dot(start, high, NT) + dot(start, low, NT))
        middle[...] = to_middle(
            first_tokens, first_context, out_weight, layer_biases, norm_gains
        )
        sums[...] = jnp.zeros_like(sums)

    next_middle[...] = to_middle(tokens, context, out_weight, layer_biases, norm_gains)
    next_sums[...] = to_sums(middle[...], up_weight, down_weight, ffn_bias, layer_biases)
    rows = to_layer(sums[...], layer_biases, norm_gains).reshape(count, SLICE, width)
    layer_part[jnp.maximum(step - 1, 0)] = rows
    middle[...] = next_middle[...]
    sums[...] = next_sums[...]

    @pl.when(step == 0)
    def _():
        first_sums = jnp.concatenate(
            [sums[pl.ds(index * SLICE, ROW_TILE)] for index in range(count)], 0
        )
        first_rows = to_layer(first_sums, layer_biases, norm_gains)
        class_low = jnp.concatenate(
            [class_weight_t[...], jnp.zeros((LANES - classes, width), f32)], 0
        ).astype(bf16)
        pre = dot(first_rows, pool_weight[...].astype(bf16)) + bias_row[:, :width]
        pooled = jnp.tanh(pre)
        pooled_low = pooled.astype(bf16)
        logits = dot(pooled_low, class_low, NT) + bias_row[:, width:]
        lane = lax.broadcasted_iota(jnp.int32, logits.shape, 1)
        row = lax.broadcasted_iota(jnp.int32, logits.shape, 0)
        target = jnp.full(logits.shape, -1, jnp.int32)
        for index in range(count):
            target = jnp.where(row == index * ROW_TILE, labels[index], target)
        logits = jnp.where(lane < classes, logits, -jnp.inf)
        powers = jnp.exp(logits - jnp.max(logits, -1, keepdims=True))
        softened = powers / jnp.sum(powers, -1, keepdims=True)
        grad_logits = softened - (lane == target).astype(f32)
        grad_logits = jnp.where(row % ROW_TILE == 0, grad_logits, 0.0).astype(bf16)
        grad_class = dot(grad_logits, pooled_low, TN)[:8]
        grad_pooled = dot(grad_logits, class_low)
        grad_pre = (grad_pooled * (1.0 - pooled * pooled)).astype(bf16)
        bias_sum = jnp.sum(grad_pre.astype(f32), 0, keepdims=True)
        logit_sum = jnp.concatenate(
            [
                jnp.sum(grad_logits.astype(f32), 0, keepdims=True),
                jnp.zeros((1, width - LANES), f32),
            ],
            1,
        )
        index = lax.broadcasted_iota(jnp.int32, grad_class.shape, 0)
        head = jnp.where(index == classes, bias_sum, grad_class)
        head = jnp.where(index == classes + 1, logit_sum, head)
        inner = folded(dot(stacked(start_t[...]), grad_pre, NT))
        factor = factor_error[...] + folded(dot(stacked(inner), first_rows))
        rows_out[...] = first_rows
        grads_out[...] = grad_pre
        pl.semaphore_wait(barrier, n_narrow + n_wide - 2)
        sum_one_narrow.start(jnp.concatenate([factor, head], 0))

    @pl.when(step == 1)
    def _():
        sum_one_wide.start(sum_one_narrow.total())

    @pl.when(step == 3)
    def _():
        total = sum_one_wide.total()
        head_out[...] = total[rank:]
        basis = orthonormal_rows(total[:rank])
        basis_out[...] = basis
        basis = stacked(basis)
        inner = folded(dot(basis, rows_out[...], NT))
        factor = folded(dot(basis, error_high[...]) + dot(basis, error_low[...]))
        sum_two_narrow.start(factor + folded(dot(stacked(inner), grads_out[...])))

    @pl.when(step == 4)
    def _():
        sum_two_wide.start(sum_two_narrow.total())

    @pl.when(step == 5)
    def _():
        factor_out[...] = sum_two_wide.total()


def ramp(n_wide, n_narrow, labels, tokens, context, *operands):
    start_t = operands[9]
    rank, width = start_t.shape
    count = tokens.shape[0]
    most = max(n_wide, n_narrow)
    shape = (count, SLICE, width)
    first_block = pl.BlockSpec(shape, lambda i: (0, 0, 0))
    next_block = pl.BlockSpec(shape, lambda i: (0, i + 1, 0))
    vmem = pl.BlockSpec(memory_space=pltpu.VMEM)
    first = ROW_TILE * count
    outs = [
        pltpu.VMEM((RAMP_STEPS - 1, *shape), bf16),
        pltpu.VMEM((count * SLICE, width), bf16),
        pltpu.VMEM((count * SLICE, width), f32),
        pltpu.VMEM((rank, width), f32),
        pltpu.VMEM((rank, width), f32),
        pltpu.VMEM((8, width), f32),
        pltpu.VMEM((first, width), bf16),
        pltpu.VMEM((first, width), bf16),
    ]
    return pl.pallas_call(
        functools.partial(ramp_kernel, n_wide, n_narrow),
        grid=(RAMP_STEPS,),
        in_specs=[pl.BlockSpec(memory_space=pltpu.SMEM)]
        + [first_block] * 2
        + [next_block] * 2
        + [vmem] * len(operands),
        out_specs=[vmem] * len(outs),
        out_shape=outs,
        scratch_shapes=[
            pltpu.VMEM((count * SLICE, width), bf16),
            pltpu.VMEM((count * SLICE, width), f32),
            pltpu.VMEM((1, width + LANES), f32),
            pltpu.VMEM((width, width), bf16),
            pltpu.VMEM((width, width), bf16),
            pltpu.VMEM((rank, width), f32),
            pltpu.VMEM((n_narrow, rank + 8, width), f32),
            pltpu.VMEM((n_wide, rank + 8, width), f32),
            pltpu.VMEM((n_narrow, rank, width), f32),
            pltpu.VMEM((n_wide, rank, width), f32),
            pltpu.SemaphoreType.DMA((4, most)),
            pltpu.SemaphoreType.DMA((4, most)),
        ],
        compiler_params=pltpu.CompilerParams(
            vmem_limit_bytes=RAMP_MIB * MIB, collective_id=0, has_side_effects=True
        ),
        name="ramp",
    )(labels, *[in_hbm(array) for array in (tokens, context, tokens, context)], *operands)


def finish_kernel(
    devices,
    tokens,
    context,
    layer_part,
    middle,
    sums,
    out_weight,
    up_weight,
    down_weight,
    ffn_bias,
    layer_biases,
    norm_gains,
    basis,
    factor,
    rows,
    grads,
    head,
    error,
    pool_weight,
    pool_moment,
    class_weight_t,
    class_moment_t,
    ramp_biases,
    bias_moment,
    layer_out,
    error_new,
    pool_weight_new,
    pool_moment_new,
    factor_new,
    class_weight_new,
    class_moment_new,
    ramp_biases_new,
    bias_moment_new,
    last_tokens,
    last_context,
    done,
    held,
    load_sem,
    part_sem,
    done_sem,
    store_sem,
):
    count, length, width = tokens.shape
    classes = class_weight_t.shape[0]
    ready = layer_part.shape[0]

    def block_of(array, index):
        return array.at[:, pl.ds(index * SLICE, SLICE)]

    parts = [
        pltpu.make_async_copy(layer_part.at[index], block_of(layer_out, index), part_sem.at[index])
        for index in range(ready)
    ]
    last = length // SLICE - 1
    loads = [
        pltpu.make_async_copy(block_of(source, last), into, load_sem.at[index])
        for index, (source, into) in enumerate([(tokens, last_tokens), (context, last_context)])
    ]
    stores = [
        pltpu.make_async_copy(held.at[index], into, store_sem.at[index])
        for index, into in enumerate([error_new, pool_weight_new, pool_moment_new])
    ]

    def done_copy(index):
        into = block_of(layer_out, ready + index)
        return pltpu.make_async_copy(done.at[index], into, done_sem.at[index])

    def finish_block(index, values):
        done[index] = to_layer(values, layer_biases, norm_gains).reshape(count, SLICE, width)
        done_copy(index).start()

    for copy in loads + parts:
        copy.start()
    finish_block(0, sums[...])
    high, mid, low = split(basis[...])
    left = jnp.concatenate([high, high, mid, mid, high, low], 0).astype(bf16)
    high, mid, low = split(factor[...])
    right = jnp.concatenate([high, mid, high, mid, low, high], 0).astype(bf16)
    approx = dot(left, right, TN)
    combined = dot(rows[...], grads[...], TN) + error[...]
    held[0] = combined - approx * (1.0 / devices)
    moment = MOMENTUM * pool_moment[...] + approx
    held[2] = moment
    held[1] = pool_weight[...] - RATE_POOL * moment
    for copy in stores:
        copy.start()
    factor_new[...] = factor[...]

    for copy in loads:
        copy.wait()
    last_middle = to_middle(last_tokens, last_context, out_weight, layer_biases, norm_gains)
    next_sums = to_sums(middle[...], up_weight, down_weight, ffn_bias, layer_biases)
    finish_block(1, next_sums)
    last_sums = to_sums(last_middle, up_weight, down_weight, ffn_bias, layer_biases)

    moment = MOMENTUM * class_moment_t[...] + head[:classes]
    class_moment_new[...] = moment
    class_weight_new[...] = class_weight_t[...] - RATE_HEAD * moment
    total = jnp.concatenate(
        [head[classes : classes + 1], head[classes + 1 : classes + 2, :classes]], 1
    )
    moment = MOMENTUM * bias_moment[...] + total.reshape(-1)
    bias_moment_new[...] = moment
    ramp_biases_new[...] = ramp_biases[...] - RATE_BIAS * moment

    finish_block(2, last_sums)
    for copy in parts + stores:
        copy.wait()
    for index in range(3):
        done_copy(index).wait()


def finish(devices, *operands):
    tokens = operands[0]
    count, length, width = tokens.shape
    vmem = pl.BlockSpec(memory_space=pltpu.VMEM)
    hbm = pl.BlockSpec(memory_space=pltpu.HBM)
    layer_part, factor = operands[2], operands[12]
    large = (tokens, *operands[16:19])
    small = (factor, *operands[19:])
    shape = (count, SLICE, width)
    return pl.pallas_call(
        functools.partial(finish_kernel, devices),
        in_specs=[hbm] * 2 + [vmem] * (len(operands) - 2),
        out_specs=[hbm] * len(large) + [vmem] * len(small),
        out_shape=[pltpu.HBM(array.shape, array.dtype) for array in large]
        + [jax.ShapeDtypeStruct(array.shape, array.dtype) for array in small],
        scratch_shapes=[
            pltpu.VMEM(shape, bf16),
            pltpu.VMEM(shape, bf16),
            pltpu.VMEM((3, *shape), bf16),
            pltpu.VMEM((3, width, width), f32),
            pltpu.SemaphoreType.DMA((2,)),
            pltpu.SemaphoreType.DMA((layer_part.shape[0],)),
            pltpu.SemaphoreType.DMA((3,)),
            pltpu.SemaphoreType.DMA((3,)),
        ],
        compiler_params=pltpu.CompilerParams(vmem_limit_bytes=FINISH_MIB * MIB),
        name="finish",
    )(*[in_hbm(array) for array in operands[:2]], *operands[2:])


def body(
    n_wide,
    n_narrow,
    tokens,
    labels,
    qkv_weight,
    out_weight,
    up_weight,
    down_weight,
    ffn_bias,
    layer_biases,
    norm_gains,
    pool_weight,
    pool_moment,
    class_weight,
    class_moment,
    ramp_biases,
    bias_moment,
    start_factor,
    error_buffer,
):
    width = tokens.shape[1]
    carried = (
        out_weight,
        up_weight,
        down_weight,
        ffn_bias,
        layer_biases,
        norm_gains,
        error_buffer,
        pool_weight,
        pool_moment,
        class_weight.T,
        class_moment.T,
        ramp_biases,
        bias_moment,
        start_factor.T,
    )
    context, *carried = attention(tokens, qkv_weight, layer_biases, carried)
    layer = carried[:6]
    error, pool_weight, pool_moment, class_weight, class_moment = carried[6:11]
    ramp_biases, bias_moment, start = carried[11:]
    context = context.reshape(-1, SEQ_LEN, width)
    sequences = tokens.reshape(-1, SEQ_LEN, width)
    layer_part, middle, sums, basis, factor, head, first_rows, grads = ramp(
        n_wide,
        n_narrow,
        labels,
        sequences,
        context,
        *layer,
        pool_weight,
        class_weight,
        ramp_biases,
        start,
        error,
    )
    (
        layer_out,
        error_new,
        pool_weight_new,
        pool_moment_new,
        factor_new,
        class_weight_new,
        class_moment_new,
        ramp_biases_new,
        bias_moment_new,
    ) = finish(
        n_wide * n_narrow,
        sequences,
        context,
        layer_part,
        middle,
        sums,
        *layer,
        basis,
        factor,
        first_rows,
        grads,
        head,
        error,
        pool_weight,
        pool_moment,
        class_weight,
        class_moment,
        ramp_biases,
        bias_moment,
    )
    return (
        layer_out.reshape(tokens.shape),
        pool_moment_new,
        pool_weight_new,
        class_moment_new.T,
        class_weight_new.T,
        bias_moment_new,
        ramp_biases_new,
        error_new,
        factor_new.T,
    )


def solution(mesh):
    rows = P(("wide", "narrow"), None)
    in_specs = (rows, P(("wide", "narrow"))) + (P(),) * 14 + (rows,)
    out_specs = (rows,) + (P(),) * 6 + (rows, P())
    return jax.shard_map(
        functools.partial(body, mesh.shape["wide"], mesh.shape["narrow"]),
        mesh=mesh,
        in_specs=in_specs,
        out_specs=out_specs,
        check_vma=False,
    )
```

```python
import functools

import jax
import jax.numpy as jnp
from jax import lax
from jax.experimental import pallas as pl
from jax.experimental.pallas import tpu as pltpu
from jax.sharding import PartitionSpec as P

HEAD_DIM = 64
SEQ_LEN = 1024
PAIR = 128
V_ROWS = 80
ROW_TILE = 16
LANES = 128
SLICE = 128
LATE_STEPS = 2
LOG2E = 1.4426950408889634
SAFE = 2.0**100
MOMENTUM = 0.9
RATE_POOL = 0.03
RATE_HEAD = 0.002
RATE_BIAS = 0.03
MIB = 1024 * 1024
ATTENTION_MIB = 24
RAMP_MIB = 16
FINISH_MIB = 16

f32 = jnp.float32
bf16 = jnp.bfloat16
NT = ((1,), (1,))
TN = ((0,), (0,))


def in_hbm(array):
    return pltpu.with_memory_space_constraint(array, pltpu.HBM)


def dot(left, right, contract=((1,), (0,))):
    return lax.dot_general(left, right, (contract, ((), ())), preferred_element_type=f32)


def norm_rows(values, gain, shift):
    centred = values - jnp.mean(values, -1, keepdims=True)
    variance = jnp.mean(centred * centred, -1, keepdims=True)
    return centred * lax.rsqrt(variance + 1e-12) * gain + shift


def gelu(values):
    half = 0.5 * values
    return half * lax.erf(values * 0.7071067811865476) + half


def head_sums(scores, values_aug, shifted):
    if shifted:
        scores = scores - jnp.max(scores, 0, keepdims=True)
    return dot(values_aug, jnp.exp2(scores * LOG2E).astype(bf16))


def put_context(context_t, head, sums):
    scale = 1.0 / sums[HEAD_DIM : HEAD_DIM + 8]
    groups = [sums[g : g + 8] * scale for g in range(0, HEAD_DIM, 8)]
    rows = pl.ds(pl.multiple_of(head * HEAD_DIM, HEAD_DIM), HEAD_DIM)
    context_t[rows, :] = jnp.concatenate(groups, 0).astype(bf16)


def attention_kernel(carried, tokens, qkv_weight, layer_biases, *refs):
    sources, (sequences, context), targets = (
        refs[:carried],
        refs[carried : carried + 2],
        refs[carried + 2 :][:carried],
    )
    (
        key_weight,
        query_weight_t,
        value_weight_t,
        query_bias,
        value_bias,
        keys,
        queries_t,
        values_t,
        context_t,
        low,
        high,
        weight_sem,
        token_sem,
        carry_sem,
    ) = refs[2 * carried + 2 :]
    step = pl.program_id(0)
    steps = pl.num_programs(0)
    length, width = queries_t.shape[2], tokens.shape[1]
    heads = width // HEAD_DIM

    def weight_copy(index, into):
        columns = qkv_weight.at[:, pl.ds(index * width, width)]
        return pltpu.make_async_copy(columns, into, weight_sem.at[index])

    def rows_of(index):
        return pl.ds(pl.multiple_of(index * length, length), length)

    def token_copy(index):
        rows = rows_of(index)
        return pltpu.make_async_copy(tokens.at[rows], sequences.at[rows], token_sem.at[index])

    carries = [
        pltpu.make_async_copy(source, target, carry_sem.at[index])
        for index, (source, target) in enumerate(zip(sources, targets, strict=True))
    ]
    query_weight = context.at[pl.ds(0, width)]
    value_weight = context.at[pl.ds(width, width)]
    query_copy = weight_copy(0, query_weight)
    key_copy = weight_copy(1, key_weight)
    value_copy = weight_copy(2, value_weight)

    @pl.when(step == 0)
    def _():
        query_copy.start()
        value_copy.start()
        token_copy(0).start()
        key_copy.start()
        columns = jnp.concatenate([layer_biases[...], jnp.zeros((2, width), f32)], 0).T
        query_bias[...] = jnp.broadcast_to(columns[:, 0:1], (width, LANES))
        value_bias[...] = jnp.broadcast_to(columns[:, 1:2], (width, LANES))
        queries_t[...] = jnp.zeros_like(queries_t)
        values_t[:, HEAD_DIM:, :] = jnp.ones((heads, V_ROWS - HEAD_DIM, length), bf16)
        query_copy.wait()
        query_weight_t[...] = query_weight[...].T
        value_copy.wait()
        value_weight_t[...] = value_weight[...].T
        key_copy.wait()
        @pl.loop(1, steps)
        def _(index):
            token_copy(index).start()

        for copy in carries:
            copy.start()

    token_copy(step).wait()

    def wide_bias(bias):
        return jnp.concatenate([bias[...]] * (length // LANES), 1)

    sequence = sequences[rows_of(step), :]
    key_rows = dot(sequence, key_weight[...]).astype(bf16)
    for pair in range(heads // 2):
        keys[pair] = key_rows[:, pair * PAIR : (pair + 1) * PAIR]

    query_cols = ((dot(query_weight_t[...], sequence, NT) + wide_bias(query_bias)) * 0.125).astype(bf16)
    value_cols = (dot(value_weight_t[...], sequence, NT) + wide_bias(value_bias)).astype(bf16)
    for head in range(heads):
        own = slice(head * HEAD_DIM, (head + 1) * HEAD_DIM)
        half = (head % 2) * HEAD_DIM
        queries_t[head, half : half + HEAD_DIM, :] = query_cols[own]
        values_t[head, :HEAD_DIM, :] = value_cols[own]

    low[...] = jnp.ones_like(low)
    high[...] = jnp.ones_like(high)

    for head in range(heads):
        sums = head_sums(dot(keys[head // 2], queries_t[head]), values_t[head], False)
        denominators = sums[HEAD_DIM : HEAD_DIM + 8]
        low[...] = jnp.minimum(low[...], denominators)
        high[...] = jnp.maximum(high[...], denominators)
        put_context(context_t, head, sums)
        if head % 2:
            lanes = slice((head // 2) * PAIR, (head // 2 + 1) * PAIR)
            context[rows_of(step), lanes] = context_t[lanes, :].T

    in_range = (jnp.min(low[...]) > 1.0 / SAFE) & (jnp.max(high[...]) < SAFE)

    @pl.when(jnp.logical_not(in_range))
    def _():
        @pl.loop(0, heads)
        def _(head):
            sums = head_sums(dot(keys[head // 2], queries_t[head]), values_t[head], True)
            put_context(context_t, head, sums)

        context[rows_of(step), :] = context_t[...].T

    @pl.when(step == steps - 1)
    def _():
        for copy in carries:
            copy.wait()


def attention(tokens, qkv_weight, layer_biases, carried):
    rows, width = tokens.shape
    count = rows // SEQ_LEN
    heads = width // HEAD_DIM
    hbm = pl.BlockSpec(memory_space=pltpu.HBM)
    square = pltpu.VMEM((width, width), bf16)
    return pl.pallas_call(
        functools.partial(attention_kernel, len(carried)),
        grid=(count,),
        in_specs=[hbm, hbm, pl.BlockSpec((6, width), lambda i: (0, 0))] + [hbm] * len(carried),
        out_specs=[pl.BlockSpec(memory_space=pltpu.VMEM)] * (2 + len(carried)),
        out_shape=[pltpu.VMEM(array.shape, array.dtype) for array in (tokens, tokens, *carried)],
        scratch_shapes=[square] * 3
        + [
            pltpu.VMEM((width, LANES), f32),
            pltpu.VMEM((width, LANES), f32),
            pltpu.VMEM((heads // 2, SEQ_LEN, PAIR), bf16),
            pltpu.VMEM((heads, PAIR, SEQ_LEN), bf16),
            pltpu.VMEM((heads, V_ROWS, SEQ_LEN), bf16),
            pltpu.VMEM((width, SEQ_LEN), bf16),
            pltpu.VMEM((8, SEQ_LEN), f32),
            pltpu.VMEM((8, SEQ_LEN), f32),
            pltpu.SemaphoreType.DMA((3,)),
            pltpu.SemaphoreType.DMA((count,)),
            pltpu.SemaphoreType.DMA((len(carried),)),
        ],
        compiler_params=pltpu.CompilerParams(vmem_limit_bytes=ATTENTION_MIB * MIB),
        name="attention",
    )(in_hbm(tokens), in_hbm(qkv_weight), layer_biases, *[in_hbm(array) for array in carried])


def to_middle(block, tokens, context, out_weight, biases, gains):
    def rows(array):
        return array[:, block * SLICE : (block + 1) * SLICE].reshape(-1, array.shape[2])

    attended = dot(rows(context), out_weight[...]) + biases[2:3]
    return norm_rows(rows(tokens).astype(f32) + attended, gains[0:1], biases[3:4]).astype(bf16)


def to_sums(middle, up_weight, down_weight, ffn_bias, biases):
    hidden = gelu(dot(middle, up_weight[...]) + ffn_bias[...].reshape(1, -1)).astype(bf16)
    return middle.astype(f32) + dot(hidden, down_weight[...]) + biases[4:5]


def to_layer(sums, biases, gains):
    return norm_rows(sums, gains[1:2], biases[5:6]).astype(bf16)


def orthonormal_rows(factor):
    index = lax.broadcasted_iota(jnp.int32, factor.shape, 0)
    for row in range(factor.shape[0]):
        vector = factor[row : row + 1]
        vector = vector * lax.rsqrt(jnp.sum(vector * vector, -1, keepdims=True) + 1e-06)
        along = jnp.sum(factor * vector, -1, keepdims=True)
        factor = jnp.where(index > row, factor - along * vector, factor)
        factor = jnp.where(index == row, vector, factor)
    return factor


def split(values):
    first = values.astype(bf16).astype(f32)
    second = (values - first).astype(bf16).astype(f32)
    return first, second, values - first - second


def stacked(values):
    return jnp.concatenate(split(values), 0).astype(bf16)


def folded(values):
    rows = values.shape[0] // 3
    return values[:rows] + values[rows : 2 * rows] + values[2 * rows :]


class Exchange:
    def __init__(self, slots, send_sem, recv_sem, me, count, device_of):
        self.slots, self.send_sem, self.recv_sem = slots, send_sem, recv_sem
        self.me, self.count, self.device_of = me, count, device_of

    def copy(self, step, slot, device):
        return pltpu.make_async_remote_copy(
            src_ref=self.slots.at[slot],
            dst_ref=self.slots.at[slot],
            send_sem=self.send_sem.at[step],
            recv_sem=self.recv_sem.at[slot],
            device_id=self.device_of(device),
            device_id_type=pl.DeviceIdType.MESH,
        )

    def greet(self, barrier):
        for step in range(1, self.count):
            pl.semaphore_signal(
                barrier,
                inc=1,
                device_id=self.device_of(lax.rem(self.me + step, self.count)),
                device_id_type=pl.DeviceIdType.MESH,
            )

    def start(self, value):
        self.slots[self.me] = value
        for step in range(1, self.count):
            self.copy(step, self.me, lax.rem(self.me + step, self.count)).start()

    def total(self):
        for step in range(1, self.count):
            source = lax.rem(self.me + self.count - step, self.count)
            self.copy(step, source, source).wait_recv()
            self.copy(step, self.me, lax.rem(self.me + step, self.count)).wait_send()
        total = self.slots[0]
        for other in range(1, self.count):
            total = total + self.slots[other]
        return total


def head_gradients(labels, first_rows, pool_weight, class_weight_t, ramp_biases):
    classes, width = class_weight_t.shape
    class_low = jnp.concatenate(
        [class_weight_t[...], jnp.zeros((LANES - classes, width), f32)], 0
    ).astype(bf16)
    biases = jnp.concatenate([ramp_biases[...], jnp.zeros((LANES - classes,), f32)], 0)
    biases = biases.reshape(1, -1)
    pre = dot(first_rows, pool_weight[...].astype(bf16)) + biases[:, :width]
    pooled = jnp.tanh(pre)
    pooled_low = pooled.astype(bf16)
    logits = dot(pooled_low, class_low, NT) + biases[:, width:]
    lane = lax.broadcasted_iota(jnp.int32, logits.shape, 1)
    row = lax.broadcasted_iota(jnp.int32, logits.shape, 0)
    target = jnp.full(logits.shape, -1, jnp.int32)
    for index in range(first_rows.shape[0] // ROW_TILE):
        target = jnp.where(row == index * ROW_TILE, labels[index], target)
    logits = jnp.where(lane < classes, logits, -jnp.inf)
    powers = jnp.exp(logits - jnp.max(logits, -1, keepdims=True))
    softened = powers / jnp.sum(powers, -1, keepdims=True)
    grad_logits = softened - (lane == target).astype(f32)
    grad_logits = jnp.where(row % ROW_TILE == 0, grad_logits, 0.0).astype(bf16)
    grad_class = dot(grad_logits, pooled_low, TN)[:8]
    grad_pooled = dot(grad_logits, class_low)
    grad_pre = (grad_pooled * (1.0 - pooled * pooled)).astype(bf16)
    bias_sum = jnp.sum(grad_pre.astype(f32), 0, keepdims=True)
    logit_sum = jnp.sum(grad_logits.astype(f32), 0, keepdims=True)
    logit_sum = jnp.concatenate([logit_sum, jnp.zeros((1, width - LANES), f32)], 1)
    index = lax.broadcasted_iota(jnp.int32, grad_class.shape, 0)
    head = jnp.where(index == classes, bias_sum, grad_class)
    return grad_pre, jnp.where(index == classes + 1, logit_sum, head)


def ramp_kernel(
    n_wide,
    n_narrow,
    labels,
    tokens,
    context,
    out_weight,
    up_weight,
    down_weight,
    ffn_bias,
    layer_biases,
    norm_gains,
    pool_weight,
    class_weight_t,
    ramp_biases,
    start_t,
    error,
    layer_part,
    middle_out,
    sums_out,
    basis_out,
    factor_out,
    head_out,
    rows_out,
    grads_out,
    narrow_one,
    wide_one,
    narrow_head,
    wide_head,
    narrow_two,
    wide_two,
    send_sem,
    recv_sem,
):
    wide, narrow = lax.axis_index("wide"), lax.axis_index("narrow")
    count, _, width = tokens.shape
    rank = start_t.shape[0]

    def group(index, slots, by_narrow):
        semaphores = send_sem.at[index], recv_sem.at[index]
        if by_narrow:
            return Exchange(slots, *semaphores, narrow, n_narrow, lambda i: (wide, i))
        return Exchange(slots, *semaphores, wide, n_wide, lambda i: (i, narrow))

    sum_one_narrow = group(0, narrow_one, True)
    sum_one_wide = group(1, wide_one, False)
    sum_head_narrow = group(2, narrow_head, True)
    sum_head_wide = group(3, wide_head, False)
    sum_two_narrow = group(4, narrow_two, True)
    sum_two_wide = group(5, wide_two, False)
    barrier = pltpu.get_barrier_semaphore()
    sum_one_narrow.greet(barrier)
    sum_one_wide.greet(barrier)

    steps = layer_part.shape[0] + 1
    middle = {}
    sums = {}

    def middle_of(block):
        middle[block] = to_middle(
            block, tokens, context, out_weight, layer_biases, norm_gains
        )

    def layer_of(block):
        rows = to_layer(sums.pop(block), layer_biases, norm_gains)
        layer_part[block] = rows.reshape(count, SLICE, width)

    def sums_of(block):
        sums[block] = to_sums(
            middle.pop(block), up_weight, down_weight, ffn_bias, layer_biases
        )

    middle_of(0)
    error_high = error[...].astype(bf16)
    error_low = (error[...] - error_high.astype(f32)).astype(bf16)
    start = stacked(start_t[...])
    factor = folded(dot(start, error_high, NT) + dot(start, error_low, NT))
    middle_of(1)
    sums_of(0)

    first = [sums[0][index * SLICE : index * SLICE + ROW_TILE] for index in range(count)]
    first_rows = to_layer(jnp.concatenate(first, 0), layer_biases, norm_gains)
    grads, head = head_gradients(labels, first_rows, pool_weight, class_weight_t, ramp_biases)
    factor = factor + folded(dot(stacked(folded(dot(start, grads, NT))), first_rows))
    rows_out[...] = first_rows
    grads_out[...] = grads
    middle_of(2)
    pl.semaphore_wait(barrier, n_narrow + n_wide - 2)
    sum_one_narrow.start(factor)

    sums_of(1)
    layer_of(0)
    sum_one_wide.start(sum_one_narrow.total())
    sum_head_narrow.start(head)

    middle_of(3)
    sums_of(2)
    layer_of(1)
    middle_of(4)
    sum_head_wide.start(sum_head_narrow.total())
    basis = orthonormal_rows(sum_one_wide.total())
    basis_out[...] = basis
    basis = stacked(basis)
    factor = folded(dot(basis, error_high) + dot(basis, error_low))
    factor = factor + folded(dot(stacked(folded(dot(basis, rows_out[...], NT))), grads_out[...]))
    sums_of(3)
    layer_of(2)
    sum_two_narrow.start(factor)

    middle_of(5)
    sums_of(4)
    layer_of(3)
    sum_two_wide.start(sum_two_narrow.total())

    for block in range(5, steps):
        middle_of(block + 1)
        sums_of(block)
        layer_of(block - 1)
    middle_out[...] = middle[steps]
    sums_out[...] = sums[steps - 1]
    head_out[...] = sum_head_wide.total()
    factor_out[...] = sum_two_wide.total()


def ramp(n_wide, n_narrow, labels, tokens, context, *operands):
    start_t = operands[9]
    rank, width = start_t.shape
    count, length, _ = tokens.shape
    most = max(n_wide, n_narrow)
    vmem = pl.BlockSpec(memory_space=pltpu.VMEM)
    steps = length // SLICE - LATE_STEPS
    first = ROW_TILE * count
    outs = [
        pltpu.VMEM((steps - 1, count, SLICE, width), bf16),
        pltpu.VMEM((count * SLICE, width), bf16),
        pltpu.VMEM((count * SLICE, width), f32),
        pltpu.VMEM((rank, width), f32),
        pltpu.VMEM((rank, width), f32),
        pltpu.VMEM((8, width), f32),
        pltpu.VMEM((first, width), bf16),
        pltpu.VMEM((first, width), bf16),
    ]
    return pl.pallas_call(
        functools.partial(ramp_kernel, n_wide, n_narrow),
        in_specs=[pl.BlockSpec(memory_space=pltpu.SMEM)] + [vmem] * (2 + len(operands)),
        out_specs=[vmem] * len(outs),
        out_shape=outs,
        scratch_shapes=[
            pltpu.VMEM((n_narrow, rank, width), f32),
            pltpu.VMEM((n_wide, rank, width), f32),
            pltpu.VMEM((n_narrow, 8, width), f32),
            pltpu.VMEM((n_wide, 8, width), f32),
            pltpu.VMEM((n_narrow, rank, width), f32),
            pltpu.VMEM((n_wide, rank, width), f32),
            pltpu.SemaphoreType.DMA((6, most)),
            pltpu.SemaphoreType.DMA((6, most)),
        ],
        compiler_params=pltpu.CompilerParams(
            vmem_limit_bytes=RAMP_MIB * MIB, collective_id=0, has_side_effects=True
        ),
        name="ramp",
    )(labels, tokens, context, *operands)


def finish_kernel(
    devices,
    tokens,
    context,
    layer_part,
    middle,
    sums,
    out_weight,
    up_weight,
    down_weight,
    ffn_bias,
    layer_biases,
    norm_gains,
    basis,
    factor,
    rows,
    grads,
    head,
    error,
    pool_weight,
    pool_moment,
    class_weight_t,
    class_moment_t,
    ramp_biases,
    bias_moment,
    layer_out,
    error_new,
    pool_weight_new,
    pool_moment_new,
    factor_new,
    class_weight_new,
    class_moment_new,
    ramp_biases_new,
    bias_moment_new,
    done,
    held,
    load_sem,
    part_sem,
    done_sem,
    store_sem,
):
    ready, count, _, width = layer_part.shape
    classes = class_weight_t.shape[0]

    def block_of(array, index):
        return array.at[:, pl.ds(index * SLICE, SLICE)]

    parts = [
        pltpu.make_async_copy(layer_part.at[index], block_of(layer_out, index), part_sem.at[index])
        for index in range(ready)
    ]
    stores = [
        pltpu.make_async_copy(held.at[index], into, store_sem.at[index])
        for index, into in enumerate([error_new, pool_weight_new, pool_moment_new])
    ]

    def done_copy(index):
        into = block_of(layer_out, ready + index)
        return pltpu.make_async_copy(done.at[index], into, done_sem.at[index])

    def finish_block(index, values):
        done[index] = to_layer(values, layer_biases, norm_gains).reshape(count, SLICE, width)
        done_copy(index).start()

    load = pltpu.make_async_copy(pool_moment, held.at[2], load_sem)
    load.start()
    for copy in parts:
        copy.start()
    finish_block(0, sums[...])
    factor_new[...] = factor[...]

    first_block = ready + 1
    middle = {first_block: middle[...]}
    for block in range(first_block, first_block + LATE_STEPS):
        if block + 1 < first_block + LATE_STEPS:
            middle[block + 1] = to_middle(
                block + 1, tokens, context, out_weight, layer_biases, norm_gains
            )
        next_sums = to_sums(middle[block], up_weight, down_weight, ffn_bias, layer_biases)
        finish_block(block - ready, next_sums)

    moment = MOMENTUM * class_moment_t[...] + head[:classes]
    class_moment_new[...] = moment
    class_weight_new[...] = class_weight_t[...] - RATE_HEAD * moment
    total = jnp.concatenate(
        [head[classes : classes + 1], head[classes + 1 : classes + 2, :classes]], 1
    )
    moment = MOMENTUM * bias_moment[...] + total.reshape(-1)
    bias_moment_new[...] = moment
    ramp_biases_new[...] = ramp_biases[...] - RATE_BIAS * moment

    high, mid, low = split(basis[...])
    left = jnp.concatenate([high, high, mid, mid, high, low], 0).astype(bf16)
    high, mid, low = split(factor[...])
    right = jnp.concatenate([high, mid, high, mid, low, high], 0).astype(bf16)
    approx = dot(left, right, TN)
    combined = dot(rows[...], grads[...], TN) + error[...]
    held[0] = combined - approx * (1.0 / devices)
    load.wait()
    moment = MOMENTUM * held[2] + approx
    held[2] = moment
    held[1] = pool_weight[...] - RATE_POOL * moment
    for copy in stores:
        copy.start()
    for copy in parts + stores:
        copy.wait()
    for index in range(1 + LATE_STEPS):
        done_copy(index).wait()


def finish(devices, *operands):
    vmem = pl.BlockSpec(memory_space=pltpu.VMEM)
    hbm = pl.BlockSpec(memory_space=pltpu.HBM)
    tokens, layer_part, factor = operands[0], operands[2], operands[12]
    ready, *shape = layer_part.shape
    width = shape[-1]
    large = (tokens, *operands[16:19])
    small = (factor, *operands[19:])
    return pl.pallas_call(
        functools.partial(finish_kernel, devices),
        in_specs=[vmem] * 18 + [hbm] + [vmem] * (len(operands) - 19),
        out_specs=[hbm] * len(large) + [vmem] * len(small),
        out_shape=[pltpu.HBM(array.shape, array.dtype) for array in large]
        + [jax.ShapeDtypeStruct(array.shape, array.dtype) for array in small],
        scratch_shapes=[
            pltpu.VMEM((1 + LATE_STEPS, *shape), bf16),
            pltpu.VMEM((3, width, width), f32),
            pltpu.SemaphoreType.DMA,
            pltpu.SemaphoreType.DMA((ready,)),
            pltpu.SemaphoreType.DMA((1 + LATE_STEPS,)),
            pltpu.SemaphoreType.DMA((3,)),
        ],
        compiler_params=pltpu.CompilerParams(vmem_limit_bytes=FINISH_MIB * MIB),
        name="finish",
    )(*operands[:18], in_hbm(operands[18]), *operands[19:])


def body(
    n_wide,
    n_narrow,
    tokens,
    labels,
    qkv_weight,
    out_weight,
    up_weight,
    down_weight,
    ffn_bias,
    layer_biases,
    norm_gains,
    pool_weight,
    pool_moment,
    class_weight,
    class_moment,
    ramp_biases,
    bias_moment,
    start_factor,
    error_buffer,
):
    width = tokens.shape[1]
    carried = (
        out_weight,
        up_weight,
        down_weight,
        ffn_bias,
        layer_biases,
        norm_gains,
        error_buffer,
        pool_weight,
        class_weight.T,
        class_moment.T,
        ramp_biases,
        bias_moment,
        start_factor.T,
    )
    sequences, context, *carried = attention(tokens, qkv_weight, layer_biases, carried)
    layer = carried[:6]
    error, pool_weight, class_weight, class_moment = carried[6:10]
    ramp_biases, bias_moment, start = carried[10:]
    context = context.reshape(-1, SEQ_LEN, width)
    sequences = sequences.reshape(-1, SEQ_LEN, width)
    layer_part, middle, sums, basis, factor, head, first_rows, grads = ramp(
        n_wide,
        n_narrow,
        labels,
        sequences,
        context,
        *layer,
        pool_weight,
        class_weight,
        ramp_biases,
        start,
        error,
    )
    (
        layer_out,
        error_new,
        pool_weight_new,
        pool_moment_new,
        factor_new,
        class_weight_new,
        class_moment_new,
        ramp_biases_new,
        bias_moment_new,
    ) = finish(
        n_wide * n_narrow,
        sequences,
        context,
        layer_part,
        middle,
        sums,
        *layer,
        basis,
        factor,
        first_rows,
        grads,
        head,
        error,
        pool_weight,
        pool_moment,
        class_weight,
        class_moment,
        ramp_biases,
        bias_moment,
    )
    return (
        layer_out.reshape(tokens.shape),
        pool_moment_new,
        pool_weight_new,
        class_moment_new.T,
        class_weight_new.T,
        bias_moment_new,
        ramp_biases_new,
        error_new,
        factor_new.T,
    )


def solution(mesh):
    rows = P(("wide", "narrow"), None)
    in_specs = (rows, P(("wide", "narrow"))) + (P(),) * 14 + (rows,)
    out_specs = (rows,) + (P(),) * 6 + (rows, P())
    return jax.shard_map(
        functools.partial(body, mesh.shape["wide"], mesh.shape["narrow"]),
        mesh=mesh,
        in_specs=in_specs,
        out_specs=out_specs,
        check_vma=False,
    )
```

```python
import functools

import jax
import jax.numpy as jnp
from jax import lax
from jax.experimental import pallas as pl
from jax.experimental.pallas import tpu as pltpu
from jax.sharding import PartitionSpec as P

HEAD_DIM = 64
SEQ_LEN = 1024
PAIR = 128
V_ROWS = 80
ROW_TILE = 16
LANES = 128
SLICE = 128
LATE_STEPS = 2
HEAD_GROUP = 4
LOG2E = 1.4426950408889634
SAFE = 2.0**100
MOMENTUM = 0.9
RATE_POOL = 0.03
RATE_HEAD = 0.002
RATE_BIAS = 0.03
MIB = 1024 * 1024
ATTENTION_MIB = 23
RAMP_MIB = 12
FINISH_MIB = 14

f32 = jnp.float32
bf16 = jnp.bfloat16
NT = ((1,), (1,))
TN = ((0,), (0,))


def in_hbm(array):
    return pltpu.with_memory_space_constraint(array, pltpu.HBM)


def dot(left, right, contract=((1,), (0,))):
    return lax.dot_general(left, right, (contract, ((), ())), preferred_element_type=f32)


def norm_rows(values, gain, shift):
    centred = values - jnp.mean(values, -1, keepdims=True)
    variance = jnp.mean(centred * centred, -1, keepdims=True)
    return centred * lax.rsqrt(variance + 1e-12) * gain + shift


def gelu(values):
    half = 0.5 * values
    return half * lax.erf(values * 0.7071067811865476) + half


def head_sums(scores, values_aug, shifted):
    if shifted:
        scores = scores - jnp.max(scores, 0, keepdims=True)
    return dot(values_aug, jnp.exp2(scores * LOG2E).astype(bf16))


def put_context(context_t, head, sums):
    scale = 1.0 / sums[HEAD_DIM : HEAD_DIM + 8]
    groups = [sums[g : g + 8] * scale for g in range(0, HEAD_DIM, 8)]
    rows = pl.ds(pl.multiple_of(head * HEAD_DIM, HEAD_DIM), HEAD_DIM)
    context_t[rows, :] = jnp.concatenate(groups, 0).astype(bf16)


def attention_kernel(carried, tokens, qkv_weight, layer_biases, *refs):
    sources, (sequences, context), targets = (
        refs[:carried],
        refs[carried : carried + 2],
        refs[carried + 2 :][:carried],
    )
    (
        key_weight,
        query_weight_t,
        value_weight_t,
        query_bias,
        value_bias,
        keys,
        queries_t,
        values_t,
        context_t,
        low,
        high,
        weight_sem,
        token_sem,
        carry_sem,
    ) = refs[2 * carried + 2 :]
    step = pl.program_id(0)
    steps = pl.num_programs(0)
    length, width = queries_t.shape[2], tokens.shape[1]
    heads = width // HEAD_DIM

    def weight_copy(index, into):
        columns = qkv_weight.at[:, pl.ds(index * width, width)]
        return pltpu.make_async_copy(columns, into, weight_sem.at[index])

    def rows_of(index):
        return pl.ds(pl.multiple_of(index * length, length), length)

    def token_copy(index):
        rows = rows_of(index)
        return pltpu.make_async_copy(tokens.at[rows], sequences.at[rows], token_sem.at[index])

    carries = [
        pltpu.make_async_copy(source, target, carry_sem.at[index])
        for index, (source, target) in enumerate(zip(sources, targets, strict=True))
    ]
    query_weight = context.at[pl.ds(0, width)]
    value_weight = context.at[pl.ds(width, width)]
    query_copy = weight_copy(0, query_weight)
    key_copy = weight_copy(1, key_weight)
    value_copy = weight_copy(2, value_weight)

    @pl.when(step == 0)
    def _():
        query_copy.start()
        value_copy.start()
        token_copy(0).start()
        key_copy.start()
        columns = jnp.concatenate([layer_biases[...], jnp.zeros((2, width), f32)], 0).T
        query_bias[...] = jnp.broadcast_to(columns[:, 0:1], (width, LANES))
        value_bias[...] = jnp.broadcast_to(columns[:, 1:2], (width, LANES))
        queries_t[...] = jnp.zeros_like(queries_t)
        values_t[:, HEAD_DIM:, :] = jnp.ones((heads, V_ROWS - HEAD_DIM, length), bf16)
        query_copy.wait()
        query_weight_t[...] = query_weight[...].T
        value_copy.wait()
        value_weight_t[...] = value_weight[...].T
        key_copy.wait()
        @pl.loop(1, steps)
        def _(index):
            token_copy(index).start()

        for copy in carries:
            copy.start()

    token_copy(step).wait()

    def wide_bias(bias):
        return jnp.concatenate([bias[...]] * (length // LANES), 1)

    sequence = sequences[rows_of(step), :]
    key_rows = dot(sequence, key_weight[...]).astype(bf16)
    for pair in range(heads // 2):
        keys[pair] = key_rows[:, pair * PAIR : (pair + 1) * PAIR]

    query_cols = ((dot(query_weight_t[...], sequence, NT) + wide_bias(query_bias)) * 0.125).astype(bf16)
    value_cols = (dot(value_weight_t[...], sequence, NT) + wide_bias(value_bias)).astype(bf16)
    for head in range(heads):
        own = slice(head * HEAD_DIM, (head + 1) * HEAD_DIM)
        half = (head % 2) * HEAD_DIM
        queries_t[head, half : half + HEAD_DIM, :] = query_cols[own]
        values_t[head, :HEAD_DIM, :] = value_cols[own]

    low[...] = jnp.ones_like(low)
    high[...] = jnp.ones_like(high)

    @pl.loop(0, heads // HEAD_GROUP)
    def _(group):
        for offset in range(HEAD_GROUP):
            head = group * HEAD_GROUP + offset
            sums = head_sums(dot(keys[head // 2], queries_t[head]), values_t[head], False)
            denominators = sums[HEAD_DIM : HEAD_DIM + 8]
            low[...] = jnp.minimum(low[...], denominators)
            high[...] = jnp.maximum(high[...], denominators)
            put_context(context_t, head, sums)
            if offset % 2:
                lanes = pl.ds(pl.multiple_of((head // 2) * PAIR, PAIR), PAIR)
                context[rows_of(step), lanes] = context_t[lanes, :].T

    in_range = (jnp.min(low[...]) > 1.0 / SAFE) & (jnp.max(high[...]) < SAFE)

    @pl.when(jnp.logical_not(in_range))
    def _():
        @pl.loop(0, heads)
        def _(head):
            sums = head_sums(dot(keys[head // 2], queries_t[head]), values_t[head], True)
            put_context(context_t, head, sums)

        context[rows_of(step), :] = context_t[...].T

    @pl.when(step == steps - 1)
    def _():
        for copy in carries:
            copy.wait()


def attention(tokens, qkv_weight, layer_biases, carried):
    rows, width = tokens.shape
    count = rows // SEQ_LEN
    heads = width // HEAD_DIM
    hbm = pl.BlockSpec(memory_space=pltpu.HBM)
    square = pltpu.VMEM((width, width), bf16)
    return pl.pallas_call(
        functools.partial(attention_kernel, len(carried)),
        grid=(count,),
        in_specs=[hbm, hbm, pl.BlockSpec((6, width), lambda i: (0, 0))] + [hbm] * len(carried),
        out_specs=[pl.BlockSpec(memory_space=pltpu.VMEM)] * (2 + len(carried)),
        out_shape=[pltpu.VMEM(array.shape, array.dtype) for array in (tokens, tokens, *carried)],
        scratch_shapes=[square] * 3
        + [
            pltpu.VMEM((width, LANES), f32),
            pltpu.VMEM((width, LANES), f32),
            pltpu.VMEM((heads // 2, SEQ_LEN, PAIR), bf16),
            pltpu.VMEM((heads, PAIR, SEQ_LEN), bf16),
            pltpu.VMEM((heads, V_ROWS, SEQ_LEN), bf16),
            pltpu.VMEM((width, SEQ_LEN), bf16),
            pltpu.VMEM((8, SEQ_LEN), f32),
            pltpu.VMEM((8, SEQ_LEN), f32),
            pltpu.SemaphoreType.DMA((3,)),
            pltpu.SemaphoreType.DMA((count,)),
            pltpu.SemaphoreType.DMA((len(carried),)),
        ],
        compiler_params=pltpu.CompilerParams(vmem_limit_bytes=ATTENTION_MIB * MIB),
        name="attention",
    )(in_hbm(tokens), in_hbm(qkv_weight), layer_biases, *[in_hbm(array) for array in carried])


def to_middle(block, tokens, context, out_weight, biases, gains):
    where = pl.ds(pl.multiple_of(block * SLICE, SLICE), SLICE)

    def rows(array):
        return array[:, where, :].reshape(-1, array.shape[2])

    attended = dot(rows(context), out_weight[...]) + biases[2:3]
    return norm_rows(rows(tokens).astype(f32) + attended, gains[0:1], biases[3:4]).astype(bf16)


def to_sums(middle, up_weight, down_weight, ffn_bias, biases):
    hidden = gelu(dot(middle, up_weight[...]) + ffn_bias[...].reshape(1, -1)).astype(bf16)
    return middle.astype(f32) + dot(hidden, down_weight[...]) + biases[4:5]


def to_layer(sums, biases, gains):
    return norm_rows(sums, gains[1:2], biases[5:6]).astype(bf16)


def orthonormal_rows(factor):
    index = lax.broadcasted_iota(jnp.int32, factor.shape, 0)
    for row in range(factor.shape[0]):
        vector = factor[row : row + 1]
        vector = vector * lax.rsqrt(jnp.sum(vector * vector, -1, keepdims=True) + 1e-06)
        along = jnp.sum(factor * vector, -1, keepdims=True)
        factor = jnp.where(index > row, factor - along * vector, factor)
        factor = jnp.where(index == row, vector, factor)
    return factor


def split(values):
    first = values.astype(bf16).astype(f32)
    second = (values - first).astype(bf16).astype(f32)
    return first, second, values - first - second


def stacked(values):
    return jnp.concatenate(split(values), 0).astype(bf16)


def folded(values):
    rows = values.shape[0] // 3
    return values[:rows] + values[rows : 2 * rows] + values[2 * rows :]


class Exchange:
    def __init__(self, slots, send_sem, recv_sem, me, count, device_of):
        self.slots, self.send_sem, self.recv_sem = slots, send_sem, recv_sem
        self.me, self.count, self.device_of = me, count, device_of

    def copy(self, step, slot, device):
        return pltpu.make_async_remote_copy(
            src_ref=self.slots.at[slot],
            dst_ref=self.slots.at[slot],
            send_sem=self.send_sem.at[step],
            recv_sem=self.recv_sem.at[slot],
            device_id=self.device_of(device),
            device_id_type=pl.DeviceIdType.MESH,
        )

    def greet(self, barrier):
        for step in range(1, self.count):
            pl.semaphore_signal(
                barrier,
                inc=1,
                device_id=self.device_of(lax.rem(self.me + step, self.count)),
                device_id_type=pl.DeviceIdType.MESH,
            )

    def start(self, value):
        self.slots[self.me] = value
        for step in range(1, self.count):
            self.copy(step, self.me, lax.rem(self.me + step, self.count)).start()

    def total(self):
        for step in range(1, self.count):
            source = lax.rem(self.me + self.count - step, self.count)
            self.copy(step, source, source).wait_recv()
            self.copy(step, self.me, lax.rem(self.me + step, self.count)).wait_send()
        total = self.slots[0]
        for other in range(1, self.count):
            total = total + self.slots[other]
        return total


def head_gradients(labels, first_rows, pool_weight, class_weight_t, ramp_biases):
    classes, width = class_weight_t.shape
    class_low = jnp.concatenate(
        [class_weight_t[...], jnp.zeros((LANES - classes, width), f32)], 0
    ).astype(bf16)
    biases = jnp.concatenate([ramp_biases[...], jnp.zeros((LANES - classes,), f32)], 0)
    biases = biases.reshape(1, -1)
    pre = dot(first_rows, pool_weight[...].astype(bf16)) + biases[:, :width]
    pooled = jnp.tanh(pre)
    pooled_low = pooled.astype(bf16)
    logits = dot(pooled_low, class_low, NT) + biases[:, width:]
    lane = lax.broadcasted_iota(jnp.int32, logits.shape, 1)
    row = lax.broadcasted_iota(jnp.int32, logits.shape, 0)
    target = jnp.full(logits.shape, -1, jnp.int32)
    for index in range(first_rows.shape[0] // ROW_TILE):
        target = jnp.where(row == index * ROW_TILE, labels[index], target)
    logits = jnp.where(lane < classes, logits, -jnp.inf)
    powers = jnp.exp(logits - jnp.max(logits, -1, keepdims=True))
    softened = powers / jnp.sum(powers, -1, keepdims=True)
    grad_logits = softened - (lane == target).astype(f32)
    grad_logits = jnp.where(row % ROW_TILE == 0, grad_logits, 0.0).astype(bf16)
    grad_class = dot(grad_logits, pooled_low, TN)[:8]
    grad_pooled = dot(grad_logits, class_low)
    grad_pre = (grad_pooled * (1.0 - pooled * pooled)).astype(bf16)
    bias_sum = jnp.sum(grad_pre.astype(f32), 0, keepdims=True)
    logit_sum = jnp.sum(grad_logits.astype(f32), 0, keepdims=True)
    logit_sum = jnp.concatenate([logit_sum, jnp.zeros((1, width - LANES), f32)], 1)
    index = lax.broadcasted_iota(jnp.int32, grad_class.shape, 0)
    head = jnp.where(index == classes, bias_sum, grad_class)
    return grad_pre, jnp.where(index == classes + 1, logit_sum, head)


def ramp_kernel(
    n_wide,
    n_narrow,
    labels,
    tokens,
    context,
    out_weight,
    up_weight,
    down_weight,
    ffn_bias,
    layer_biases,
    norm_gains,
    pool_weight,
    class_weight_t,
    ramp_biases,
    start_t,
    error,
    layer_part,
    middle_even,
    sums_odd,
    basis_out,
    factor_out,
    head_out,
    rows_out,
    grads_out,
    middle_odd,
    sums_even,
    error_high,
    error_low,
    factor_error,
    narrow_one,
    wide_one,
    narrow_two,
    wide_two,
    send_sem,
    recv_sem,
):
    turn = pl.program_id(0)
    wide, narrow = lax.axis_index("wide"), lax.axis_index("narrow")
    count, _, width = tokens.shape
    rank = start_t.shape[0]
    middle = (middle_even, middle_odd)
    sums = (sums_even, sums_odd)

    def group(index, slots, by_narrow):
        semaphores = send_sem.at[index], recv_sem.at[index]
        if by_narrow:
            return Exchange(slots, *semaphores, narrow, n_narrow, lambda i: (wide, i))
        return Exchange(slots, *semaphores, wide, n_wide, lambda i: (i, narrow))

    sum_one_narrow = group(0, narrow_one, True)
    sum_one_wide = group(1, wide_one, False)
    sum_two_narrow = group(2, narrow_two, True)
    sum_two_wide = group(3, wide_two, False)
    barrier = pltpu.get_barrier_semaphore()

    def middle_of(block, odd):
        middle[odd][...] = to_middle(
            block, tokens, context, out_weight, layer_biases, norm_gains
        )

    def step(index, odd):
        middle_of(index + 1, 1 - odd)
        sums[odd][...] = to_sums(
            middle[odd][...], up_weight, down_weight, ffn_bias, layer_biases
        )
        rows = to_layer(sums[1 - odd][...], layer_biases, norm_gains)
        layer_part[jnp.maximum(index - 1, 0)] = rows.reshape(count, SLICE, width)

    @pl.when(turn == 0)
    def _():
        sum_one_narrow.greet(barrier)
        sum_one_wide.greet(barrier)
        high = error[...].astype(bf16)
        low = (error[...] - high.astype(f32)).astype(bf16)
        error_high[...] = high
        error_low[...] = low
        start = stacked(start_t[...])
        factor_error[...] = folded(dot(start, high, NT) + dot(start, low, NT))
        middle_of(0, 0)
        sums_odd[...] = jnp.zeros_like(sums_odd)

    step(2 * turn, 0)

    @pl.when(turn == 0)
    def _():
        first = [sums_even[pl.ds(index * SLICE, ROW_TILE)] for index in range(count)]
        first_rows = to_layer(jnp.concatenate(first, 0), layer_biases, norm_gains)
        grads, head = head_gradients(
            labels, first_rows, pool_weight, class_weight_t, ramp_biases
        )
        inner = folded(dot(stacked(start_t[...]), grads, NT))
        factor = factor_error[...] + folded(dot(stacked(inner), first_rows))
        rows_out[...] = first_rows
        grads_out[...] = grads
        pl.semaphore_wait(barrier, n_narrow + n_wide - 2)
        sum_one_narrow.start(jnp.concatenate([factor, head], 0))

    @pl.when(turn == 2)
    def _():
        sum_two_wide.start(sum_two_narrow.total())

    step(2 * turn + 1, 1)

    @pl.when(turn == 0)
    def _():
        sum_one_wide.start(sum_one_narrow.total())

    @pl.when(turn == 1)
    def _():
        total = sum_one_wide.total()
        head_out[...] = total[rank:]
        basis = orthonormal_rows(total[:rank])
        basis_out[...] = basis
        basis = stacked(basis)
        inner = folded(dot(basis, rows_out[...], NT))
        factor = folded(dot(basis, error_high[...]) + dot(basis, error_low[...]))
        sum_two_narrow.start(factor + folded(dot(stacked(inner), grads_out[...])))

    @pl.when(turn == pl.num_programs(0) - 1)
    def _():
        factor_out[...] = sum_two_wide.total()


def ramp(n_wide, n_narrow, labels, tokens, context, *operands):
    start_t = operands[9]
    rank, width = start_t.shape
    count, length, _ = tokens.shape
    most = max(n_wide, n_narrow)
    vmem = pl.BlockSpec(memory_space=pltpu.VMEM)
    steps = length // SLICE - LATE_STEPS
    first = ROW_TILE * count
    outs = [
        pltpu.VMEM((steps - 1, count, SLICE, width), bf16),
        pltpu.VMEM((count * SLICE, width), bf16),
        pltpu.VMEM((count * SLICE, width), f32),
        pltpu.VMEM((rank, width), f32),
        pltpu.VMEM((rank, width), f32),
        pltpu.VMEM((8, width), f32),
        pltpu.VMEM((first, width), bf16),
        pltpu.VMEM((first, width), bf16),
    ]
    return pl.pallas_call(
        functools.partial(ramp_kernel, n_wide, n_narrow),
        grid=(steps // 2,),
        in_specs=[pl.BlockSpec(memory_space=pltpu.SMEM)] + [vmem] * (2 + len(operands)),
        out_specs=[vmem] * len(outs),
        out_shape=outs,
        scratch_shapes=[
            pltpu.VMEM((count * SLICE, width), bf16),
            pltpu.VMEM((count * SLICE, width), f32),
            pltpu.VMEM((width, width), bf16),
            pltpu.VMEM((width, width), bf16),
            pltpu.VMEM((rank, width), f32),
            pltpu.VMEM((n_narrow, rank + 8, width), f32),
            pltpu.VMEM((n_wide, rank + 8, width), f32),
            pltpu.VMEM((n_narrow, rank, width), f32),
            pltpu.VMEM((n_wide, rank, width), f32),
            pltpu.SemaphoreType.DMA((4, most)),
            pltpu.SemaphoreType.DMA((4, most)),
        ],
        compiler_params=pltpu.CompilerParams(
            vmem_limit_bytes=RAMP_MIB * MIB, collective_id=0, has_side_effects=True
        ),
        name="ramp",
    )(labels, tokens, context, *operands)


def finish_kernel(
    devices,
    tokens,
    context,
    layer_part,
    middle,
    sums,
    out_weight,
    up_weight,
    down_weight,
    ffn_bias,
    layer_biases,
    norm_gains,
    basis,
    factor,
    rows,
    grads,
    head,
    error,
    pool_weight,
    pool_moment,
    class_weight_t,
    class_moment_t,
    ramp_biases,
    bias_moment,
    layer_out,
    error_new,
    pool_weight_new,
    pool_moment_new,
    factor_new,
    class_weight_new,
    class_moment_new,
    ramp_biases_new,
    bias_moment_new,
    done,
    held,
    part_sem,
    done_sem,
    store_sem,
):
    ready, count, _, width = layer_part.shape
    classes = class_weight_t.shape[0]

    def block_of(array, index):
        return array.at[:, pl.ds(index * SLICE, SLICE)]

    parts = [
        pltpu.make_async_copy(layer_part.at[index], block_of(layer_out, index), part_sem.at[index])
        for index in range(ready)
    ]
    stores = [
        pltpu.make_async_copy(held.at[index], into, store_sem.at[index])
        for index, into in enumerate([error_new, pool_weight_new, pool_moment_new])
    ]

    def done_copy(index):
        into = block_of(layer_out, ready + index)
        return pltpu.make_async_copy(done.at[index], into, done_sem.at[index])

    def finish_block(index, values):
        done[index] = to_layer(values, layer_biases, norm_gains).reshape(count, SLICE, width)
        done_copy(index).start()

    for copy in parts:
        copy.start()
    finish_block(0, sums[...])
    high, mid, low = split(basis[...])
    left = jnp.concatenate([high, high, mid, mid, high, low], 0).astype(bf16)
    high, mid, low = split(factor[...])
    right = jnp.concatenate([high, mid, high, mid, low, high], 0).astype(bf16)
    approx = dot(left, right, TN)
    combined = dot(rows[...], grads[...], TN) + error[...]
    held[0] = combined - approx * (1.0 / devices)
    moment = MOMENTUM * pool_moment[...] + approx
    held[2] = moment
    held[1] = pool_weight[...] - RATE_POOL * moment
    for copy in stores:
        copy.start()
    factor_new[...] = factor[...]

    first_block = ready + 1
    middle = {first_block: middle[...]}
    for block in range(first_block, first_block + LATE_STEPS):
        if block + 1 < first_block + LATE_STEPS:
            middle[block + 1] = to_middle(
                block + 1, tokens, context, out_weight, layer_biases, norm_gains
            )
        next_sums = to_sums(middle[block], up_weight, down_weight, ffn_bias, layer_biases)
        finish_block(block - ready, next_sums)

    moment = MOMENTUM * class_moment_t[...] + head[:classes]
    class_moment_new[...] = moment
    class_weight_new[...] = class_weight_t[...] - RATE_HEAD * moment
    total = jnp.concatenate(
        [head[classes : classes + 1], head[classes + 1 : classes + 2, :classes]], 1
    )
    moment = MOMENTUM * bias_moment[...] + total.reshape(-1)
    bias_moment_new[...] = moment
    ramp_biases_new[...] = ramp_biases[...] - RATE_BIAS * moment

    for copy in parts + stores:
        copy.wait()
    for index in range(1 + LATE_STEPS):
        done_copy(index).wait()


def finish(devices, *operands):
    vmem = pl.BlockSpec(memory_space=pltpu.VMEM)
    hbm = pl.BlockSpec(memory_space=pltpu.HBM)
    tokens, layer_part, factor = operands[0], operands[2], operands[12]
    ready, *shape = layer_part.shape
    width = shape[-1]
    large = (tokens, *operands[16:19])
    small = (factor, *operands[19:])
    return pl.pallas_call(
        functools.partial(finish_kernel, devices),
        in_specs=[vmem] * len(operands),
        out_specs=[hbm] * len(large) + [vmem] * len(small),
        out_shape=[pltpu.HBM(array.shape, array.dtype) for array in large]
        + [jax.ShapeDtypeStruct(array.shape, array.dtype) for array in small],
        scratch_shapes=[
            pltpu.VMEM((1 + LATE_STEPS, *shape), bf16),
            pltpu.VMEM((3, width, width), f32),
            pltpu.SemaphoreType.DMA((ready,)),
            pltpu.SemaphoreType.DMA((1 + LATE_STEPS,)),
            pltpu.SemaphoreType.DMA((3,)),
        ],
        compiler_params=pltpu.CompilerParams(vmem_limit_bytes=FINISH_MIB * MIB),
        name="finish",
    )(*operands)


def body(
    n_wide,
    n_narrow,
    tokens,
    labels,
    qkv_weight,
    out_weight,
    up_weight,
    down_weight,
    ffn_bias,
    layer_biases,
    norm_gains,
    pool_weight,
    pool_moment,
    class_weight,
    class_moment,
    ramp_biases,
    bias_moment,
    start_factor,
    error_buffer,
):
    width = tokens.shape[1]
    carried = (
        out_weight,
        up_weight,
        down_weight,
        ffn_bias,
        layer_biases,
        norm_gains,
        error_buffer,
        pool_weight,
        pool_moment,
        class_weight.T,
        class_moment.T,
        ramp_biases,
        bias_moment,
        start_factor.T,
    )
    sequences, context, *carried = attention(tokens, qkv_weight, layer_biases, carried)
    layer = carried[:6]
    error, pool_weight, pool_moment, class_weight, class_moment = carried[6:11]
    ramp_biases, bias_moment, start = carried[11:]
    context = context.reshape(-1, SEQ_LEN, width)
    sequences = sequences.reshape(-1, SEQ_LEN, width)
    layer_part, middle, sums, basis, factor, head, first_rows, grads = ramp(
        n_wide,
        n_narrow,
        labels,
        sequences,
        context,
        *layer,
        pool_weight,
        class_weight,
        ramp_biases,
        start,
        error,
    )
    (
        layer_out,
        error_new,
        pool_weight_new,
        pool_moment_new,
        factor_new,
        class_weight_new,
        class_moment_new,
        ramp_biases_new,
        bias_moment_new,
    ) = finish(
        n_wide * n_narrow,
        sequences,
        context,
        layer_part,
        middle,
        sums,
        *layer,
        basis,
        factor,
        first_rows,
        grads,
        head,
        error,
        pool_weight,
        pool_moment,
        class_weight,
        class_moment,
        ramp_biases,
        bias_moment,
    )
    return (
        layer_out.reshape(tokens.shape),
        pool_moment_new,
        pool_weight_new,
        class_moment_new.T,
        class_weight_new.T,
        bias_moment_new,
        ramp_biases_new,
        error_new,
        factor_new.T,
    )


def solution(mesh):
    rows = P(("wide", "narrow"), None)
    in_specs = (rows, P(("wide", "narrow"))) + (P(),) * 14 + (rows,)
    out_specs = (rows,) + (P(),) * 6 + (rows, P())
    return jax.shard_map(
        functools.partial(body, mesh.shape["wide"], mesh.shape["narrow"]),
        mesh=mesh,
        in_specs=in_specs,
        out_specs=out_specs,
        check_vma=False,
    )
```

```python
import functools

import jax
import jax.numpy as jnp
from jax import lax
from jax.experimental import pallas as pl
from jax.experimental.pallas import tpu as pltpu
from jax.sharding import PartitionSpec as P

HEAD_DIM = 64
SEQ_LEN = 1024
PAIR = 128
V_ROWS = 80
ROW_TILE = 16
LANES = 128
SLICE = 128
LATE_STEPS = 2
HEAD_GROUP = 6
LOG2E = 1.4426950408889634
SAFE = 2.0**100
MOMENTUM = 0.9
RATE_POOL = 0.03
RATE_HEAD = 0.002
RATE_BIAS = 0.03
MIB = 1024 * 1024
ATTENTION_MIB = 23
RAMP_MIB = 12
FINISH_MIB = 14

f32 = jnp.float32
bf16 = jnp.bfloat16
NT = ((1,), (1,))
TN = ((0,), (0,))


def in_hbm(array):
    return pltpu.with_memory_space_constraint(array, pltpu.HBM)


def dot(left, right, contract=((1,), (0,))):
    return lax.dot_general(left, right, (contract, ((), ())), preferred_element_type=f32)


def norm_rows(values, gain, shift):
    centred = values - jnp.mean(values, -1, keepdims=True)
    variance = jnp.mean(centred * centred, -1, keepdims=True)
    return centred * lax.rsqrt(variance + 1e-12) * gain + shift


def gelu(values):
    half = 0.5 * values
    return half * lax.erf(values * 0.7071067811865476) + half


def head_sums(scores, values_aug, shifted):
    if shifted:
        scores = scores - jnp.max(scores, 0, keepdims=True)
    return dot(values_aug, jnp.exp2(scores * LOG2E).astype(bf16))


def put_context(context_t, head, sums):
    scale = 1.0 / sums[HEAD_DIM : HEAD_DIM + 8]
    groups = [sums[g : g + 8] * scale for g in range(0, HEAD_DIM, 8)]
    rows = pl.ds(pl.multiple_of(head * HEAD_DIM, HEAD_DIM), HEAD_DIM)
    context_t[rows, :] = jnp.concatenate(groups, 0).astype(bf16)


def attention_kernel(carried, tokens, qkv_weight, layer_biases, *refs):
    sources, (sequences, context), targets = (
        refs[:carried],
        refs[carried : carried + 2],
        refs[carried + 2 :][:carried],
    )
    (
        key_weight,
        query_weight_t,
        value_weight_t,
        query_bias,
        value_bias,
        keys,
        queries_t,
        values_t,
        context_t,
        low,
        high,
        weight_sem,
        token_sem,
        carry_sem,
    ) = refs[2 * carried + 2 :]
    step = pl.program_id(0)
    steps = pl.num_programs(0)
    length, width = queries_t.shape[2], tokens.shape[1]
    heads = width // HEAD_DIM

    def weight_copy(index, into):
        columns = qkv_weight.at[:, pl.ds(index * width, width)]
        return pltpu.make_async_copy(columns, into, weight_sem.at[index])

    def rows_of(index):
        return pl.ds(pl.multiple_of(index * length, length), length)

    def token_copy(index):
        rows = rows_of(index)
        return pltpu.make_async_copy(tokens.at[rows], sequences.at[rows], token_sem.at[index])

    carries = [
        pltpu.make_async_copy(source, target, carry_sem.at[index])
        for index, (source, target) in enumerate(zip(sources, targets, strict=True))
    ]
    query_weight = context.at[pl.ds(0, width)]
    value_weight = context.at[pl.ds(width, width)]
    query_copy = weight_copy(0, query_weight)
    key_copy = weight_copy(1, key_weight)
    value_copy = weight_copy(2, value_weight)

    @pl.when(step == 0)
    def _():
        query_copy.start()
        value_copy.start()
        token_copy(0).start()
        key_copy.start()
        columns = jnp.concatenate([layer_biases[...], jnp.zeros((2, width), f32)], 0).T
        query_bias[...] = jnp.broadcast_to(columns[:, 0:1], (width, LANES))
        value_bias[...] = jnp.broadcast_to(columns[:, 1:2], (width, LANES))
        queries_t[...] = jnp.zeros_like(queries_t)
        values_t[:, HEAD_DIM:, :] = jnp.ones((heads, V_ROWS - HEAD_DIM, length), bf16)
        query_copy.wait()
        query_weight_t[...] = query_weight[...].T
        value_copy.wait()
        value_weight_t[...] = value_weight[...].T
        key_copy.wait()
        @pl.loop(1, steps)
        def _(index):
            token_copy(index).start()

        for copy in carries:
            copy.start()

    token_copy(step).wait()

    def wide_bias(bias):
        return jnp.concatenate([bias[...]] * (length // LANES), 1)

    sequence = sequences[rows_of(step), :]
    key_rows = dot(sequence, key_weight[...]).astype(bf16)
    for pair in range(heads // 2):
        keys[pair] = key_rows[:, pair * PAIR : (pair + 1) * PAIR]

    query_cols = ((dot(query_weight_t[...], sequence, NT) + wide_bias(query_bias)) * 0.125).astype(bf16)
    value_cols = (dot(value_weight_t[...], sequence, NT) + wide_bias(value_bias)).astype(bf16)
    for head in range(heads):
        own = slice(head * HEAD_DIM, (head + 1) * HEAD_DIM)
        half = (head % 2) * HEAD_DIM
        queries_t[head, half : half + HEAD_DIM, :] = query_cols[own]
        values_t[head, :HEAD_DIM, :] = value_cols[own]

    low[...] = jnp.ones_like(low)
    high[...] = jnp.ones_like(high)

    @pl.loop(0, heads // HEAD_GROUP)
    def _(group):
        for offset in range(HEAD_GROUP):
            head = group * HEAD_GROUP + offset
            sums = head_sums(dot(keys[head // 2], queries_t[head]), values_t[head], False)
            denominators = sums[HEAD_DIM : HEAD_DIM + 8]
            low[...] = jnp.minimum(low[...], denominators)
            high[...] = jnp.maximum(high[...], denominators)
            put_context(context_t, head, sums)
            if offset % 2:
                lanes = pl.ds(pl.multiple_of((head // 2) * PAIR, PAIR), PAIR)
                context[rows_of(step), lanes] = context_t[lanes, :].T

    in_range = (jnp.min(low[...]) > 1.0 / SAFE) & (jnp.max(high[...]) < SAFE)

    @pl.when(jnp.logical_not(in_range))
    def _():
        @pl.loop(0, heads)
        def _(head):
            sums = head_sums(dot(keys[head // 2], queries_t[head]), values_t[head], True)
            put_context(context_t, head, sums)

        context[rows_of(step), :] = context_t[...].T

    @pl.when(step == steps - 1)
    def _():
        for copy in carries:
            copy.wait()


def attention(tokens, qkv_weight, layer_biases, carried):
    rows, width = tokens.shape
    count = rows // SEQ_LEN
    heads = width // HEAD_DIM
    hbm = pl.BlockSpec(memory_space=pltpu.HBM)
    square = pltpu.VMEM((width, width), bf16)
    return pl.pallas_call(
        functools.partial(attention_kernel, len(carried)),
        grid=(count,),
        in_specs=[hbm, hbm, pl.BlockSpec((6, width), lambda i: (0, 0))] + [hbm] * len(carried),
        out_specs=[pl.BlockSpec(memory_space=pltpu.VMEM)] * (2 + len(carried)),
        out_shape=[pltpu.VMEM(array.shape, array.dtype) for array in (tokens, tokens, *carried)],
        scratch_shapes=[square] * 3
        + [
            pltpu.VMEM((width, LANES), f32),
            pltpu.VMEM((width, LANES), f32),
            pltpu.VMEM((heads // 2, SEQ_LEN, PAIR), bf16),
            pltpu.VMEM((heads, PAIR, SEQ_LEN), bf16),
            pltpu.VMEM((heads, V_ROWS, SEQ_LEN), bf16),
            pltpu.VMEM((width, SEQ_LEN), bf16),
            pltpu.VMEM((8, SEQ_LEN), f32),
            pltpu.VMEM((8, SEQ_LEN), f32),
            pltpu.SemaphoreType.DMA((3,)),
            pltpu.SemaphoreType.DMA((count,)),
            pltpu.SemaphoreType.DMA((len(carried),)),
        ],
        compiler_params=pltpu.CompilerParams(vmem_limit_bytes=ATTENTION_MIB * MIB),
        name="attention",
    )(in_hbm(tokens), in_hbm(qkv_weight), layer_biases, *[in_hbm(array) for array in carried])


def to_middle(block, tokens, context, out_weight, biases, gains):
    where = pl.ds(pl.multiple_of(block * SLICE, SLICE), SLICE)

    def rows(array):
        return array[:, where, :].reshape(-1, array.shape[2])

    attended = dot(rows(context), out_weight[...]) + biases[2:3]
    return norm_rows(rows(tokens).astype(f32) + attended, gains[0:1], biases[3:4]).astype(bf16)


def to_sums(middle, up_weight, down_weight, ffn_bias, biases):
    hidden = gelu(dot(middle, up_weight[...]) + ffn_bias[...].reshape(1, -1)).astype(bf16)
    return middle.astype(f32) + dot(hidden, down_weight[...]) + biases[4:5]


def to_layer(sums, biases, gains):
    return norm_rows(sums, gains[1:2], biases[5:6]).astype(bf16)


def orthonormal_rows(factor):
    index = lax.broadcasted_iota(jnp.int32, factor.shape, 0)
    for row in range(factor.shape[0]):
        vector = factor[row : row + 1]
        vector = vector * lax.rsqrt(jnp.sum(vector * vector, -1, keepdims=True) + 1e-06)
        along = jnp.sum(factor * vector, -1, keepdims=True)
        factor = jnp.where(index > row, factor - along * vector, factor)
        factor = jnp.where(index == row, vector, factor)
    return factor


def split(values):
    first = values.astype(bf16).astype(f32)
    second = (values - first).astype(bf16).astype(f32)
    return first, second, values - first - second


def stacked(values):
    return jnp.concatenate(split(values), 0).astype(bf16)


def folded(values):
    rows = values.shape[0] // 3
    return values[:rows] + values[rows : 2 * rows] + values[2 * rows :]


class Exchange:
    def __init__(self, slots, send_sem, recv_sem, me, count, device_of):
        self.slots, self.send_sem, self.recv_sem = slots, send_sem, recv_sem
        self.me, self.count, self.device_of = me, count, device_of

    def copy(self, step, slot, device):
        return pltpu.make_async_remote_copy(
            src_ref=self.slots.at[slot],
            dst_ref=self.slots.at[slot],
            send_sem=self.send_sem.at[step],
            recv_sem=self.recv_sem.at[slot],
            device_id=self.device_of(device),
            device_id_type=pl.DeviceIdType.MESH,
        )

    def greet(self, barrier):
        for step in range(1, self.count):
            pl.semaphore_signal(
                barrier,
                inc=1,
                device_id=self.device_of(lax.rem(self.me + step, self.count)),
                device_id_type=pl.DeviceIdType.MESH,
            )

    def start(self, value):
        self.slots[self.me] = value
        for step in range(1, self.count):
            self.copy(step, self.me, lax.rem(self.me + step, self.count)).start()

    def total(self):
        for step in range(1, self.count):
            source = lax.rem(self.me + self.count - step, self.count)
            self.copy(step, source, source).wait_recv()
            self.copy(step, self.me, lax.rem(self.me + step, self.count)).wait_send()
        total = self.slots[0]
        for other in range(1, self.count):
            total = total + self.slots[other]
        return total


def head_gradients(labels, first_rows, pool_weight, class_weight_t, ramp_biases):
    classes, width = class_weight_t.shape
    class_low = jnp.concatenate(
        [class_weight_t[...], jnp.zeros((LANES - classes, width), f32)], 0
    ).astype(bf16)
    biases = jnp.concatenate([ramp_biases[...], jnp.zeros((LANES - classes,), f32)], 0)
    biases = biases.reshape(1, -1)
    pre = dot(first_rows, pool_weight[...].astype(bf16)) + biases[:, :width]
    pooled = jnp.tanh(pre)
    pooled_low = pooled.astype(bf16)
    logits = dot(pooled_low, class_low, NT) + biases[:, width:]
    lane = lax.broadcasted_iota(jnp.int32, logits.shape, 1)
    row = lax.broadcasted_iota(jnp.int32, logits.shape, 0)
    target = jnp.full(logits.shape, -1, jnp.int32)
    for index in range(first_rows.shape[0] // ROW_TILE):
        target = jnp.where(row == index * ROW_TILE, labels[index], target)
    logits = jnp.where(lane < classes, logits, -jnp.inf)
    powers = jnp.exp(logits - jnp.max(logits, -1, keepdims=True))
    softened = powers / jnp.sum(powers, -1, keepdims=True)
    grad_logits = softened - (lane == target).astype(f32)
    grad_logits = jnp.where(row % ROW_TILE == 0, grad_logits, 0.0).astype(bf16)
    grad_class = dot(grad_logits, pooled_low, TN)[:8]
    grad_pooled = dot(grad_logits, class_low)
    grad_pre = (grad_pooled * (1.0 - pooled * pooled)).astype(bf16)
    bias_sum = jnp.sum(grad_pre.astype(f32), 0, keepdims=True)
    logit_sum = jnp.sum(grad_logits.astype(f32), 0, keepdims=True)
    logit_sum = jnp.concatenate([logit_sum, jnp.zeros((1, width - LANES), f32)], 1)
    index = lax.broadcasted_iota(jnp.int32, grad_class.shape, 0)
    head = jnp.where(index == classes, bias_sum, grad_class)
    return grad_pre, jnp.where(index == classes + 1, logit_sum, head)


def ramp_kernel(
    n_wide,
    n_narrow,
    labels,
    tokens,
    context,
    out_weight,
    up_weight,
    down_weight,
    ffn_bias,
    layer_biases,
    norm_gains,
    pool_weight,
    class_weight_t,
    ramp_biases,
    start_t,
    error,
    layer_part,
    middle_even,
    sums_odd,
    basis_out,
    factor_out,
    head_out,
    rows_out,
    grads_out,
    middle_odd,
    sums_even,
    error_high,
    error_low,
    factor_error,
    narrow_one,
    wide_one,
    narrow_two,
    wide_two,
    send_sem,
    recv_sem,
):
    turn = pl.program_id(0)
    wide, narrow = lax.axis_index("wide"), lax.axis_index("narrow")
    count, _, width = tokens.shape
    rank = start_t.shape[0]
    middle = (middle_even, middle_odd)
    sums = (sums_even, sums_odd)

    def group(index, slots, by_narrow):
        semaphores = send_sem.at[index], recv_sem.at[index]
        if by_narrow:
            return Exchange(slots, *semaphores, narrow, n_narrow, lambda i: (wide, i))
        return Exchange(slots, *semaphores, wide, n_wide, lambda i: (i, narrow))

    sum_one_narrow = group(0, narrow_one, True)
    sum_one_wide = group(1, wide_one, False)
    sum_two_narrow = group(2, narrow_two, True)
    sum_two_wide = group(3, wide_two, False)
    barrier = pltpu.get_barrier_semaphore()

    def middle_of(block, odd):
        middle[odd][...] = to_middle(
            block, tokens, context, out_weight, layer_biases, norm_gains
        )

    def sums_of(odd):
        sums[odd][...] = to_sums(
            middle[odd][...], up_weight, down_weight, ffn_bias, layer_biases
        )

    def layer_of(block, odd):
        rows = to_layer(sums[odd][...], layer_biases, norm_gains)
        layer_part[block] = rows.reshape(count, SLICE, width)

    @pl.when(turn == 0)
    def _():
        sum_one_narrow.greet(barrier)
        sum_one_wide.greet(barrier)
        high = error[...].astype(bf16)
        low = (error[...] - high.astype(f32)).astype(bf16)
        error_high[...] = high
        error_low[...] = low
        start = stacked(start_t[...])
        factor_error[...] = folded(dot(start, high, NT) + dot(start, low, NT))
        middle_of(0, 0)
        sums_odd[...] = jnp.zeros_like(sums_odd)

    middle_of(2 * turn + 1, 1)
    sums_of(0)

    @pl.when(turn == 0)
    def _():
        first = [sums_even[pl.ds(index * SLICE, ROW_TILE)] for index in range(count)]
        first_rows = to_layer(jnp.concatenate(first, 0), layer_biases, norm_gains)
        grads, head = head_gradients(
            labels, first_rows, pool_weight, class_weight_t, ramp_biases
        )
        inner = folded(dot(stacked(start_t[...]), grads, NT))
        factor = factor_error[...] + folded(dot(stacked(inner), first_rows))
        rows_out[...] = first_rows
        grads_out[...] = grads
        pl.semaphore_wait(barrier, n_narrow + n_wide - 2)
        sum_one_narrow.start(jnp.concatenate([factor, head], 0))

    @pl.when(turn == 2)
    def _():
        sum_two_wide.start(sum_two_narrow.total())

    layer_of(jnp.maximum(2 * turn - 1, 0), 1)
    middle_of(2 * turn + 2, 0)
    sums_of(1)
    layer_of(2 * turn, 0)

    @pl.when(turn == 0)
    def _():
        sum_one_wide.start(sum_one_narrow.total())

    @pl.when(turn == 1)
    def _():
        total = sum_one_wide.total()
        head_out[...] = total[rank:]
        basis = orthonormal_rows(total[:rank])
        basis_out[...] = basis
        basis = stacked(basis)
        inner = folded(dot(basis, rows_out[...], NT))
        factor = folded(dot(basis, error_high[...]) + dot(basis, error_low[...]))
        sum_two_narrow.start(factor + folded(dot(stacked(inner), grads_out[...])))

    @pl.when(turn == pl.num_programs(0) - 1)
    def _():
        factor_out[...] = sum_two_wide.total()


def ramp(n_wide, n_narrow, labels, tokens, context, *operands):
    start_t = operands[9]
    rank, width = start_t.shape
    count, length, _ = tokens.shape
    most = max(n_wide, n_narrow)
    vmem = pl.BlockSpec(memory_space=pltpu.VMEM)
    steps = length // SLICE - LATE_STEPS
    first = ROW_TILE * count
    outs = [
        pltpu.VMEM((steps - 1, count, SLICE, width), bf16),
        pltpu.VMEM((count * SLICE, width), bf16),
        pltpu.VMEM((count * SLICE, width), f32),
        pltpu.VMEM((rank, width), f32),
        pltpu.VMEM((rank, width), f32),
        pltpu.VMEM((8, width), f32),
        pltpu.VMEM((first, width), bf16),
        pltpu.VMEM((first, width), bf16),
    ]
    return pl.pallas_call(
        functools.partial(ramp_kernel, n_wide, n_narrow),
        grid=(steps // 2,),
        in_specs=[pl.BlockSpec(memory_space=pltpu.SMEM)] + [vmem] * (2 + len(operands)),
        out_specs=[vmem] * len(outs),
        out_shape=outs,
        scratch_shapes=[
            pltpu.VMEM((count * SLICE, width), bf16),
            pltpu.VMEM((count * SLICE, width), f32),
            pltpu.VMEM((width, width), bf16),
            pltpu.VMEM((width, width), bf16),
            pltpu.VMEM((rank, width), f32),
            pltpu.VMEM((n_narrow, rank + 8, width), f32),
            pltpu.VMEM((n_wide, rank + 8, width), f32),
            pltpu.VMEM((n_narrow, rank, width), f32),
            pltpu.VMEM((n_wide, rank, width), f32),
            pltpu.SemaphoreType.DMA((4, most)),
            pltpu.SemaphoreType.DMA((4, most)),
        ],
        compiler_params=pltpu.CompilerParams(
            vmem_limit_bytes=RAMP_MIB * MIB, collective_id=0, has_side_effects=True
        ),
        name="ramp",
    )(labels, tokens, context, *operands)


def finish_kernel(
    devices,
    tokens,
    context,
    layer_part,
    middle,
    sums,
    out_weight,
    up_weight,
    down_weight,
    ffn_bias,
    layer_biases,
    norm_gains,
    basis,
    factor,
    rows,
    grads,
    head,
    error,
    pool_weight,
    pool_moment,
    class_weight_t,
    class_moment_t,
    ramp_biases,
    bias_moment,
    layer_out,
    error_new,
    pool_weight_new,
    pool_moment_new,
    factor_new,
    class_weight_new,
    class_moment_new,
    ramp_biases_new,
    bias_moment_new,
    done,
    held,
    part_sem,
    done_sem,
    store_sem,
):
    ready, count, _, width = layer_part.shape
    classes = class_weight_t.shape[0]

    def block_of(array, index):
        return array.at[:, pl.ds(index * SLICE, SLICE)]

    parts = [
        pltpu.make_async_copy(layer_part.at[index], block_of(layer_out, index), part_sem.at[index])
        for index in range(ready)
    ]
    stores = [
        pltpu.make_async_copy(held.at[index], into, store_sem.at[index])
        for index, into in enumerate([error_new, pool_weight_new, pool_moment_new])
    ]

    def done_copy(index, sequence):
        into = layer_out.at[sequence, pl.ds((ready + index) * SLICE, SLICE)]
        return pltpu.make_async_copy(
            done.at[index, sequence], into, done_sem.at[index, sequence]
        )

    def finish_block(index, values):
        for sequence in range(count):
            rows = values[sequence * SLICE : (sequence + 1) * SLICE]
            done[index, sequence] = to_layer(rows, layer_biases, norm_gains)
            done_copy(index, sequence).start()

    for copy in parts:
        copy.start()
    finish_block(0, sums[...])
    high, mid, low = split(basis[...])
    left = jnp.concatenate([high, high, mid, mid, high, low], 0).astype(bf16)
    high, mid, low = split(factor[...])
    right = jnp.concatenate([high, mid, high, mid, low, high], 0).astype(bf16)
    approx = dot(left, right, TN)
    combined = dot(rows[...], grads[...], TN) + error[...]
    held[0] = combined - approx * (1.0 / devices)
    moment = MOMENTUM * pool_moment[...] + approx
    held[2] = moment
    held[1] = pool_weight[...] - RATE_POOL * moment
    for copy in stores:
        copy.start()
    factor_new[...] = factor[...]

    first_block = ready + 1
    middle = {first_block: middle[...]}
    for block in range(first_block, first_block + LATE_STEPS):
        if block + 1 < first_block + LATE_STEPS:
            middle[block + 1] = to_middle(
                block + 1, tokens, context, out_weight, layer_biases, norm_gains
            )
        next_sums = to_sums(middle[block], up_weight, down_weight, ffn_bias, layer_biases)
        finish_block(block - ready, next_sums)

    moment = MOMENTUM * class_moment_t[...] + head[:classes]
    class_moment_new[...] = moment
    class_weight_new[...] = class_weight_t[...] - RATE_HEAD * moment
    total = jnp.concatenate(
        [head[classes : classes + 1], head[classes + 1 : classes + 2, :classes]], 1
    )
    moment = MOMENTUM * bias_moment[...] + total.reshape(-1)
    bias_moment_new[...] = moment
    ramp_biases_new[...] = ramp_biases[...] - RATE_BIAS * moment

    for copy in parts + stores:
        copy.wait()
    for index in range(1 + LATE_STEPS):
        for sequence in range(count):
            done_copy(index, sequence).wait()


def finish(devices, *operands):
    vmem = pl.BlockSpec(memory_space=pltpu.VMEM)
    hbm = pl.BlockSpec(memory_space=pltpu.HBM)
    tokens, layer_part, factor = operands[0], operands[2], operands[12]
    ready, *shape = layer_part.shape
    width = shape[-1]
    large = (tokens, *operands[16:19])
    small = (factor, *operands[19:])
    return pl.pallas_call(
        functools.partial(finish_kernel, devices),
        in_specs=[vmem] * len(operands),
        out_specs=[hbm] * len(large) + [vmem] * len(small),
        out_shape=[pltpu.HBM(array.shape, array.dtype) for array in large]
        + [jax.ShapeDtypeStruct(array.shape, array.dtype) for array in small],
        scratch_shapes=[
            pltpu.VMEM((1 + LATE_STEPS, *shape), bf16),
            pltpu.VMEM((3, width, width), f32),
            pltpu.SemaphoreType.DMA((ready,)),
            pltpu.SemaphoreType.DMA((1 + LATE_STEPS, shape[0])),
            pltpu.SemaphoreType.DMA((3,)),
        ],
        compiler_params=pltpu.CompilerParams(vmem_limit_bytes=FINISH_MIB * MIB),
        name="finish",
    )(*operands)


def body(
    n_wide,
    n_narrow,
    tokens,
    labels,
    qkv_weight,
    out_weight,
    up_weight,
    down_weight,
    ffn_bias,
    layer_biases,
    norm_gains,
    pool_weight,
    pool_moment,
    class_weight,
    class_moment,
    ramp_biases,
    bias_moment,
    start_factor,
    error_buffer,
):
    width = tokens.shape[1]
    carried = (
        out_weight,
        up_weight,
        down_weight,
        ffn_bias,
        layer_biases,
        norm_gains,
        error_buffer,
        pool_weight,
        pool_moment,
        class_weight.T,
        class_moment.T,
        ramp_biases,
        bias_moment,
        start_factor.T,
    )
    sequences, context, *carried = attention(tokens, qkv_weight, layer_biases, carried)
    layer = carried[:6]
    error, pool_weight, pool_moment, class_weight, class_moment = carried[6:11]
    ramp_biases, bias_moment, start = carried[11:]
    context = context.reshape(-1, SEQ_LEN, width)
    sequences = sequences.reshape(-1, SEQ_LEN, width)
    layer_part, middle, sums, basis, factor, head, first_rows, grads = ramp(
        n_wide,
        n_narrow,
        labels,
        sequences,
        context,
        *layer,
        pool_weight,
        class_weight,
        ramp_biases,
        start,
        error,
    )
    (
        layer_out,
        error_new,
        pool_weight_new,
        pool_moment_new,
        factor_new,
        class_weight_new,
        class_moment_new,
        ramp_biases_new,
        bias_moment_new,
    ) = finish(
        n_wide * n_narrow,
        sequences,
        context,
        layer_part,
        middle,
        sums,
        *layer,
        basis,
        factor,
        first_rows,
        grads,
        head,
        error,
        pool_weight,
        pool_moment,
        class_weight,
        class_moment,
        ramp_biases,
        bias_moment,
    )
    return (
        layer_out.reshape(tokens.shape),
        pool_moment_new,
        pool_weight_new,
        class_moment_new.T,
        class_weight_new.T,
        bias_moment_new,
        ramp_biases_new,
        error_new,
        factor_new.T,
    )


def solution(mesh):
    rows = P(("wide", "narrow"), None)
    in_specs = (rows, P(("wide", "narrow"))) + (P(),) * 14 + (rows,)
    out_specs = (rows,) + (P(),) * 6 + (rows, P())
    return jax.shard_map(
        functools.partial(body, mesh.shape["wide"], mesh.shape["narrow"]),
        mesh=mesh,
        in_specs=in_specs,
        out_specs=out_specs,
        check_vma=False,
    )
```

```python
import functools

import jax
import jax.numpy as jnp
from jax import lax
from jax.experimental import pallas as pl
from jax.experimental.pallas import tpu as pltpu
from jax.sharding import PartitionSpec as P

HEAD_DIM = 64
SEQ_LEN = 1024
PAIR = 128
V_ROWS = 80
ROW_TILE = 16
LANES = 128
SLICE = 128
LATE_STEPS = 2
HEAD_GROUP = 6
LOG2E = 1.4426950408889634
SAFE = 2.0**100
MOMENTUM = 0.9
RATE_POOL = 0.03
RATE_HEAD = 0.002
RATE_BIAS = 0.03
MIB = 1024 * 1024
ATTENTION_MIB = 23
RAMP_MIB = 11.25
FINISH_MIB = 14

f32 = jnp.float32
bf16 = jnp.bfloat16
NT = ((1,), (1,))
TN = ((0,), (0,))


def in_hbm(array):
    return pltpu.with_memory_space_constraint(array, pltpu.HBM)


def dot(left, right, contract=((1,), (0,))):
    return lax.dot_general(left, right, (contract, ((), ())), preferred_element_type=f32)


def norm_rows(values, gain, shift):
    centred = values - jnp.mean(values, -1, keepdims=True)
    variance = jnp.mean(centred * centred, -1, keepdims=True)
    return centred * lax.rsqrt(variance + 1e-12) * gain + shift


def gelu(values):
    half = 0.5 * values
    return half * lax.erf(values * 0.7071067811865476) + half


def head_sums(scores, values_aug, shifted):
    if shifted:
        scores = scores - jnp.max(scores, 0, keepdims=True)
    return dot(values_aug, jnp.exp2(scores * LOG2E).astype(bf16))


def put_context(context_t, head, sums):
    scale = 1.0 / sums[HEAD_DIM : HEAD_DIM + 8]
    groups = [sums[g : g + 8] * scale for g in range(0, HEAD_DIM, 8)]
    rows = pl.ds(pl.multiple_of(head * HEAD_DIM, HEAD_DIM), HEAD_DIM)
    context_t[rows, :] = jnp.concatenate(groups, 0).astype(bf16)


def attention_kernel(carried, tokens, qkv_weight, layer_biases, *refs):
    sources, (sequences, context), targets = (
        refs[:carried],
        refs[carried : carried + 2],
        refs[carried + 2 :][:carried],
    )
    (
        key_weight,
        query_weight_t,
        value_weight_t,
        query_bias,
        value_bias,
        keys,
        queries_t,
        values_t,
        context_t,
        low,
        weight_sem,
        token_sem,
        carry_sem,
    ) = refs[2 * carried + 2 :]
    step = pl.program_id(0)
    steps = pl.num_programs(0)
    length, width = queries_t.shape[2], tokens.shape[1]
    heads = width // HEAD_DIM

    def weight_copy(index, into):
        columns = qkv_weight.at[:, pl.ds(index * width, width)]
        return pltpu.make_async_copy(columns, into, weight_sem.at[index])

    def rows_of(index):
        return pl.ds(pl.multiple_of(index * length, length), length)

    def token_copy(index):
        rows = rows_of(index)
        return pltpu.make_async_copy(tokens.at[rows], sequences.at[rows], token_sem.at[index])

    carries = [
        pltpu.make_async_copy(source, target, carry_sem.at[index])
        for index, (source, target) in enumerate(zip(sources, targets, strict=True))
    ]
    query_weight = context.at[pl.ds(0, width)]
    value_weight = context.at[pl.ds(width, width)]
    query_copy = weight_copy(0, query_weight)
    key_copy = weight_copy(1, key_weight)
    value_copy = weight_copy(2, value_weight)

    @pl.when(step == 0)
    def _():
        token_copy(0).start()
        query_copy.start()
        value_copy.start()
        key_copy.start()
        columns = jnp.concatenate([layer_biases[...], jnp.zeros((2, width), f32)], 0).T
        query_bias[...] = jnp.broadcast_to(columns[:, 0:1], (width, LANES))
        value_bias[...] = jnp.broadcast_to(columns[:, 1:2], (width, LANES))
        queries_t[...] = jnp.zeros_like(queries_t)
        values_t[:, HEAD_DIM:, :] = jnp.ones((heads, V_ROWS - HEAD_DIM, length), bf16)
        query_copy.wait()
        query_weight_t[...] = query_weight[...].T
        value_copy.wait()
        value_weight_t[...] = value_weight[...].T
        key_copy.wait()
        @pl.loop(1, steps)
        def _(index):
            token_copy(index).start()

        for copy in carries:
            copy.start()

    token_copy(step).wait()

    def wide_bias(bias):
        return jnp.concatenate([bias[...]] * (length // LANES), 1)

    sequence = sequences[rows_of(step), :]
    key_rows = dot(sequence, key_weight[...]).astype(bf16)
    for pair in range(heads // 2):
        keys[pair] = key_rows[:, pair * PAIR : (pair + 1) * PAIR]

    query_cols = ((dot(query_weight_t[...], sequence, NT) + wide_bias(query_bias)) * 0.125).astype(bf16)
    value_cols = (dot(value_weight_t[...], sequence, NT) + wide_bias(value_bias)).astype(bf16)
    for head in range(heads):
        own = slice(head * HEAD_DIM, (head + 1) * HEAD_DIM)
        half = (head % 2) * HEAD_DIM
        queries_t[head, half : half + HEAD_DIM, :] = query_cols[own]
        values_t[head, :HEAD_DIM, :] = value_cols[own]

    low[...] = jnp.ones_like(low)

    @pl.loop(0, heads // HEAD_GROUP)
    def _(group):
        for offset in range(HEAD_GROUP):
            head = group * HEAD_GROUP + offset
            sums = head_sums(dot(keys[head // 2], queries_t[head]), values_t[head], False)
            denominators = sums[HEAD_DIM : HEAD_DIM + 8]
            low[...] = jnp.minimum(low[...], jnp.minimum(denominators, 1.0 / denominators))
            put_context(context_t, head, sums)
            if offset % 2:
                lanes = pl.ds(pl.multiple_of((head // 2) * PAIR, PAIR), PAIR)
                context[rows_of(step), lanes] = context_t[lanes, :].T

    in_range = jnp.min(low[...]) > 1.0 / SAFE

    @pl.when(jnp.logical_not(in_range))
    def _():
        @pl.loop(0, heads)
        def _(head):
            sums = head_sums(dot(keys[head // 2], queries_t[head]), values_t[head], True)
            put_context(context_t, head, sums)

        context[rows_of(step), :] = context_t[...].T

    @pl.when(step == steps - 1)
    def _():
        for copy in carries:
            copy.wait()


def attention(tokens, qkv_weight, layer_biases, carried):
    rows, width = tokens.shape
    count = rows // SEQ_LEN
    heads = width // HEAD_DIM
    hbm = pl.BlockSpec(memory_space=pltpu.HBM)
    square = pltpu.VMEM((width, width), bf16)
    return pl.pallas_call(
        functools.partial(attention_kernel, len(carried)),
        grid=(count,),
        in_specs=[hbm, hbm, pl.BlockSpec((6, width), lambda i: (0, 0))] + [hbm] * len(carried),
        out_specs=[pl.BlockSpec(memory_space=pltpu.VMEM)] * (2 + len(carried)),
        out_shape=[pltpu.VMEM(array.shape, array.dtype) for array in (tokens, tokens, *carried)],
        scratch_shapes=[square] * 3
        + [
            pltpu.VMEM((width, LANES), f32),
            pltpu.VMEM((width, LANES), f32),
            pltpu.VMEM((heads // 2, SEQ_LEN, PAIR), bf16),
            pltpu.VMEM((heads, PAIR, SEQ_LEN), bf16),
            pltpu.VMEM((heads, V_ROWS, SEQ_LEN), bf16),
            pltpu.VMEM((width, SEQ_LEN), bf16),
            pltpu.VMEM((8, SEQ_LEN), f32),
            pltpu.SemaphoreType.DMA((3,)),
            pltpu.SemaphoreType.DMA((count,)),
            pltpu.SemaphoreType.DMA((len(carried),)),
        ],
        compiler_params=pltpu.CompilerParams(vmem_limit_bytes=ATTENTION_MIB * MIB),
        name="attention",
    )(in_hbm(tokens), in_hbm(qkv_weight), layer_biases, *[in_hbm(array) for array in carried])


def to_middle(block, tokens, context, out_weight, biases, gains):
    where = pl.ds(pl.multiple_of(block * SLICE, SLICE), SLICE)

    def rows(array):
        return array[:, where, :].reshape(-1, array.shape[2])

    attended = dot(rows(context), out_weight[...]) + biases[2:3]
    return norm_rows(rows(tokens).astype(f32) + attended, gains[0:1], biases[3:4]).astype(bf16)


def to_sums(middle, up_weight, down_weight, ffn_bias, biases):
    hidden = gelu(dot(middle, up_weight[...]) + ffn_bias[...].reshape(1, -1)).astype(bf16)
    return middle.astype(f32) + dot(hidden, down_weight[...]) + biases[4:5]


def to_layer(sums, biases, gains):
    return norm_rows(sums, gains[1:2], biases[5:6]).astype(bf16)


def orthonormal_rows(factor):
    index = lax.broadcasted_iota(jnp.int32, factor.shape, 0)
    for row in range(factor.shape[0]):
        vector = factor[row : row + 1]
        along = jnp.sum(factor * vector, -1, keepdims=True)
        scale = lax.rsqrt(along[row : row + 1] + 1e-06)
        vector = vector * scale
        factor = jnp.where(index > row, factor - along * scale * vector, factor)
        factor = jnp.where(index == row, vector, factor)
    return factor


def split(values):
    first = values.astype(bf16).astype(f32)
    second = (values - first).astype(bf16).astype(f32)
    return first, second, values - first - second


def stacked(values):
    return jnp.concatenate(split(values), 0).astype(bf16)


def folded(values):
    rows = values.shape[0] // 3
    return values[:rows] + values[rows : 2 * rows] + values[2 * rows :]


class Exchange:
    def __init__(self, slots, send_sem, recv_sem, me, count, device_of):
        self.slots, self.send_sem, self.recv_sem = slots, send_sem, recv_sem
        self.me, self.count, self.device_of = me, count, device_of

    def copy(self, step, slot, device):
        return pltpu.make_async_remote_copy(
            src_ref=self.slots.at[slot],
            dst_ref=self.slots.at[slot],
            send_sem=self.send_sem.at[step],
            recv_sem=self.recv_sem.at[slot],
            device_id=self.device_of(device),
            device_id_type=pl.DeviceIdType.MESH,
        )

    def greet(self, barrier):
        for step in range(1, self.count):
            pl.semaphore_signal(
                barrier,
                inc=1,
                device_id=self.device_of(lax.rem(self.me + step, self.count)),
                device_id_type=pl.DeviceIdType.MESH,
            )

    def start(self, value):
        self.slots[self.me] = value
        for step in range(1, self.count):
            self.copy(step, self.me, lax.rem(self.me + step, self.count)).start()

    def total(self):
        for step in range(1, self.count):
            source = lax.rem(self.me + self.count - step, self.count)
            self.copy(step, source, source).wait_recv()
            self.copy(step, self.me, lax.rem(self.me + step, self.count)).wait_send()
        total = self.slots[0]
        for other in range(1, self.count):
            total = total + self.slots[other]
        return total


def head_gradients(labels, first_rows, pool_weight, class_weight_t, ramp_biases):
    classes, width = class_weight_t.shape
    class_low = jnp.concatenate(
        [class_weight_t[...], jnp.zeros((LANES - classes, width), f32)], 0
    ).astype(bf16)
    biases = jnp.concatenate([ramp_biases[...], jnp.zeros((LANES - classes,), f32)], 0)
    biases = biases.reshape(1, -1)
    pre = dot(first_rows, pool_weight[...].astype(bf16)) + biases[:, :width]
    pooled = jnp.tanh(pre)
    pooled_low = pooled.astype(bf16)
    logits = dot(pooled_low, class_low, NT) + biases[:, width:]
    lane = lax.broadcasted_iota(jnp.int32, logits.shape, 1)
    row = lax.broadcasted_iota(jnp.int32, logits.shape, 0)
    target = jnp.full(logits.shape, -1, jnp.int32)
    for index in range(first_rows.shape[0] // ROW_TILE):
        target = jnp.where(row == index * ROW_TILE, labels[index], target)
    logits = jnp.where(lane < classes, logits, -jnp.inf)
    powers = jnp.exp(logits - jnp.max(logits, -1, keepdims=True))
    softened = powers / jnp.sum(powers, -1, keepdims=True)
    grad_logits = softened - (lane == target).astype(f32)
    grad_logits = jnp.where(row % ROW_TILE == 0, grad_logits, 0.0).astype(bf16)
    grad_class = dot(grad_logits, pooled_low, TN)[:8]
    grad_pooled = dot(grad_logits, class_low)
    grad_pre = (grad_pooled * (1.0 - pooled * pooled)).astype(bf16)
    bias_sum = jnp.sum(grad_pre.astype(f32), 0, keepdims=True)
    logit_sum = jnp.sum(grad_logits.astype(f32), 0, keepdims=True)
    logit_sum = jnp.concatenate([logit_sum, jnp.zeros((1, width - LANES), f32)], 1)
    index = lax.broadcasted_iota(jnp.int32, grad_class.shape, 0)
    head = jnp.where(index == classes, bias_sum, grad_class)
    return grad_pre, jnp.where(index == classes + 1, logit_sum, head)


def ramp_kernel(
    n_wide,
    n_narrow,
    labels,
    tokens,
    context,
    out_weight,
    up_weight,
    down_weight,
    ffn_bias,
    layer_biases,
    norm_gains,
    pool_weight,
    class_weight_t,
    ramp_biases,
    start_t,
    error,
    layer_part,
    middle_even,
    middle_last,
    basis_out,
    factor_out,
    head_out,
    rows_out,
    grads_out,
    middle_odd,
    sums_even,
    sums_odd,
    error_high,
    error_low,
    factor_error,
    narrow_one,
    wide_one,
    narrow_two,
    wide_two,
    send_sem,
    recv_sem,
):
    turn = pl.program_id(0)
    wide, narrow = lax.axis_index("wide"), lax.axis_index("narrow")
    count, _, width = tokens.shape
    rank = start_t.shape[0]
    middle = (middle_even, middle_odd)
    sums = (sums_even, sums_odd)

    def group(index, slots, by_narrow):
        semaphores = send_sem.at[index], recv_sem.at[index]
        if by_narrow:
            return Exchange(slots, *semaphores, narrow, n_narrow, lambda i: (wide, i))
        return Exchange(slots, *semaphores, wide, n_wide, lambda i: (i, narrow))

    sum_one_narrow = group(0, narrow_one, True)
    sum_one_wide = group(1, wide_one, False)
    sum_two_narrow = group(2, narrow_two, True)
    sum_two_wide = group(3, wide_two, False)
    barrier = pltpu.get_barrier_semaphore()

    def middle_of(block, odd):
        middle[odd][...] = to_middle(
            block, tokens, context, out_weight, layer_biases, norm_gains
        )

    def sums_of(odd):
        sums[odd][...] = to_sums(
            middle[odd][...], up_weight, down_weight, ffn_bias, layer_biases
        )

    def layer_of(block, odd):
        rows = to_layer(sums[odd][...], layer_biases, norm_gains)
        layer_part[block] = rows.reshape(count, SLICE, width)

    @pl.when(turn == 0)
    def _():
        sum_one_narrow.greet(barrier)
        sum_one_wide.greet(barrier)
        high = error[...].astype(bf16)
        low = (error[...] - high.astype(f32)).astype(bf16)
        error_high[...] = high
        error_low[...] = low
        start = stacked(start_t[...])
        factor_error[...] = folded(dot(start, high, NT) + dot(start, low, NT))
        middle_of(0, 0)
        sums_odd[...] = jnp.zeros_like(sums_odd)

    middle_of(2 * turn + 1, 1)
    sums_of(0)

    @pl.when(turn == 0)
    def _():
        first = [sums_even[pl.ds(index * SLICE, ROW_TILE)] for index in range(count)]
        first_rows = to_layer(jnp.concatenate(first, 0), layer_biases, norm_gains)
        grads, head = head_gradients(
            labels, first_rows, pool_weight, class_weight_t, ramp_biases
        )
        inner = folded(dot(stacked(start_t[...]), grads, NT))
        factor = factor_error[...] + folded(dot(stacked(inner), first_rows))
        rows_out[...] = first_rows
        grads_out[...] = grads
        pl.semaphore_wait(barrier, n_narrow + n_wide - 2)
        sum_one_narrow.start(jnp.concatenate([factor, head], 0))

    @pl.when(turn == 2)
    def _():
        sum_two_wide.start(sum_two_narrow.total())

    layer_of(jnp.maximum(2 * turn - 1, 0), 1)
    middle_of(2 * turn + 2, 0)
    sums_of(1)
    layer_of(2 * turn, 0)

    @pl.when(turn == 0)
    def _():
        sum_one_wide.start(sum_one_narrow.total())

    @pl.when(turn == 1)
    def _():
        total = sum_one_wide.total()
        head_out[...] = total[rank:]
        basis = orthonormal_rows(total[:rank])
        basis_out[...] = basis
        basis = stacked(basis)
        inner = folded(dot(basis, rows_out[...], NT))
        factor = folded(dot(basis, error_high[...]) + dot(basis, error_low[...]))
        sum_two_narrow.start(factor + folded(dot(stacked(inner), grads_out[...])))

    @pl.when(turn == pl.num_programs(0) - 1)
    def _():
        last = layer_part.shape[0] - 1
        layer_of(last, 1)
        middle_last[...] = to_middle(
            last + 2, tokens, context, out_weight, layer_biases, norm_gains
        )
        factor_out[...] = sum_two_wide.total()


def ramp(n_wide, n_narrow, labels, tokens, context, *operands):
    start_t = operands[9]
    rank, width = start_t.shape
    count, length, _ = tokens.shape
    most = max(n_wide, n_narrow)
    vmem = pl.BlockSpec(memory_space=pltpu.VMEM)
    steps = length // SLICE - LATE_STEPS
    first = ROW_TILE * count
    outs = [
        pltpu.VMEM((steps, count, SLICE, width), bf16),
        pltpu.VMEM((count * SLICE, width), bf16),
        pltpu.VMEM((count * SLICE, width), bf16),
        pltpu.VMEM((rank, width), f32),
        pltpu.VMEM((rank, width), f32),
        pltpu.VMEM((8, width), f32),
        pltpu.VMEM((first, width), bf16),
        pltpu.VMEM((first, width), bf16),
    ]
    slots = (n_wide + n_narrow) * (2 * rank + 8) * width * 4
    return pl.pallas_call(
        functools.partial(ramp_kernel, n_wide, n_narrow),
        grid=(steps // 2,),
        in_specs=[pl.BlockSpec(memory_space=pltpu.SMEM)] + [vmem] * (2 + len(operands)),
        out_specs=[vmem] * len(outs),
        out_shape=outs,
        scratch_shapes=[
            pltpu.VMEM((count * SLICE, width), bf16),
            pltpu.VMEM((count * SLICE, width), f32),
            pltpu.VMEM((count * SLICE, width), f32),
            pltpu.VMEM((width, width), bf16),
            pltpu.VMEM((width, width), bf16),
            pltpu.VMEM((rank, width), f32),
            pltpu.VMEM((n_narrow, rank + 8, width), f32),
            pltpu.VMEM((n_wide, rank + 8, width), f32),
            pltpu.VMEM((n_narrow, rank, width), f32),
            pltpu.VMEM((n_wide, rank, width), f32),
            pltpu.SemaphoreType.DMA((4, most)),
            pltpu.SemaphoreType.DMA((4, most)),
        ],
        compiler_params=pltpu.CompilerParams(
            vmem_limit_bytes=int(RAMP_MIB * MIB) + slots, collective_id=0, has_side_effects=True
        ),
        name="ramp",
    )(labels, tokens, context, *operands)


def finish_kernel(
    devices,
    layer_part,
    first_middle,
    last_middle,
    up_weight,
    down_weight,
    ffn_bias,
    layer_biases,
    norm_gains,
    basis,
    factor,
    rows,
    grads,
    head,
    error,
    pool_weight,
    pool_moment,
    class_weight_t,
    class_moment_t,
    ramp_biases,
    bias_moment,
    layer_out,
    error_new,
    pool_weight_new,
    pool_moment_new,
    factor_new,
    class_weight_new,
    class_moment_new,
    ramp_biases_new,
    bias_moment_new,
    done,
    held,
    part_sem,
    done_sem,
    store_sem,
):
    ready, count, _, width = layer_part.shape
    classes = class_weight_t.shape[0]

    def block_of(array, index):
        return array.at[:, pl.ds(index * SLICE, SLICE)]

    parts = [
        pltpu.make_async_copy(layer_part.at[index], block_of(layer_out, index), part_sem.at[index])
        for index in range(ready)
    ]
    stores = [
        pltpu.make_async_copy(held.at[index], into, store_sem.at[index])
        for index, into in enumerate([error_new, pool_weight_new, pool_moment_new])
    ]

    def done_copy(index, sequence):
        into = layer_out.at[sequence, pl.ds((ready + index) * SLICE, SLICE)]
        return pltpu.make_async_copy(
            done.at[index, sequence], into, done_sem.at[index, sequence]
        )

    def finish_block(index, values):
        for sequence in range(count):
            rows = values[sequence * SLICE : (sequence + 1) * SLICE]
            done[index, sequence] = to_layer(rows, layer_biases, norm_gains)
            done_copy(index, sequence).start()

    for copy in parts:
        copy.start()
    sums = to_sums(first_middle[...], up_weight, down_weight, ffn_bias, layer_biases)
    finish_block(0, sums)
    high, mid, low = split(basis[...])
    left = jnp.concatenate([high, high, mid, mid, high, low], 0).astype(bf16)
    high, mid, low = split(factor[...])
    right = jnp.concatenate([high, mid, high, mid, low, high], 0).astype(bf16)
    approx = dot(left, right, TN)
    combined = dot(rows[...], grads[...], TN) + error[...]
    held[0] = combined - approx * (1.0 / devices)
    moment = MOMENTUM * pool_moment[...] + approx
    held[2] = moment
    held[1] = pool_weight[...] - RATE_POOL * moment
    for copy in stores:
        copy.start()
    factor_new[...] = factor[...]

    sums = to_sums(last_middle[...], up_weight, down_weight, ffn_bias, layer_biases)
    finish_block(1, sums)

    moment = MOMENTUM * class_moment_t[...] + head[:classes]
    class_moment_new[...] = moment
    class_weight_new[...] = class_weight_t[...] - RATE_HEAD * moment
    total = jnp.concatenate(
        [head[classes : classes + 1], head[classes + 1 : classes + 2, :classes]], 1
    )
    moment = MOMENTUM * bias_moment[...] + total.reshape(-1)
    bias_moment_new[...] = moment
    ramp_biases_new[...] = ramp_biases[...] - RATE_BIAS * moment

    for copy in parts + stores:
        copy.wait()
    for index in range(LATE_STEPS):
        for sequence in range(count):
            done_copy(index, sequence).wait()


def finish(devices, tokens, *operands):
    vmem = pl.BlockSpec(memory_space=pltpu.VMEM)
    hbm = pl.BlockSpec(memory_space=pltpu.HBM)
    layer_part, factor = operands[0], operands[9]
    ready, *shape = layer_part.shape
    width = shape[-1]
    large = (tokens, *operands[13:16])
    small = (factor, *operands[16:])
    return pl.pallas_call(
        functools.partial(finish_kernel, devices),
        in_specs=[vmem] * len(operands),
        out_specs=[hbm] * len(large) + [vmem] * len(small),
        out_shape=[pltpu.HBM(array.shape, array.dtype) for array in large]
        + [jax.ShapeDtypeStruct(array.shape, array.dtype) for array in small],
        scratch_shapes=[
            pltpu.VMEM((LATE_STEPS, *shape), bf16),
            pltpu.VMEM((3, width, width), f32),
            pltpu.SemaphoreType.DMA((ready,)),
            pltpu.SemaphoreType.DMA((LATE_STEPS, shape[0])),
            pltpu.SemaphoreType.DMA((3,)),
        ],
        compiler_params=pltpu.CompilerParams(vmem_limit_bytes=FINISH_MIB * MIB),
        name="finish",
    )(*operands)


def body(
    n_wide,
    n_narrow,
    tokens,
    labels,
    qkv_weight,
    out_weight,
    up_weight,
    down_weight,
    ffn_bias,
    layer_biases,
    norm_gains,
    pool_weight,
    pool_moment,
    class_weight,
    class_moment,
    ramp_biases,
    bias_moment,
    start_factor,
    error_buffer,
):
    width = tokens.shape[1]
    carried = (
        out_weight,
        up_weight,
        down_weight,
        ffn_bias,
        layer_biases,
        norm_gains,
        error_buffer,
        pool_weight,
        pool_moment,
        class_weight.T,
        class_moment.T,
        ramp_biases,
        bias_moment,
        start_factor.T,
    )
    sequences, context, *carried = attention(tokens, qkv_weight, layer_biases, carried)
    layer = carried[:6]
    error, pool_weight, pool_moment, class_weight, class_moment = carried[6:11]
    ramp_biases, bias_moment, start = carried[11:]
    context = context.reshape(-1, SEQ_LEN, width)
    sequences = sequences.reshape(-1, SEQ_LEN, width)
    layer_part, middle, last_middle, basis, factor, head, first_rows, grads = ramp(
        n_wide,
        n_narrow,
        labels,
        sequences,
        context,
        *layer,
        pool_weight,
        class_weight,
        ramp_biases,
        start,
        error,
    )
    (
        layer_out,
        error_new,
        pool_weight_new,
        pool_moment_new,
        factor_new,
        class_weight_new,
        class_moment_new,
        ramp_biases_new,
        bias_moment_new,
    ) = finish(
        n_wide * n_narrow,
        sequences,
        layer_part,
        middle,
        last_middle,
        *layer[1:],
        basis,
        factor,
        first_rows,
        grads,
        head,
        error,
        pool_weight,
        pool_moment,
        class_weight,
        class_moment,
        ramp_biases,
        bias_moment,
    )
    return (
        layer_out.reshape(tokens.shape),
        pool_moment_new,
        pool_weight_new,
        class_moment_new.T,
        class_weight_new.T,
        bias_moment_new,
        ramp_biases_new,
        error_new,
        factor_new.T,
    )


def solution(mesh):
    rows = P(("wide", "narrow"), None)
    in_specs = (rows, P(("wide", "narrow"))) + (P(),) * 14 + (rows,)
    out_specs = (rows,) + (P(),) * 6 + (rows, P())
    return jax.shard_map(
        functools.partial(body, mesh.shape["wide"], mesh.shape["narrow"]),
        mesh=mesh,
        in_specs=in_specs,
        out_specs=out_specs,
        check_vma=False,
    )
```

```python
import functools

import jax
import jax.numpy as jnp
from jax import lax
from jax.experimental import pallas as pl
from jax.experimental.pallas import tpu as pltpu
from jax.sharding import PartitionSpec as P

HEAD_DIM = 64
SEQ_LEN = 1024
PAIR = 128
V_ROWS = 80
ROW_TILE = 16
LANES = 128
SLICE = 128
LATE_STEPS = 2
HEAD_GROUP = 6
LOG2E = 1.4426950408889634
SAFE = 2.0**100
MOMENTUM = 0.9
RATE_POOL = 0.03
RATE_HEAD = 0.002
RATE_BIAS = 0.03
MIB = 1024 * 1024
ATTENTION_MIB = 23
RAMP_MIB = 11.25
FINISH_MIB = 14

f32 = jnp.float32
bf16 = jnp.bfloat16
NT = ((1,), (1,))
TN = ((0,), (0,))


def in_hbm(array):
    return pltpu.with_memory_space_constraint(array, pltpu.HBM)


def dot(left, right, contract=((1,), (0,))):
    return lax.dot_general(left, right, (contract, ((), ())), preferred_element_type=f32)


def norm_rows(values, gain, shift):
    centred = values - jnp.mean(values, -1, keepdims=True)
    variance = jnp.mean(centred * centred, -1, keepdims=True)
    return centred * lax.rsqrt(variance + 1e-12) * gain + shift


def gelu(values):
    half = 0.5 * values
    return half * lax.erf(values * 0.7071067811865476) + half


def head_sums(scores, values_aug, shifted):
    if shifted:
        scores = scores - jnp.max(scores, 0, keepdims=True)
    return dot(values_aug, jnp.exp2(scores * LOG2E).astype(bf16))


def put_context(context_t, head, sums):
    scale = 1.0 / sums[HEAD_DIM : HEAD_DIM + 8]
    groups = [sums[g : g + 8] * scale for g in range(0, HEAD_DIM, 8)]
    rows = pl.ds(pl.multiple_of(head * HEAD_DIM, HEAD_DIM), HEAD_DIM)
    context_t[rows, :] = jnp.concatenate(groups, 0).astype(bf16)


def attention_kernel(carried, tokens, qkv_weight, layer_biases, *refs):
    sources, (sequences, context), targets = (
        refs[:carried],
        refs[carried : carried + 2],
        refs[carried + 2 :][:carried],
    )
    (
        key_weight,
        query_weight_t,
        value_weight_t,
        query_bias,
        value_bias,
        keys,
        queries_t,
        values_t,
        context_t,
        low,
        weight_sem,
        token_sem,
        carry_sem,
    ) = refs[2 * carried + 2 :]
    step = pl.program_id(0)
    steps = pl.num_programs(0)
    length, width = queries_t.shape[2], tokens.shape[1]
    heads = width // HEAD_DIM

    def weight_copy(index, into):
        columns = qkv_weight.at[:, pl.ds(index * width, width)]
        return pltpu.make_async_copy(columns, into, weight_sem.at[index])

    def rows_of(index):
        return pl.ds(pl.multiple_of(index * length, length), length)

    def token_copy(index):
        rows = rows_of(index)
        return pltpu.make_async_copy(tokens.at[rows], sequences.at[rows], token_sem.at[index])

    carries = [
        pltpu.make_async_copy(source, target, carry_sem.at[index])
        for index, (source, target) in enumerate(zip(sources, targets, strict=True))
    ]
    query_weight = context.at[pl.ds(0, width)]
    value_weight = context.at[pl.ds(width, width)]
    query_copy = weight_copy(0, query_weight)
    key_copy = weight_copy(1, key_weight)
    value_copy = weight_copy(2, value_weight)

    @pl.when(step == 0)
    def _():
        token_copy(0).start()
        query_copy.start()
        value_copy.start()
        key_copy.start()
        columns = jnp.concatenate([layer_biases[...], jnp.zeros((2, width), f32)], 0).T
        query_bias[...] = jnp.broadcast_to(columns[:, 0:1], (width, LANES))
        value_bias[...] = jnp.broadcast_to(columns[:, 1:2], (width, LANES))
        queries_t[...] = jnp.zeros_like(queries_t)
        values_t[:, HEAD_DIM:, :] = jnp.ones((heads, V_ROWS - HEAD_DIM, length), bf16)
        query_copy.wait()
        query_weight_t[...] = query_weight[...].T
        value_copy.wait()
        value_weight_t[...] = value_weight[...].T
        key_copy.wait()
        @pl.loop(1, steps)
        def _(index):
            token_copy(index).start()

        for copy in carries:
            copy.start()

    token_copy(step).wait()

    def wide_bias(bias):
        return jnp.concatenate([bias[...]] * (length // LANES), 1)

    sequence = sequences[rows_of(step), :]
    key_rows = dot(sequence, key_weight[...]).astype(bf16)
    for pair in range(heads // 2):
        keys[pair] = key_rows[:, pair * PAIR : (pair + 1) * PAIR]

    query_cols = ((dot(query_weight_t[...], sequence, NT) + wide_bias(query_bias)) * 0.125).astype(bf16)
    value_cols = (dot(value_weight_t[...], sequence, NT) + wide_bias(value_bias)).astype(bf16)
    for head in range(heads):
        own = slice(head * HEAD_DIM, (head + 1) * HEAD_DIM)
        half = (head % 2) * HEAD_DIM
        queries_t[head, half : half + HEAD_DIM, :] = query_cols[own]
        values_t[head, :HEAD_DIM, :] = value_cols[own]

    low[...] = jnp.ones_like(low)

    @pl.loop(0, heads // HEAD_GROUP)
    def _(group):
        for offset in range(HEAD_GROUP):
            head = group * HEAD_GROUP + offset
            sums = head_sums(dot(keys[head // 2], queries_t[head]), values_t[head], False)
            denominators = sums[HEAD_DIM : HEAD_DIM + 8]
            low[...] = jnp.minimum(low[...], jnp.minimum(denominators, 1.0 / denominators))
            put_context(context_t, head, sums)
            if offset % 2:
                lanes = pl.ds(pl.multiple_of((head // 2) * PAIR, PAIR), PAIR)
                context[rows_of(step), lanes] = context_t[lanes, :].T

    in_range = jnp.min(low[...]) > 1.0 / SAFE

    @pl.when(jnp.logical_not(in_range))
    def _():
        @pl.loop(0, heads)
        def _(head):
            sums = head_sums(dot(keys[head // 2], queries_t[head]), values_t[head], True)
            put_context(context_t, head, sums)

        context[rows_of(step), :] = context_t[...].T

    @pl.when(step == steps - 1)
    def _():
        for copy in carries:
            copy.wait()


def attention(tokens, qkv_weight, layer_biases, carried):
    rows, width = tokens.shape
    count = rows // SEQ_LEN
    heads = width // HEAD_DIM
    hbm = pl.BlockSpec(memory_space=pltpu.HBM)
    square = pltpu.VMEM((width, width), bf16)
    return pl.pallas_call(
        functools.partial(attention_kernel, len(carried)),
        grid=(count,),
        in_specs=[hbm, hbm, pl.BlockSpec((6, width), lambda i: (0, 0))] + [hbm] * len(carried),
        out_specs=[pl.BlockSpec(memory_space=pltpu.VMEM)] * (2 + len(carried)),
        out_shape=[pltpu.VMEM(array.shape, array.dtype) for array in (tokens, tokens, *carried)],
        scratch_shapes=[square] * 3
        + [
            pltpu.VMEM((width, LANES), f32),
            pltpu.VMEM((width, LANES), f32),
            pltpu.VMEM((heads // 2, SEQ_LEN, PAIR), bf16),
            pltpu.VMEM((heads, PAIR, SEQ_LEN), bf16),
            pltpu.VMEM((heads, V_ROWS, SEQ_LEN), bf16),
            pltpu.VMEM((width, SEQ_LEN), bf16),
            pltpu.VMEM((8, SEQ_LEN), f32),
            pltpu.SemaphoreType.DMA((3,)),
            pltpu.SemaphoreType.DMA((count,)),
            pltpu.SemaphoreType.DMA((len(carried),)),
        ],
        compiler_params=pltpu.CompilerParams(vmem_limit_bytes=ATTENTION_MIB * MIB),
        name="attention",
    )(in_hbm(tokens), in_hbm(qkv_weight), layer_biases, *[in_hbm(array) for array in carried])


def to_middle(block, tokens, context, out_weight, biases, gains):
    where = pl.ds(pl.multiple_of(block * SLICE, SLICE), SLICE)

    def rows(array):
        return array[:, where, :].reshape(-1, array.shape[2])

    attended = dot(rows(context), out_weight[...]) + biases[2:3]
    return norm_rows(rows(tokens).astype(f32) + attended, gains[0:1], biases[3:4]).astype(bf16)


def to_sums(middle, up_weight, down_weight, ffn_bias, biases):
    hidden = gelu(dot(middle, up_weight[...]) + ffn_bias[...].reshape(1, -1)).astype(bf16)
    return middle.astype(f32) + dot(hidden, down_weight[...]) + biases[4:5]


def to_layer(sums, biases, gains):
    return norm_rows(sums, gains[1:2], biases[5:6]).astype(bf16)


def orthonormal_rows(factor):
    index = lax.broadcasted_iota(jnp.int32, factor.shape, 0)
    for row in range(factor.shape[0]):
        vector = factor[row : row + 1]
        along = jnp.sum(factor * vector, -1, keepdims=True)
        scale = lax.rsqrt(along[row : row + 1] + 1e-06)
        vector = vector * scale
        factor = jnp.where(index > row, factor - along * scale * vector, factor)
        factor = jnp.where(index == row, vector, factor)
    return factor


def split(values):
    first = values.astype(bf16).astype(f32)
    second = (values - first).astype(bf16).astype(f32)
    return first, second, values - first - second


def stacked(values):
    return jnp.concatenate(split(values), 0).astype(bf16)


def folded(values):
    rows = values.shape[0] // 3
    return values[:rows] + values[rows : 2 * rows] + values[2 * rows :]


class Exchange:
    def __init__(self, slots, send_sem, recv_sem, me, count, device_of):
        self.slots, self.send_sem, self.recv_sem = slots, send_sem, recv_sem
        self.me, self.count, self.device_of = me, count, device_of

    def copy(self, step, slot, device):
        return pltpu.make_async_remote_copy(
            src_ref=self.slots.at[slot],
            dst_ref=self.slots.at[slot],
            send_sem=self.send_sem.at[step],
            recv_sem=self.recv_sem.at[slot],
            device_id=self.device_of(device),
            device_id_type=pl.DeviceIdType.MESH,
        )

    def greet(self, barrier):
        for step in range(1, self.count):
            pl.semaphore_signal(
                barrier,
                inc=1,
                device_id=self.device_of(lax.rem(self.me + step, self.count)),
                device_id_type=pl.DeviceIdType.MESH,
            )

    def start(self, value):
        self.slots[self.me] = value
        for step in range(1, self.count):
            self.copy(step, self.me, lax.rem(self.me + step, self.count)).start()

    def total(self):
        for step in range(1, self.count):
            source = lax.rem(self.me + self.count - step, self.count)
            self.copy(step, source, source).wait_recv()
            self.copy(step, self.me, lax.rem(self.me + step, self.count)).wait_send()
        total = self.slots[0]
        for other in range(1, self.count):
            total = total + self.slots[other]
        return total


def head_gradients(labels, first_rows, pool_weight, class_weight_t, ramp_biases):
    classes, width = class_weight_t.shape
    class_low = jnp.concatenate(
        [class_weight_t[...], jnp.zeros((LANES - classes, width), f32)], 0
    ).astype(bf16)
    biases = jnp.concatenate([ramp_biases[...], jnp.zeros((LANES - classes,), f32)], 0)
    biases = biases.reshape(1, -1)
    pre = dot(first_rows, pool_weight[...].astype(bf16)) + biases[:, :width]
    pooled = jnp.tanh(pre)
    pooled_low = pooled.astype(bf16)
    logits = dot(pooled_low, class_low, NT) + biases[:, width:]
    lane = lax.broadcasted_iota(jnp.int32, logits.shape, 1)
    row = lax.broadcasted_iota(jnp.int32, logits.shape, 0)
    target = jnp.full(logits.shape, -1, jnp.int32)
    for index in range(first_rows.shape[0] // ROW_TILE):
        target = jnp.where(row == index * ROW_TILE, labels[index], target)
    logits = jnp.where(lane < classes, logits, -jnp.inf)
    powers = jnp.exp(logits - jnp.max(logits, -1, keepdims=True))
    softened = powers / jnp.sum(powers, -1, keepdims=True)
    grad_logits = softened - (lane == target).astype(f32)
    grad_logits = jnp.where(row % ROW_TILE == 0, grad_logits, 0.0).astype(bf16)
    grad_class = dot(grad_logits, pooled_low, TN)[:8]
    grad_pooled = dot(grad_logits, class_low)
    grad_pre = (grad_pooled * (1.0 - pooled * pooled)).astype(bf16)
    bias_sum = jnp.sum(grad_pre.astype(f32), 0, keepdims=True)
    logit_sum = jnp.sum(grad_logits.astype(f32), 0, keepdims=True)
    logit_sum = jnp.concatenate([logit_sum, jnp.zeros((1, width - LANES), f32)], 1)
    index = lax.broadcasted_iota(jnp.int32, grad_class.shape, 0)
    head = jnp.where(index == classes, bias_sum, grad_class)
    return grad_pre, jnp.where(index == classes + 1, logit_sum, head)


def ramp_kernel(
    n_wide,
    n_narrow,
    labels,
    tokens,
    context,
    out_weight,
    up_weight,
    down_weight,
    ffn_bias,
    layer_biases,
    norm_gains,
    pool_weight,
    class_weight_t,
    ramp_biases,
    start_t,
    error,
    layer_part,
    middle_even,
    middle_last,
    basis_out,
    factor_out,
    head_out,
    rows_out,
    grads_out,
    middle_odd,
    sums_even,
    sums_odd,
    error_high,
    error_low,
    factor_error,
    narrow_one,
    wide_one,
    narrow_two,
    wide_two,
    send_sem,
    recv_sem,
):
    turn = pl.program_id(0)
    wide, narrow = lax.axis_index("wide"), lax.axis_index("narrow")
    count, _, width = tokens.shape
    rank = start_t.shape[0]
    middle = (middle_even, middle_odd)
    sums = (sums_even, sums_odd)

    def group(index, slots, by_narrow):
        semaphores = send_sem.at[index], recv_sem.at[index]
        if by_narrow:
            return Exchange(slots, *semaphores, narrow, n_narrow, lambda i: (wide, i))
        return Exchange(slots, *semaphores, wide, n_wide, lambda i: (i, narrow))

    sum_one_narrow = group(0, narrow_one, True)
    sum_one_wide = group(1, wide_one, False)
    sum_two_narrow = group(2, narrow_two, True)
    sum_two_wide = group(3, wide_two, False)
    barrier = pltpu.get_barrier_semaphore()

    def middle_of(block, odd):
        middle[odd][...] = to_middle(
            block, tokens, context, out_weight, layer_biases, norm_gains
        )

    def sums_of(odd):
        sums[odd][...] = to_sums(
            middle[odd][...], up_weight, down_weight, ffn_bias, layer_biases
        )

    def layer_of(block, odd):
        rows = to_layer(sums[odd][...], layer_biases, norm_gains)
        layer_part[block] = rows.reshape(count, SLICE, width)

    @pl.when(turn == 0)
    def _():
        sum_one_narrow.greet(barrier)
        sum_one_wide.greet(barrier)
        high = error[...].astype(bf16)
        low = (error[...] - high.astype(f32)).astype(bf16)
        error_high[...] = high
        error_low[...] = low
        start = stacked(start_t[...])
        factor_error[...] = folded(dot(start, high, NT) + dot(start, low, NT))
        middle_of(0, 0)
        sums_odd[...] = jnp.zeros_like(sums_odd)

    middle_of(2 * turn + 1, 1)
    sums_of(0)

    @pl.when(turn == 0)
    def _():
        first = [sums_even[pl.ds(index * SLICE, ROW_TILE)] for index in range(count)]
        first_rows = to_layer(jnp.concatenate(first, 0), layer_biases, norm_gains)
        grads, head = head_gradients(
            labels, first_rows, pool_weight, class_weight_t, ramp_biases
        )
        inner = folded(dot(stacked(start_t[...]), grads, NT))
        factor = factor_error[...] + folded(dot(stacked(inner), first_rows))
        rows_out[...] = first_rows
        grads_out[...] = grads
        pl.semaphore_wait(barrier, n_narrow + n_wide - 2)
        sum_one_narrow.start(jnp.concatenate([factor, head], 0))

    @pl.when(turn == 2)
    def _():
        sum_two_wide.start(sum_two_narrow.total())

    middle_of(2 * turn + 2, 0)
    layer_of(jnp.maximum(2 * turn - 1, 0), 1)
    sums_of(1)
    layer_of(2 * turn, 0)

    @pl.when(turn == 0)
    def _():
        sum_one_wide.start(sum_one_narrow.total())

    @pl.when(turn == 1)
    def _():
        total = sum_one_wide.total()
        head_out[...] = total[rank:]
        basis = orthonormal_rows(total[:rank])
        basis_out[...] = basis
        basis = stacked(basis)
        inner = folded(dot(basis, rows_out[...], NT))
        factor = folded(dot(basis, error_high[...]) + dot(basis, error_low[...]))
        sum_two_narrow.start(factor + folded(dot(stacked(inner), grads_out[...])))

    @pl.when(turn == pl.num_programs(0) - 1)
    def _():
        last = layer_part.shape[0] - 1
        layer_of(last, 1)
        middle_last[...] = to_middle(
            last + 2, tokens, context, out_weight, layer_biases, norm_gains
        )
        factor_out[...] = sum_two_wide.total()


def ramp(n_wide, n_narrow, labels, tokens, context, *operands):
    start_t = operands[9]
    rank, width = start_t.shape
    count, length, _ = tokens.shape
    most = max(n_wide, n_narrow)
    vmem = pl.BlockSpec(memory_space=pltpu.VMEM)
    steps = length // SLICE - LATE_STEPS
    first = ROW_TILE * count
    outs = [
        pltpu.VMEM((steps, count, SLICE, width), bf16),
        pltpu.VMEM((count * SLICE, width), bf16),
        pltpu.VMEM((count * SLICE, width), bf16),
        pltpu.VMEM((rank, width), f32),
        pltpu.VMEM((rank, width), f32),
        pltpu.VMEM((8, width), f32),
        pltpu.VMEM((first, width), bf16),
        pltpu.VMEM((first, width), bf16),
    ]
    slots = (n_wide + n_narrow) * (2 * rank + 8) * width * 4
    return pl.pallas_call(
        functools.partial(ramp_kernel, n_wide, n_narrow),
        grid=(steps // 2,),
        in_specs=[pl.BlockSpec(memory_space=pltpu.SMEM)] + [vmem] * (2 + len(operands)),
        out_specs=[vmem] * len(outs),
        out_shape=outs,
        scratch_shapes=[
            pltpu.VMEM((count * SLICE, width), bf16),
            pltpu.VMEM((count * SLICE, width), f32),
            pltpu.VMEM((count * SLICE, width), f32),
            pltpu.VMEM((width, width), bf16),
            pltpu.VMEM((width, width), bf16),
            pltpu.VMEM((rank, width), f32),
            pltpu.VMEM((n_narrow, rank + 8, width), f32),
            pltpu.VMEM((n_wide, rank + 8, width), f32),
            pltpu.VMEM((n_narrow, rank, width), f32),
            pltpu.VMEM((n_wide, rank, width), f32),
            pltpu.SemaphoreType.DMA((4, most)),
            pltpu.SemaphoreType.DMA((4, most)),
        ],
        compiler_params=pltpu.CompilerParams(
            vmem_limit_bytes=int(RAMP_MIB * MIB) + slots, collective_id=0, has_side_effects=True
        ),
        name="ramp",
    )(labels, tokens, context, *operands)


def finish_kernel(
    devices,
    layer_part,
    first_middle,
    last_middle,
    up_weight,
    down_weight,
    ffn_bias,
    layer_biases,
    norm_gains,
    basis,
    factor,
    rows,
    grads,
    head,
    error,
    pool_weight,
    pool_moment,
    class_weight_t,
    class_moment_t,
    ramp_biases,
    bias_moment,
    layer_out,
    error_new,
    pool_weight_new,
    pool_moment_new,
    factor_new,
    class_weight_new,
    class_moment_new,
    ramp_biases_new,
    bias_moment_new,
    done,
    held,
    part_sem,
    done_sem,
    store_sem,
):
    ready, count, _, width = layer_part.shape
    classes = class_weight_t.shape[0]

    def block_of(array, index):
        return array.at[:, pl.ds(index * SLICE, SLICE)]

    parts = [
        pltpu.make_async_copy(layer_part.at[index], block_of(layer_out, index), part_sem.at[index])
        for index in range(ready)
    ]
    stores = [
        pltpu.make_async_copy(held.at[index], into, store_sem.at[index])
        for index, into in enumerate([error_new, pool_weight_new, pool_moment_new])
    ]

    def done_copy(index, sequence):
        into = layer_out.at[sequence, pl.ds((ready + index) * SLICE, SLICE)]
        return pltpu.make_async_copy(
            done.at[index, sequence], into, done_sem.at[index, sequence]
        )

    def finish_block(index, values):
        for sequence in range(count):
            rows = values[sequence * SLICE : (sequence + 1) * SLICE]
            done[index, sequence] = to_layer(rows, layer_biases, norm_gains)
            done_copy(index, sequence).start()

    for copy in parts:
        copy.start()
    sums = to_sums(first_middle[...], up_weight, down_weight, ffn_bias, layer_biases)
    finish_block(0, sums)
    high, mid, low = split(basis[...])
    left = jnp.concatenate([high, high, mid, mid, high, low], 0).astype(bf16)
    high, mid, low = split(factor[...])
    right = jnp.concatenate([high, mid, high, mid, low, high], 0).astype(bf16)
    approx = dot(left, right, TN)
    combined = dot(rows[...], grads[...], TN) + error[...]
    held[0] = combined - approx * (1.0 / devices)
    moment = MOMENTUM * pool_moment[...] + approx
    held[2] = moment
    held[1] = pool_weight[...] - RATE_POOL * moment
    for copy in stores:
        copy.start()
    factor_new[...] = factor[...]

    sums = to_sums(last_middle[...], up_weight, down_weight, ffn_bias, layer_biases)
    finish_block(1, sums)

    moment = MOMENTUM * class_moment_t[...] + head[:classes]
    class_moment_new[...] = moment
    class_weight_new[...] = class_weight_t[...] - RATE_HEAD * moment
    total = jnp.concatenate(
        [head[classes : classes + 1], head[classes + 1 : classes + 2, :classes]], 1
    )
    moment = MOMENTUM * bias_moment[...] + total.reshape(-1)
    bias_moment_new[...] = moment
    ramp_biases_new[...] = ramp_biases[...] - RATE_BIAS * moment

    for copy in parts + stores:
        copy.wait()
    for index in range(LATE_STEPS):
        for sequence in range(count):
            done_copy(index, sequence).wait()


def finish(devices, tokens, *operands):
    vmem = pl.BlockSpec(memory_space=pltpu.VMEM)
    hbm = pl.BlockSpec(memory_space=pltpu.HBM)
    layer_part, factor = operands[0], operands[9]
    ready, *shape = layer_part.shape
    width = shape[-1]
    large = (tokens, *operands[13:16])
    small = (factor, *operands[16:])
    return pl.pallas_call(
        functools.partial(finish_kernel, devices),
        in_specs=[vmem] * len(operands),
        out_specs=[hbm] * len(large) + [vmem] * len(small),
        out_shape=[pltpu.HBM(array.shape, array.dtype) for array in large]
        + [jax.ShapeDtypeStruct(array.shape, array.dtype) for array in small],
        scratch_shapes=[
            pltpu.VMEM((LATE_STEPS, *shape), bf16),
            pltpu.VMEM((3, width, width), f32),
            pltpu.SemaphoreType.DMA((ready,)),
            pltpu.SemaphoreType.DMA((LATE_STEPS, shape[0])),
            pltpu.SemaphoreType.DMA((3,)),
        ],
        compiler_params=pltpu.CompilerParams(vmem_limit_bytes=FINISH_MIB * MIB),
        name="finish",
    )(*operands)


def body(
    n_wide,
    n_narrow,
    tokens,
    labels,
    qkv_weight,
    out_weight,
    up_weight,
    down_weight,
    ffn_bias,
    layer_biases,
    norm_gains,
    pool_weight,
    pool_moment,
    class_weight,
    class_moment,
    ramp_biases,
    bias_moment,
    start_factor,
    error_buffer,
):
    width = tokens.shape[1]
    carried = (
        out_weight,
        up_weight,
        down_weight,
        ffn_bias,
        layer_biases,
        norm_gains,
        error_buffer,
        pool_weight,
        pool_moment,
        class_weight.T,
        class_moment.T,
        ramp_biases,
        bias_moment,
        start_factor.T,
    )
    sequences, context, *carried = attention(tokens, qkv_weight, layer_biases, carried)
    layer = carried[:6]
    error, pool_weight, pool_moment, class_weight, class_moment = carried[6:11]
    ramp_biases, bias_moment, start = carried[11:]
    context = context.reshape(-1, SEQ_LEN, width)
    sequences = sequences.reshape(-1, SEQ_LEN, width)
    layer_part, middle, last_middle, basis, factor, head, first_rows, grads = ramp(
        n_wide,
        n_narrow,
        labels,
        sequences,
        context,
        *layer,
        pool_weight,
        class_weight,
        ramp_biases,
        start,
        error,
    )
    (
        layer_out,
        error_new,
        pool_weight_new,
        pool_moment_new,
        factor_new,
        class_weight_new,
        class_moment_new,
        ramp_biases_new,
        bias_moment_new,
    ) = finish(
        n_wide * n_narrow,
        sequences,
        layer_part,
        middle,
        last_middle,
        *layer[1:],
        basis,
        factor,
        first_rows,
        grads,
        head,
        error,
        pool_weight,
        pool_moment,
        class_weight,
        class_moment,
        ramp_biases,
        bias_moment,
    )
    return (
        layer_out.reshape(tokens.shape),
        pool_moment_new,
        pool_weight_new,
        class_moment_new.T,
        class_weight_new.T,
        bias_moment_new,
        ramp_biases_new,
        error_new,
        factor_new.T,
    )


def solution(mesh):
    rows = P(("wide", "narrow"), None)
    in_specs = (rows, P(("wide", "narrow"))) + (P(),) * 14 + (rows,)
    out_specs = (rows,) + (P(),) * 6 + (rows, P())
    return jax.shard_map(
        functools.partial(body, mesh.shape["wide"], mesh.shape["narrow"]),
        mesh=mesh,
        in_specs=in_specs,
        out_specs=out_specs,
        check_vma=False,
    )
```
